512 devices in a mesh: space: 64 (over z, y_hi, core), spec: 8 (over y_lo, x).
Axes of the slice: x: 4, y: 8 (y_hi: 4, y_lo: 2; y = y_hi * 2 + y_lo), z: 8, core: 2. Of those that a mesh axis runs over, the one named last changes fastest.
Arguments:
- spectrum: float32 [24, 25, 256, 1024], P('spec', None, 'space'), as said below
- sea_mask: int32 [256, 1024], P('space'), may hold values 0 or 1
- turning: float32 [256, 1024], P('space'), may hold values from -0.4 to 0.4
- wind_u: float32 [256, 1024], P('space'), may hold values from -4 to 4
- wind_v: float32 [256, 1024], P('space'), may hold values from -4 to 4
Outputs:
- updated: float32 [24, 25, 256, 1024], P('spec', None, 'space')
The draws below stay inside these ranges and needn't reach their ends.
Inputs may be any that keep to these rules, and one draw needn't show every extreme that they name: `spectrum`: positive.
All inputs are finite; a program needn't handle non-finite values. No bound on the sum of `sea_mask` on one device may be relied on, other than what follows from the above.
Results may differ from the reference program's by a relative error of at most 0.00002.
Values sent between devices are 32-bit elements; how exact they have to be, the bound alone decides.
No kernel may reach another device: no remote copies, remote signals or barrier semaphores. Data moves between devices by JAX's collectives and lax.ppermute only.
A program may use at most 64 MiB of HBM per device.

```python
import jax
import jax.numpy as jnp

DIRS = 24
FREQS = 25
SUB = 4
NLON = 1024
NLAT = 256


def draw_spectrum(key, part):
    first = jax.random.fold_in(jax.random.fold_in(key, 17), 0)
    shape = (DIRS, FREQS, NLAT, NLON)
    ramp = 1.0 + 2.0 * jnp.arange(DIRS).astype(jnp.float32) / (DIRS - 1)
    base = jax.random.uniform(first, shape, jnp.float32, 0.3, 1.7)
    return (base * ramp[:, None, None, None]).astype(jnp.float32)


def place_ends(result, own_key, low, high):
    place = [jax.random.randint(jax.random.fold_in(own_key, axis), (), 0, length) for axis, length in enumerate(result.shape)]
    main_axis = result.shape.index(max(result.shape))
    beside = place[:main_axis] + [(place[main_axis] + 1) % result.shape[main_axis]] + place[main_axis + 1:]
    return result.at[tuple(place)].set(low).at[tuple(beside)].set(high)


def block_levels(rng, extent, shards, smallest, high):
    def one(axis_at, blocks):
        heights = jax.random.uniform(jax.random.fold_in(jax.random.fold_in(rng, 6), axis_at), (blocks,), jnp.float32, smallest / len(shards), high / len(shards))
        return jnp.repeat(jnp.exp(heights), extent[axis_at] // blocks).reshape((-1,) + (1,) * (len(extent) - axis_at - 1))

    level = one(*shards[0])
    for cut in shards[1:]:
        level = level * one(*cut)
    return level


def scatter_about(stream_key, extent, spread, bound, shards=(), kind=jnp.bfloat16):
    entries = jax.random.normal(stream_key, extent, jnp.float32) * spread
    if len(shards) > 0:
        entries = block_levels(stream_key, extent, shards, -0.22, 0.18) * entries
    return jnp.clip(entries, min=-bound, max=bound).astype(kind)


def setup_inputs(seed: int = 0) -> dict:
    streams_of = jax.random.split(jax.random.key(seed), 6)
    return {
        "spectrum": draw_spectrum(jax.random.fold_in(streams_of[5], 71), 0),
        "sea_mask": place_ends((jax.random.randint(streams_of[1], (NLAT, NLON), 0, 4) < 3).astype(jnp.int32), jax.random.fold_in(streams_of[1], 1), 0, 1),
        "turning": jnp.clip(jax.random.uniform(streams_of[2], (NLAT, NLON), jnp.float32, -0.4, 0.4) * block_levels(streams_of[2], (NLAT, NLON), ((0, 64),), -0.4, 0.0), -0.4, 0.4),
        "wind_u": scatter_about(streams_of[3], (NLAT, NLON), 1.0, 4.0, ((0, 64),), jnp.float32),
        "wind_v": scatter_about(streams_of[4], (NLAT, NLON), 1.0, 4.0, ((0, 64),), jnp.float32),
    }


def tables(dir_index):
    theta = 2.0 * jnp.pi * dir_index.astype(jnp.float32) / DIRS
    freq = jnp.arange(FREQS).astype(jnp.float32)
    fr = jnp.power(jnp.float32(1.1), freq - (FREQS // 2))
    speed = jnp.power(jnp.float32(1.1), -freq)
    rfac = 0.5 + 0.5 * speed
    mux = (0.42 * speed[None, :] * jnp.cos(theta)[:, None])[:, :, None, None]
    muy = (0.42 * speed[None, :] * jnp.sin(theta)[:, None])[:, :, None, None]
    return theta, fr, rfac, mux, muy


def reference(spectrum, sea_mask, turning, wind_u, wind_v):
    theta, fr, rfac, mux, muy = tables(jnp.arange(DIRS))
    sea = (sea_mask == 1).astype(jnp.float32)
    action = spectrum * sea
    mth = turning[None, None] * rfac[None, :, None, None]
    for step in range(SUB):
        padded = jnp.pad(action, ((0, 0), (0, 0), (1, 1), (1, 1)))
        south = padded[:, :, :-2, 1:-1]
        north = padded[:, :, 2:, 1:-1]
        west = padded[:, :, 1:-1, :-2]
        east = padded[:, :, 1:-1, 2:]
        before = jnp.roll(action, 1, axis=0)
        after = jnp.roll(action, -1, axis=0)
        fresh = action - jnp.maximum(mux, 0.0) * (action - west) - jnp.maximum(-mux, 0.0) * (action - east)
        fresh = fresh - jnp.maximum(muy, 0.0) * (action - south) - jnp.maximum(-muy, 0.0) * (action - north)
        fresh = fresh - jnp.maximum(mth, 0.0) * (action - before) - jnp.maximum(-mth, 0.0) * (action - after)
        action = fresh * sea
    fr_sq = (fr * fr)[None, :, None, None]
    mean_zero = jnp.sum(action, axis=(0, 1)) / (DIRS * FREQS)
    mean_two = jnp.sum(action * fr_sq, axis=(0, 1)) / (DIRS * FREQS)
    along = wind_u[None] * jnp.cos(theta)[:, None, None] + wind_v[None] * jnp.sin(theta)[:, None, None]
    growth = 0.5 * fr[None, :, None, None] * jnp.maximum(along, 0.0)[:, None]
    decay = 0.5 * fr_sq * (mean_two / (1.0 + mean_zero))[None, None]
    return action * (1.0 + growth) / (1.0 + decay)
```

```python
import functools

import jax
import jax.numpy as jnp
import numpy as np
from jax import lax
from jax.experimental import pallas as pl
from jax.experimental.pallas import tpu as pltpu
from jax.sharding import PartitionSpec as P

DIRS = 24
FREQS = 25
SUB = 4
INTERPRET = False

THETA = (np.float32(2.0 * np.pi) * np.arange(DIRS, dtype=np.float32) / np.float32(DIRS)).astype(
    np.float32
)
COS = np.cos(THETA).astype(np.float32)
SIN = np.sin(THETA).astype(np.float32)
FREQ = np.arange(FREQS, dtype=np.float64)
FR = (1.1 ** (FREQ - FREQS // 2)).astype(np.float32)
SPEED = (1.1 ** (-FREQ)).astype(np.float32)
RFAC = (np.float32(0.5) + np.float32(0.5) * SPEED).astype(np.float32)
CX = np.abs(np.float32(0.42) * SPEED[:, None] * COS[None, :]).astype(np.float32)
CY = np.abs(np.float32(0.42) * SPEED[:, None] * SIN[None, :]).astype(np.float32)
C0 = (1.0 - CX.astype(np.float64) - CY.astype(np.float64)).astype(np.float32)

LANES = 128
FULL = 3
TILES = FULL * 8 + 3
SLOTS = TILES + FULL + 2

SOUTH = [d for d in range(DIRS) if SIN[d] >= 0]
NORTH = [d for d in range(DIRS) if SIN[d] < 0]
REACH = SUB - 1
S_DIRS = [(SOUTH[0] - REACH + i) % DIRS for i in range(len(SOUTH) + 2 * REACH)]
N_DIRS = [(NORTH[0] - REACH + i) % DIRS for i in range(len(NORTH) + 2 * REACH)]
EXTRAS = []
for k in range(1, REACH + 1):
    EXTRAS += [
        ("s", (SOUTH[-1] + k) % DIRS, k),
        ("s", (SOUTH[0] - k) % DIRS, k),
        ("n", (NORTH[-1] + k) % DIRS, k),
        ("n", (NORTH[0] - k) % DIRS, k),
    ]
EXTRA_AT = {(w, d): i for i, (w, d, _) in enumerate(EXTRAS)}


def window(d):
    return "s" if d in SOUTH else "n"


def step_kernel(group, cx, cy, c0, rfac, frsq, own, south, north, sea, turn, out, st_a, st_b, ex_a, ex_b):
    me = group[0]
    f_of = lambda t: jnp.where(t < FULL * 8, me * FULL + t // 8, FREQS - 1)
    map_of = lambda t: jnp.where(t < FULL * 8, t % 8, t - FULL * 8 + 8)
    slot_of = lambda t: t + t // 8 + 1
    lane = lax.broadcasted_iota(jnp.int32, (8, LANES), 1)
    row = lax.broadcasted_iota(jnp.int32, (8, LANES), 0)
    first, last, mine = lane == 0, lane == LANES - 1, row >= 4
    zero = jnp.zeros((8, LANES), jnp.float32)
    pads = [i * 9 for i in range(FULL + 1)] + [SLOTS - 1]
    for p in pads:
        for d in range(DIRS):
            st_a[d, p] = zero
            st_b[d, p] = zero
        for i in range(len(EXTRAS)):
            ex_a[i, p] = zero
            ex_b[i, p] = zero

    def fill(t, carry):
        slot, m = slot_of(t), map_of(t)
        seas = {"s": sea[0, m], "n": sea[1, m]}
        halo = {"s": (south, S_DIRS), "n": (north, N_DIRS)}

        def whole(w, d):
            ref, dirs = halo[w]
            return jnp.concatenate([ref[dirs.index(d), t], own[d, t]], axis=0) * seas[w]

        for d in range(DIRS):
            st_a[d, slot] = whole(window(d), d)
        for i, (w, d, _) in enumerate(EXTRAS):
            ex_a[i, slot] = whole(w, d)
        return carry

    lax.fori_loop(0, TILES, fill, 0)

    def make(step, src, src_ex, dst, dst_ex):
        def body(t, carry):
            slot, m, f = slot_of(t), map_of(t), f_of(t)
            rf = rfac[f]
            seas = {"s": sea[0, m], "n": sea[1, m]}
            raw = {"s": turn[0, m], "n": turn[1, m]}
            mth = {w: jnp.abs(raw[w]) * rf for w in "sn"}
            ahead = {w: raw[w] > 0 for w in "sn"}
            loaded = {}

            def tile(w, d):
                d = d % DIRS
                key = (w, d)
                if window(d) == w or step == SUB - 1:
                    key = (window(d), d)
                if key not in loaded:
                    if key[0] == window(d):
                        loaded[key] = (src, d, src[d, slot])
                    else:
                        i = EXTRA_AT[key]
                        loaded[key] = (src_ex, i, src_ex[i, slot])
                return loaded[key]

            def update(w, d):
                ref, i, a = tile(w, d)
                before, after = tile(w, d - 1)[2], tile(w, d + 1)[2]
                if COS[d] >= 0:
                    x = jnp.where(first, pltpu.roll(ref[i, slot - 1], 1, 1), pltpu.roll(a, 1, 1))
                else:
                    x = jnp.where(
                        last,
                        pltpu.roll(ref[i, slot + 1], LANES - 1, 1),
                        pltpu.roll(a, LANES - 1, 1),
                    )
                y = pltpu.roll(a, 1 if SIN[d] >= 0 else 7, 0)
                turned = mth[w] * (jnp.where(ahead[w], before, after) - a)
                return (a * c0[f, d] + x * cx[f, d] + y * cy[f, d] + turned) * seas[w]

            fresh = {}
            total = None
            for d in range(DIRS):
                new = update(window(d), d)
                if step < SUB - 1:
                    fresh[d] = new
                    dst[d, slot] = new
                else:
                    total = new if total is None else total + new
                    keep(t, d, new)
            for i, (w, d, k) in enumerate(EXTRAS):
                if k < REACH - step:
                    dst_ex[i, slot] = jnp.where(mine, fresh[d], update(w, d))
            if total is not None:
                sums(t, f, total[4:8])
            return carry

        return body

    def keep(t, d, new):
        base = (d % 3) * FULL * 8

        @pl.when(t < FULL * 8)
        def _():
            out[d // 3, base + t] = new[4:8]

        @pl.when(t == FULL * 8 + 1)
        def _():
            out[d // 3, 3 * FULL * 8 + d % 3] = new[4:8]

    def sums(t, f, total):
        at = 3 * (FULL * 8 + 1)
        weighted = total * frsq[f]

        @pl.when(t < 8)
        def _():
            out[0, at + t] = total
            out[0, at + 8 + t] = weighted

        @pl.when(jnp.logical_and(t >= 8, t < FULL * 8))
        def _():
            out[0, at + t % 8] += total
            out[0, at + 8 + t % 8] += weighted

        @pl.when(t == FULL * 8 + 1)
        def _():
            out[0, at + me] += total
            out[0, at + 8 + me] += weighted

    bufs = [(st_a, ex_a), (st_b, ex_b)]
    for step in range(SUB):
        (src, src_ex), (dst, dst_ex) = bufs[step % 2], bufs[(step + 1) % 2]
        lax.fori_loop(0, TILES, make(step, src, src_ex, dst, dst_ex), 0)
    at = 3 * (FULL * 8 + 1)
    for i in range(16):
        value = out[0, at + i]
        for s in range(1, 8):
            out[s, at + i] = value


OUT_TILES = 3 * (FULL * 8 + 1) + 16


def step_call(group, own, south, north, sea, turn):
    smem = pl.BlockSpec(memory_space=pltpu.SMEM)
    vmem = pl.BlockSpec(memory_space=pltpu.VMEM)
    state = pltpu.VMEM((DIRS, SLOTS, 8, LANES), jnp.float32)
    extra = pltpu.VMEM((len(EXTRAS), SLOTS, 8, LANES), jnp.float32)
    return pl.pallas_call(
        step_kernel,
        out_shape=jax.ShapeDtypeStruct((8, OUT_TILES, 4, LANES), jnp.float32),
        in_specs=[smem] * 6 + [vmem] * 5,
        out_specs=vmem,
        scratch_shapes=[state, state, extra, extra],
        compiler_params=pltpu.CompilerParams(vmem_limit_bytes=40 * 1024 * 1024),
        interpret=INTERPRET,
        name="steps",
    )(group, CX, CY, C0, RFAC, FR * FR, own, south, north, sea, turn)


def source_kernel(cos, sin, got, wind_u, wind_v, out):
    at = 3 * (FULL * 8 + 1)
    inverse = 1.0 / (DIRS * FREQS)

    def body(t, carry):
        m0 = got[0, at + t]
        m2 = got[0, at + 8 + t]
        for j in range(1, 8):
            m0 = m0 + got[j, at + t]
            m2 = m2 + got[j, at + 8 + t]
        ratio = 0.5 * (m2 * inverse) / (1.0 + m0 * inverse)
        u, v = wind_u[t], wind_v[t]
        gain = [0.5 * jnp.maximum(u * cos[d] + v * sin[d], 0.0) for d in range(3)]
        for f in range(FREQS):
            fr = float(FR[f])
            shrink = 1.0 / (1.0 + ratio * (fr * fr))
            for d in range(3):
                if f < 8 * FULL:
                    a = got[f // FULL, (d * FULL + f % FULL) * 8 + t]
                else:
                    a = got[t, 3 * FULL * 8 + d]
                out[d, f, t] = a * (1.0 + gain[d] * fr) * shrink
        return carry

    lax.fori_loop(0, 8, body, 0)


def source_call(cos, sin, got, wind_u, wind_v):
    smem = pl.BlockSpec(memory_space=pltpu.SMEM)
    vmem = pl.BlockSpec(memory_space=pltpu.VMEM)
    return pl.pallas_call(
        source_kernel,
        out_shape=jax.ShapeDtypeStruct((3, FREQS, 8, 4, LANES), jnp.float32),
        in_specs=[smem] * 2 + [vmem] * 3,
        out_specs=vmem,
        compiler_params=pltpu.CompilerParams(vmem_limit_bytes=40 * 1024 * 1024),
        interpret=INTERPRET,
        name="source",
    )(cos, sin, got, wind_u, wind_v)


def tiled(rows):
    return jnp.swapaxes(rows.reshape(rows.shape[:-1] + (8, LANES)), -2, -3)


def on_device(spectrum, sea_mask, turning, wind_u, wind_v):
    me = lax.axis_index("spec")
    count = lax.axis_size("space")
    up = [(i, i + 1) for i in range(count - 1)]
    down = [(j, i) for i, j in up]

    maps = jnp.stack([tiled((sea_mask == 1).astype(jnp.float32)), tiled(turning)])
    maps_south = lax.ppermute(maps, "space", up)
    maps_north = lax.ppermute(maps, "space", down)

    x = tiled(spectrum)
    whole = x[:, : 8 * FULL].reshape(3, 8, FULL * 8, 4, LANES).transpose(1, 0, 2, 3, 4)
    lastf = jnp.pad(x[:, 8 * FULL], ((0, 0), (1, 1), (0, 0), (0, 0)))
    lastf = jnp.stack([lastf[:, j : j + 3] for j in range(8)])
    packed = jnp.concatenate([whole, lastf], axis=2)
    own = lax.all_to_all(packed, "spec", 0, 0, tiled=True).reshape(DIRS, TILES, 4, LANES)

    def pick(dirs):
        cut = next((i for i in range(1, len(dirs)) if dirs[i] < dirs[i - 1]), len(dirs))
        parts = [dirs[:cut], dirs[cut:]]
        return jnp.concatenate([own[p[0] : p[-1] + 1] for p in parts if p])

    south = lax.ppermute(pick(S_DIRS), "space", up)
    north = lax.ppermute(pick(N_DIRS), "space", down)

    pair = jnp.stack(
        [jnp.concatenate([maps_south, maps], axis=2), jnp.concatenate([maps_north, maps], axis=2)]
    )
    around = jnp.pad(pair, ((0, 0), (0, 0), (1, 1), (0, 0), (0, 0)))
    around = lax.dynamic_slice_in_dim(around, me, 3, axis=2)
    pair = jnp.concatenate([pair, around], axis=2)
    made = step_call(me.reshape(1), own, south, north, pair[:, 0], pair[:, 1])
    got = lax.all_to_all(made, "spec", 0, 0, tiled=True)
    cos = lax.dynamic_slice_in_dim(jnp.asarray(COS), me * 3, 3)
    sin = lax.dynamic_slice_in_dim(jnp.asarray(SIN), me * 3, 3)
    result = source_call(cos, sin, got, tiled(wind_u), tiled(wind_v))
    return jnp.swapaxes(result, -2, -3).reshape(3, FREQS, 4, 8 * LANES)


def solution(mesh):
    rows = P("space", None)
    bins = P("spec", None, "space", None)
    return jax.shard_map(
        on_device,
        mesh=mesh,
        in_specs=(bins, rows, rows, rows, rows),
        out_specs=bins,
        check_vma=False,
    )
```

```python
import functools

import jax
import jax.numpy as jnp
import numpy as np
from jax import lax
from jax.experimental import pallas as pl
from jax.experimental.pallas import tpu as pltpu
from jax.sharding import PartitionSpec as P

DIRS = 24
FREQS = 25
SUB = 4
INTERPRET = False

THETA = (np.float32(2.0 * np.pi) * np.arange(DIRS, dtype=np.float32) / np.float32(DIRS)).astype(
    np.float32
)
COS = np.cos(THETA).astype(np.float32)
SIN = np.sin(THETA).astype(np.float32)
FREQ = np.arange(FREQS, dtype=np.float64)
FR = (1.1 ** (FREQ - FREQS // 2)).astype(np.float32)
SPEED = (1.1 ** (-FREQ)).astype(np.float32)
RFAC = (np.float32(0.5) + np.float32(0.5) * SPEED).astype(np.float32)
CX = np.abs(np.float32(0.42) * SPEED[:, None] * COS[None, :]).astype(np.float32)
CY = np.abs(np.float32(0.42) * SPEED[:, None] * SIN[None, :]).astype(np.float32)
C0 = (1.0 - CX.astype(np.float64) - CY.astype(np.float64)).astype(np.float32)

LANES = 128
FULL = 3
TILES = FULL * 8 + 3
SLOTS = TILES + FULL + 2

SOUTH = [d for d in range(DIRS) if SIN[d] >= 0]
NORTH = [d for d in range(DIRS) if SIN[d] < 0]
REACH = SUB - 1
S_DIRS = [(SOUTH[0] - REACH + i) % DIRS for i in range(len(SOUTH) + 2 * REACH)]
N_DIRS = [(NORTH[0] - REACH + i) % DIRS for i in range(len(NORTH) + 2 * REACH)]
EXTRAS = []
for k in range(1, REACH + 1):
    EXTRAS += [
        ("s", (SOUTH[-1] + k) % DIRS, k),
        ("s", (SOUTH[0] - k) % DIRS, k),
        ("n", (NORTH[-1] + k) % DIRS, k),
        ("n", (NORTH[0] - k) % DIRS, k),
    ]
EXTRA_AT = {(w, d): i for i, (w, d, _) in enumerate(EXTRAS)}


def window(d):
    return "s" if d in SOUTH else "n"


def step_kernel(group, cx, cy, c0, rfac, frsq, own, south, north, sea, turn, out, st_a, st_b, ex_a, ex_b):
    me = group[0]

    def f_of(t):
        if isinstance(t, int):
            return FREQS - 1
        return jnp.where(t < FULL * 8, me * FULL + t // 8, FREQS - 1)

    def map_of(t):
        if isinstance(t, int):
            return t - FULL * 8 + 8
        return jnp.where(t < FULL * 8, t % 8, t - FULL * 8 + 8)

    slot_of = lambda t: t + t // 8 + 1
    lane = lax.broadcasted_iota(jnp.int32, (8, LANES), 1)
    row = lax.broadcasted_iota(jnp.int32, (8, LANES), 0)
    first, last, mine = lane == 0, lane == LANES - 1, row >= 4
    zero = jnp.zeros((8, LANES), jnp.float32)
    pads = [i * 9 for i in range(FULL + 1)] + [SLOTS - 1]
    for p in pads:
        for d in range(DIRS):
            st_a[d, p] = zero
            st_b[d, p] = zero
        for i in range(len(EXTRAS)):
            ex_a[i, p] = zero
            ex_b[i, p] = zero

    def fill(t, carry):
        slot, m = slot_of(t), map_of(t)
        seas = {"s": sea[0, m], "n": sea[1, m]}
        halo = {"s": (south, S_DIRS), "n": (north, N_DIRS)}

        def whole(w, d):
            ref, dirs = halo[w]
            return jnp.concatenate([ref[dirs.index(d), t], own[d, t]], axis=0) * seas[w]

        for d in range(DIRS):
            st_a[d, slot] = whole(window(d), d)
        for i, (w, d, _) in enumerate(EXTRAS):
            ex_a[i, slot] = whole(w, d)
        return carry

    lax.fori_loop(0, TILES, fill, 0)

    def make(step, src, src_ex, dst, dst_ex):
        def body(t, carry):
            slot, m, f = slot_of(t), map_of(t), f_of(t)
            rf = rfac[f]
            seas = {"s": sea[0, m], "n": sea[1, m]}
            raw = {"s": turn[0, m], "n": turn[1, m]}
            mth = {w: jnp.abs(raw[w]) * rf for w in "sn"}
            ahead = {w: raw[w] > 0 for w in "sn"}
            loaded = {}

            def tile(w, d):
                d = d % DIRS
                key = (w, d)
                if window(d) == w or step == SUB - 1:
                    key = (window(d), d)
                if key not in loaded:
                    if key[0] == window(d):
                        loaded[key] = (src, d, src[d, slot])
                    else:
                        i = EXTRA_AT[key]
                        loaded[key] = (src_ex, i, src_ex[i, slot])
                return loaded[key]

            def update(w, d):
                ref, i, a = tile(w, d)
                before, after = tile(w, d - 1)[2], tile(w, d + 1)[2]
                if COS[d] >= 0:
                    x = jnp.where(first, pltpu.roll(ref[i, slot - 1], 1, 1), pltpu.roll(a, 1, 1))
                else:
                    x = jnp.where(
                        last,
                        pltpu.roll(ref[i, slot + 1], LANES - 1, 1),
                        pltpu.roll(a, LANES - 1, 1),
                    )
                y = pltpu.roll(a, 1 if SIN[d] >= 0 else 7, 0)
                turned = mth[w] * (jnp.where(ahead[w], before, after) - a)
                return (a * c0[f, d] + x * cx[f, d] + y * cy[f, d] + turned) * seas[w]

            fresh = {}
            total = None
            for d in range(DIRS):
                new = update(window(d), d)
                if step < SUB - 1:
                    fresh[d] = new
                    dst[d, slot] = new
                else:
                    total = new if total is None else total + new
                    keep(t, d, new)
            for i, (w, d, k) in enumerate(EXTRAS):
                if k < REACH - step:
                    dst_ex[i, slot] = jnp.where(mine, fresh[d], update(w, d))
            if total is not None:
                sums(t, f, total[4:8])
            return carry

        return body

    at = 3 * (FULL * 8 + 1)

    def keep(t, d, new):
        if isinstance(t, int):
            out[d // 3, 3 * FULL * 8 + d % 3] = new[4:8]
        else:
            out[d // 3, (d % 3) * FULL * 8 + t] = new[4:8]

    def sums(t, f, total):
        place = me if isinstance(t, int) else t % 8
        out[0, at + place] += total
        out[0, at + 8 + place] += total * frsq[f]

    for i in range(16):
        out[0, at + i] = jnp.zeros((4, LANES), jnp.float32)

    bufs = [(st_a, ex_a), (st_b, ex_b)]
    for step in range(SUB):
        (src, src_ex), (dst, dst_ex) = bufs[step % 2], bufs[(step + 1) % 2]
        body = make(step, src, src_ex, dst, dst_ex)
        if step < SUB - 1:
            lax.fori_loop(0, TILES, body, 0)
        else:
            lax.fori_loop(0, FULL * 8, body, 0)
            body(FULL * 8 + 1, 0)
    for i in range(16):
        value = out[0, at + i]
        for s in range(1, 8):
            out[s, at + i] = value


OUT_TILES = 3 * (FULL * 8 + 1) + 16


def step_call(group, own, south, north, sea, turn):
    smem = pl.BlockSpec(memory_space=pltpu.SMEM)
    vmem = pl.BlockSpec(memory_space=pltpu.VMEM)
    state = pltpu.VMEM((DIRS, SLOTS, 8, LANES), jnp.float32)
    extra = pltpu.VMEM((len(EXTRAS), SLOTS, 8, LANES), jnp.float32)
    return pl.pallas_call(
        step_kernel,
        out_shape=jax.ShapeDtypeStruct((8, OUT_TILES, 4, LANES), jnp.float32),
        in_specs=[smem] * 6 + [vmem] * 5,
        out_specs=vmem,
        scratch_shapes=[state, state, extra, extra],
        compiler_params=pltpu.CompilerParams(vmem_limit_bytes=40 * 1024 * 1024),
        interpret=INTERPRET,
        name="steps",
    )(group, CX, CY, C0, RFAC, FR * FR, own, south, north, sea, turn)


def source_kernel(cos, sin, got, wind_u, wind_v, out):
    at = 3 * (FULL * 8 + 1)
    inverse = 1.0 / (DIRS * FREQS)

    def body(t, carry):
        m0 = got[0, at + t]
        m2 = got[0, at + 8 + t]
        for j in range(1, 8):
            m0 = m0 + got[j, at + t]
            m2 = m2 + got[j, at + 8 + t]
        ratio = 0.5 * (m2 * inverse) / (1.0 + m0 * inverse)
        u, v = wind_u[t], wind_v[t]
        gain = [0.5 * jnp.maximum(u * cos[d] + v * sin[d], 0.0) for d in range(3)]
        for f in range(FREQS):
            fr = float(FR[f])
            shrink = 1.0 / (1.0 + ratio * (fr * fr))
            for d in range(3):
                if f < 8 * FULL:
                    a = got[f // FULL, (d * FULL + f % FULL) * 8 + t]
                else:
                    a = got[t, 3 * FULL * 8 + d]
                out[d, f, t] = a * (1.0 + gain[d] * fr) * shrink
        return carry

    lax.fori_loop(0, 8, body, 0)


def source_call(cos, sin, got, wind_u, wind_v):
    smem = pl.BlockSpec(memory_space=pltpu.SMEM)
    vmem = pl.BlockSpec(memory_space=pltpu.VMEM)
    return pl.pallas_call(
        source_kernel,
        out_shape=jax.ShapeDtypeStruct((3, FREQS, 8, 4, LANES), jnp.float32),
        in_specs=[smem] * 2 + [vmem] * 3,
        out_specs=vmem,
        compiler_params=pltpu.CompilerParams(vmem_limit_bytes=40 * 1024 * 1024),
        interpret=INTERPRET,
        name="source",
    )(cos, sin, got, wind_u, wind_v)


def tiled(rows):
    return jnp.swapaxes(rows.reshape(rows.shape[:-1] + (8, LANES)), -2, -3)


def on_device(spectrum, sea_mask, turning, wind_u, wind_v):
    me = lax.axis_index("spec")
    count = lax.axis_size("space")
    up = [(i, i + 1) for i in range(count - 1)]
    down = [(j, i) for i, j in up]

    maps = jnp.stack([tiled((sea_mask == 1).astype(jnp.float32)), tiled(turning)])
    maps_south = lax.ppermute(maps, "space", up)
    maps_north = lax.ppermute(maps, "space", down)

    x = tiled(spectrum)
    whole = x[:, : 8 * FULL].reshape(3, 8, FULL * 8, 4, LANES).transpose(1, 0, 2, 3, 4)
    lastf = jnp.pad(x[:, 8 * FULL], ((0, 0), (1, 1), (0, 0), (0, 0)))
    lastf = jnp.stack([lastf[:, j : j + 3] for j in range(8)])
    packed = jnp.concatenate([whole, lastf], axis=2)
    own = lax.all_to_all(packed, "spec", 0, 0, tiled=True).reshape(DIRS, TILES, 4, LANES)

    def pick(dirs):
        cut = next((i for i in range(1, len(dirs)) if dirs[i] < dirs[i - 1]), len(dirs))
        parts = [dirs[:cut], dirs[cut:]]
        return jnp.concatenate([own[p[0] : p[-1] + 1] for p in parts if p])

    south = lax.ppermute(pick(S_DIRS), "space", up)
    north = lax.ppermute(pick(N_DIRS), "space", down)

    pair = jnp.stack(
        [jnp.concatenate([maps_south, maps], axis=2), jnp.concatenate([maps_north, maps], axis=2)]
    )
    around = jnp.pad(pair, ((0, 0), (0, 0), (1, 1), (0, 0), (0, 0)))
    around = lax.dynamic_slice_in_dim(around, me, 3, axis=2)
    pair = jnp.concatenate([pair, around], axis=2)
    made = step_call(me.reshape(1), own, south, north, pair[:, 0], pair[:, 1])
    got = lax.all_to_all(made, "spec", 0, 0, tiled=True)
    cos = lax.dynamic_slice_in_dim(jnp.asarray(COS), me * 3, 3)
    sin = lax.dynamic_slice_in_dim(jnp.asarray(SIN), me * 3, 3)
    result = source_call(cos, sin, got, tiled(wind_u), tiled(wind_v))
    return jnp.swapaxes(result, -2, -3).reshape(3, FREQS, 4, 8 * LANES)


def solution(mesh):
    rows = P("space", None)
    bins = P("spec", None, "space", None)
    return jax.shard_map(
        on_device,
        mesh=mesh,
        in_specs=(bins, rows, rows, rows, rows),
        out_specs=bins,
        check_vma=False,
    )
```

```python
import functools

import jax
import jax.numpy as jnp
import numpy as np
from jax import lax
from jax.experimental import pallas as pl
from jax.experimental.pallas import tpu as pltpu
from jax.sharding import PartitionSpec as P

DIRS = 24
FREQS = 25
SUB = 4
INTERPRET = False
LANES = 128
BLOCKS = 8

THETA = (np.float32(2.0 * np.pi) * np.arange(DIRS, dtype=np.float32) / np.float32(DIRS)).astype(
    np.float32
)
COS = np.cos(THETA).astype(np.float32)
SIN = np.sin(THETA).astype(np.float32)
FREQ = np.arange(FREQS, dtype=np.float64)
FR = (1.1 ** (FREQ - FREQS // 2)).astype(np.float32)
SPEED = (1.1 ** (-FREQ)).astype(np.float32)
RFAC = (np.float32(0.5) + np.float32(0.5) * SPEED).astype(np.float32)


def grouped(values):
    kept, place = [], []
    for v in values:
        near = [i for i, k in enumerate(kept) if abs(k - v) <= 4e-7 * abs(k)]
        if not near:
            kept.append(float(v))
        place.append(near[0] if near else len(kept) - 1)
    return kept, place


WEIGHTS, PLACE = grouped(np.abs(np.concatenate([COS, SIN])).astype(np.float64))
KX, KY = PLACE[:DIRS], PLACE[DIRS:]
REST, K0 = grouped([WEIGHTS[KX[d]] + WEIGHTS[KY[d]] for d in range(DIRS)])
COEF = np.concatenate(
    [
        0.42 * SPEED.astype(np.float64)[:, None] * np.array(WEIGHTS)[None, :],
        1.0 - 0.42 * SPEED.astype(np.float64)[:, None] * np.array(REST)[None, :],
    ],
    axis=1,
).astype(np.float32)

FULL = 3
CHUNKS = ((0, 2, False), (2, 1, True))

SOUTH = [d for d in range(DIRS) if SIN[d] >= 0]
NORTH = [d for d in range(DIRS) if SIN[d] < 0]
REACH = SUB - 1
PLANES = len(SOUTH) + REACH
EXTRAS = []
for k in range(1, REACH + 1):
    EXTRAS += [
        ("s", (SOUTH[-1] + k) % DIRS, k),
        ("s", (SOUTH[0] - k) % DIRS, k),
        ("n", (NORTH[-1] + k) % DIRS, k),
        ("n", (NORTH[0] - k) % DIRS, k),
    ]
EXTRA_AT = {(w, d): i for i, (w, d, _) in enumerate(EXTRAS)}
VMEM_LIMIT = 40 * 1024 * 1024


def window(d):
    return "s" if d in SOUTH else "n"


def tiles_of(chunk):
    return chunk[1] * BLOCKS + (3 if chunk[2] else 0)


def slots_of(chunk):
    return tiles_of(chunk) + chunk[1] + (2 if chunk[2] else 1)


def made_of(chunk):
    return 3 * (chunk[1] * BLOCKS + (1 if chunk[2] else 0))


def smem():
    return pl.BlockSpec(memory_space=pltpu.SMEM)


def vmem():
    return pl.BlockSpec(memory_space=pltpu.VMEM)


def call(kernel, name, out, args, n_smem, scratch=(), cost=4_000_000):
    return pl.pallas_call(
        kernel,
        out_shape=jax.tree.map(lambda s: jax.ShapeDtypeStruct(s, jnp.float32), out, is_leaf=lambda s: isinstance(s, tuple) and isinstance(s[0], int)),
        in_specs=[smem()] * n_smem + [vmem()] * (len(args) - n_smem),
        out_specs=jax.tree.map(lambda s: vmem(), out, is_leaf=lambda s: isinstance(s, tuple) and isinstance(s[0], int)),
        scratch_shapes=list(scratch),
        compiler_params=pltpu.CompilerParams(vmem_limit_bytes=VMEM_LIMIT),
        cost_estimate=pl.CostEstimate(flops=1000, bytes_accessed=cost, transcendentals=0),
        interpret=INTERPRET,
        name=name,
    )(*args)


def pack_kernel(x, *outs):
    zero = jnp.zeros((4, LANES), jnp.float32)
    for (first, count, tail), out in zip(CHUNKS, outs):
        for d in range(3):
            for j in range(BLOCKS):
                for i in range(count):
                    for l in range(BLOCKS):
                        f = j * FULL + first + i
                        out[j, d, i * BLOCKS + l] = x[d, f, :, l * LANES : (l + 1) * LANES]
                if tail:
                    for i in range(3):
                        l = j + i - 1
                        inside = 0 <= l < BLOCKS
                        value = x[d, FREQS - 1, :, l * LANES : (l + 1) * LANES] if inside else zero
                        out[j, d, count * BLOCKS + i] = value


def halo_kernel(tiles, with_maps, *refs):
    if with_maps:
        own, maps, up, down = refs
        for k in range(2):
            for l in range(BLOCKS):
                value = maps[k, :, l * LANES : (l + 1) * LANES]
                up[PLANES * tiles + k * BLOCKS + l] = value
                down[PLANES * tiles + k * BLOCKS + l] = value
    else:
        own, up, down = refs
    ends = {
        "s": (SOUTH[-1], SOUTH[0]),
        "n": (NORTH[0], NORTH[-1]),
    }
    n = len(SOUTH)

    def body(t, carry):
        for i, d in enumerate(SOUTH):
            up[i * tiles + t] = own[d, t]
        for i, d in enumerate(NORTH):
            down[i * tiles + t] = own[d, t]
        top, low = ends["s"]
        a = [own[(top + k) % DIRS, t] for k in range(1, 4)]
        b = [own[(low - k) % DIRS, t] for k in range(1, 4)]
        up[n * tiles + t] = jnp.concatenate([a[2][3:4], a[0][1:4]], axis=0)
        up[(n + 1) * tiles + t] = jnp.concatenate([b[1][2:4], a[1][2:4]], axis=0)
        up[(n + 2) * tiles + t] = jnp.concatenate([b[2][3:4], b[0][1:4]], axis=0)
        low, top = ends["n"]
        a = [own[(low - k) % DIRS, t] for k in range(1, 4)]
        b = [own[(top + k) % DIRS, t] for k in range(1, 4)]
        down[n * tiles + t] = jnp.concatenate([a[0][0:3], a[2][0:1]], axis=0)
        down[(n + 1) * tiles + t] = jnp.concatenate([a[1][0:2], b[1][0:2]], axis=0)
        down[(n + 2) * tiles + t] = jnp.concatenate([b[0][0:3], b[2][0:1]], axis=0)
        return carry

    lax.fori_loop(0, tiles, body, 0)


def step_kernel(chunk, first_call, group, coef, rfac, frsq, own, south, north, *refs):
    begin, count, tail = chunk
    tiles, slots, made = tiles_of(chunk), slots_of(chunk), made_of(chunk)
    if first_call:
        maps, out, around, sums, st_a, st_b, ex_a, ex_b = refs
    else:
        around, given, out, st_a, st_b, ex_a, ex_b = refs
        sums = None
    me = group[0]
    whole = count * BLOCKS

    def f_of(t):
        if isinstance(t, int):
            return FREQS - 1
        f = me * FULL + begin + t // BLOCKS
        return jnp.where(t < whole, f, FREQS - 1) if tail else f

    def map_of(t):
        if isinstance(t, int):
            return me + t - whole
        l = t % BLOCKS + 1
        return jnp.where(t < whole, l, me + t - whole) if tail else l

    def slot_of(t):
        return t + t // BLOCKS + 1

    lane = lax.broadcasted_iota(jnp.int32, (8, LANES), 1)
    row = lax.broadcasted_iota(jnp.int32, (8, LANES), 0)
    start, end, mine = lane == 0, lane == LANES - 1, row < 4
    zero = jnp.zeros((8, LANES), jnp.float32)
    for p in [i * (BLOCKS + 1) for i in range(count + 1)] + ([slots - 1] if tail else []):
        for d in range(DIRS):
            st_a[d, p] = zero
            st_b[d, p] = zero
        for i in range(len(EXTRAS)):
            ex_a[i, p] = zero
            ex_b[i, p] = zero

    if first_call:
        at = PLANES * tiles
        for k in range(2):
            for w, ref in enumerate((south, north)):
                around[k, w, 0] = zero
                around[k, w, BLOCKS + 1] = zero
                for l in range(BLOCKS):
                    mid = maps[k, :, l * LANES : (l + 1) * LANES]
                    around[k, w, l + 1] = jnp.concatenate([mid, ref[at + k * BLOCKS + l]], axis=0)

    def fill(t, carry):
        slot, m = slot_of(t), map_of(t)
        seas = {"s": around[0, 0, m], "n": around[0, 1, m]}
        n = len(SOUTH)

        def whole_tile(w, d, rows):
            return jnp.concatenate([own[d, t], rows], axis=0) * seas[w]

        for i, d in enumerate(SOUTH):
            st_a[d, slot] = whole_tile("s", d, south[i * tiles + t])
        for i, d in enumerate(NORTH):
            st_a[d, slot] = whole_tile("n", d, north[i * tiles + t])
        for w, ref in (("s", south), ("n", north)):
            a, b, c = (ref[(n + i) * tiles + t] for i in range(3))
            swap = jnp.concatenate([b[2:4], b[0:2]], axis=0)
            pick = slice(0, 1) if w == "s" else slice(3, 4)
            far_a = jnp.broadcast_to(a[pick], (4, LANES))
            far_c = jnp.broadcast_to(c[pick], (4, LANES))
            if w == "s":
                top, low = SOUTH[-1], SOUTH[0]
                line = [(top + 1, a), (top + 2, b), (top + 3, far_a)]
                line += [(low - 1, c), (low - 2, swap), (low - 3, far_c)]
            else:
                low, top = NORTH[0], NORTH[-1]
                line = [(low - 1, a), (low - 2, b), (low - 3, far_a)]
                line += [(top + 1, c), (top + 2, swap), (top + 3, far_c)]
            for d, rows in line:
                ex_a[EXTRA_AT[w, d % DIRS], slot] = whole_tile(w, d % DIRS, rows)
        return carry

    lax.fori_loop(0, tiles, fill, 0)

    if first_call:
        for i in range(2 * BLOCKS):
            sums[i] = jnp.zeros((4, LANES), jnp.float32)
    else:
        for i in range(2 * BLOCKS):
            out[0, made + i] = given[i]

    def keep(t, d, new):
        if isinstance(t, int):
            out[d // 3, 3 * whole + d % 3] = new[0:4]
        else:
            out[d // 3, (d % 3) * whole + t] = new[0:4]

    def add_up(t, f, total):
        place = me if isinstance(t, int) else t % BLOCKS
        total = total[0:4]
        if first_call:
            sums[place] += total
            sums[BLOCKS + place] += total * frsq[f]
        else:
            out[0, made + place] += total
            out[0, made + BLOCKS + place] += total * frsq[f]

    def make(step, src, src_ex, dst, dst_ex):
        def body(t, carry):
            slot, m, f = slot_of(t), map_of(t), f_of(t)
            rf = rfac[f]
            coefs = [coef[f, i] for i in range(COEF.shape[1])]
            seas = {"s": around[0, 0, m], "n": around[0, 1, m]}
            raw = {"s": around[1, 0, m], "n": around[1, 1, m]}
            mth = {w: jnp.abs(raw[w]) * rf for w in "sn"}
            ahead = {w: raw[w] > 0 for w in "sn"}
            loaded = {}

            def tile(w, d):
                d = d % DIRS
                key = (w, d)
                if window(d) == w or step == SUB - 1:
                    key = (window(d), d)
                if key not in loaded:
                    if key[0] == window(d):
                        loaded[key] = (src, d, src[d, slot])
                    else:
                        i = EXTRA_AT[key]
                        loaded[key] = (src_ex, i, src_ex[i, slot])
                return loaded[key]

            def update(w, d):
                ref, i, a = tile(w, d)
                before, after = tile(w, d - 1)[2], tile(w, d + 1)[2]
                if COS[d] >= 0:
                    x = pltpu.roll(jnp.where(end, ref[i, slot - 1], a), 1, 1)
                else:
                    x = pltpu.roll(jnp.where(start, ref[i, slot + 1], a), LANES - 1, 1)
                y = pltpu.roll(a, 1 if SIN[d] >= 0 else 7, 0)
                turned = mth[w] * (jnp.where(ahead[w], before, after) - a)
                stay = coefs[len(WEIGHTS) + K0[d]]
                return (a * stay + x * coefs[KX[d]] + y * coefs[KY[d]] + turned) * seas[w]

            fresh = {}
            total = None
            for d in range(DIRS):
                new = update(window(d), d)
                if step < SUB - 1:
                    fresh[d] = new
                    dst[d, slot] = new
                else:
                    keep(t, d, new)
                    total = new if total is None else total + new
            for i, (w, d, k) in enumerate(EXTRAS):
                if k < REACH - step:
                    dst_ex[i, slot] = jnp.where(mine, fresh[d], update(w, d))
            if total is not None:
                add_up(t, f, total)
            return carry

        return body

    bufs = [(st_a, ex_a), (st_b, ex_b)]
    for step in range(SUB):
        (src, src_ex), (dst, dst_ex) = bufs[step % 2], bufs[(step + 1) % 2]
        body = make(step, src, src_ex, dst, dst_ex)
        if step < SUB - 1:
            lax.fori_loop(0, tiles, body, 0)
        else:
            lax.fori_loop(0, whole, body, 0)
            if tail:
                body(whole + 1, 0)
    if not first_call:
        for i in range(2 * BLOCKS):
            value = out[0, made + i]
            for s in range(1, BLOCKS):
                out[s, made + i] = value


def step_call(chunk, first_call, group, own, south, north, rest):
    slots, made = slots_of(chunk), made_of(chunk)
    state = pltpu.VMEM((DIRS, slots, 8, LANES), jnp.float32)
    extra = pltpu.VMEM((len(EXTRAS), slots, 8, LANES), jnp.float32)
    if first_call:
        out = [(BLOCKS, made, 4, LANES), (2, 2, BLOCKS + 2, 8, LANES), (2 * BLOCKS, 4, LANES)]
    else:
        out = [(BLOCKS, made + 2 * BLOCKS, 4, LANES)]
    args = (group, COEF, RFAC, FR * FR, own, south, north, *rest)
    return call(
        functools.partial(step_kernel, chunk, first_call),
        "steps",
        out,
        args,
        4,
        [state, state, extra, extra],
        20_000_000,
    )


def source_kernel(cos, sin, *refs):
    gots, (wind_u, wind_v, out) = refs[: len(CHUNKS)], refs[len(CHUNKS) :]
    last = gots[-1]
    at = made_of(CHUNKS[-1])
    inverse = 1.0 / (DIRS * FREQS)

    for t in range(BLOCKS):
        cols = slice(t * LANES, (t + 1) * LANES)
        m0 = last[0, at + t]
        m2 = last[0, at + BLOCKS + t]
        for j in range(1, BLOCKS):
            m0 = m0 + last[j, at + t]
            m2 = m2 + last[j, at + BLOCKS + t]
        ratio = 0.5 * (m2 * inverse) / (1.0 + m0 * inverse)
        u, v = wind_u[:, cols], wind_v[:, cols]
        gain = [0.5 * jnp.maximum(u * cos[d] + v * sin[d], 0.0) for d in range(3)]
        for (first, count, tail), got in zip(CHUNKS, gots):
            where = [
                (j * FULL + first + i, j, i * BLOCKS + t, count * BLOCKS)
                for j in range(BLOCKS)
                for i in range(count)
            ]
            if tail:
                where.append((FREQS - 1, t, 3 * count * BLOCKS, 1))
            for f, j, base, stride in where:
                fr = float(FR[f])
                shrink = 1.0 / (1.0 + ratio * (fr * fr))
                for d in range(3):
                    out[d, f, :, cols] = got[j, base + d * stride] * (1.0 + gain[d] * fr) * shrink


def on_device(spectrum, sea_mask, turning, wind_u, wind_v):
    me = lax.axis_index("spec")
    group = me.reshape(1)
    count = lax.axis_size("space")
    up = [(i, i + 1) for i in range(count - 1)]
    down = [(j, i) for i, j in up]

    maps = jnp.stack([(sea_mask == 1).astype(jnp.float32), turning])
    packs = call(
        pack_kernel,
        "pack",
        [(BLOCKS, 3, tiles_of(c), 4, LANES) for c in CHUNKS],
        (spectrum,),
        0,
    )
    rows = []
    hold = None
    for i, chunk in enumerate(CHUNKS):
        tiles = tiles_of(chunk)
        pack = packs[i]
        if hold is not None:
            pack, hold = lax.optimization_barrier((pack, hold))
            rows[-1] = (rows[-1][0],) + tuple(hold)
        own = lax.all_to_all(pack, "spec", 0, 0, tiled=True).reshape(DIRS, tiles, 4, LANES)
        size = PLANES * tiles + (2 * BLOCKS if i == 0 else 0)
        args = (own, maps) if i == 0 else (own,)
        edges = call(
            functools.partial(halo_kernel, tiles, i == 0), "halo", [(size, 4, LANES)] * 2, args, 0
        )
        rows.append((own, edges[0], edges[1]))
        hold = (edges[0], edges[1])
    (own, u, d), (own_2, u_2, d_2) = rows
    south, north = lax.ppermute(u, "space", up), lax.ppermute(d, "space", down)
    south, north, _, _ = lax.optimization_barrier((south, north, u_2, d_2))
    south_2, north_2 = lax.ppermute(u_2, "space", up), lax.ppermute(d_2, "space", down)
    rows = [(own, south, north), (own_2, south_2, north_2)]

    made, around, sums = step_call(CHUNKS[0], True, group, *rows[0], (maps,))
    made, south_2, north_2 = lax.optimization_barrier((made, south_2, north_2))
    gots = [lax.all_to_all(made, "spec", 0, 0, tiled=True)]
    (made,) = step_call(CHUNKS[1], False, group, own_2, south_2, north_2, (around, sums))
    made, gots = lax.optimization_barrier((made, gots))
    gots.append(lax.all_to_all(made, "spec", 0, 0, tiled=True))
    cos = lax.dynamic_slice_in_dim(jnp.asarray(COS), me * 3, 3)
    sin = lax.dynamic_slice_in_dim(jnp.asarray(SIN), me * 3, 3)
    return call(
        source_kernel,
        "source",
        (3, FREQS, 4, BLOCKS * LANES),
        (cos, sin, *gots, wind_u, wind_v),
        2,
    )


def solution(mesh):
    rows = P("space", None)
    bins = P("spec", None, "space", None)
    return jax.shard_map(
        on_device,
        mesh=mesh,
        in_specs=(bins, rows, rows, rows, rows),
        out_specs=bins,
        check_vma=False,
    )
```

```python
import functools

import jax
import jax.numpy as jnp
import numpy as np
from jax import lax
from jax.experimental import pallas as pl
from jax.experimental.pallas import tpu as pltpu
from jax.sharding import PartitionSpec as P

DIRS = 24
FREQS = 25
SUB = 4
INTERPRET = False
LANES = 128
BLOCKS = 8

THETA = (np.float32(2.0 * np.pi) * np.arange(DIRS, dtype=np.float32) / np.float32(DIRS)).astype(
    np.float32
)
COS = np.cos(THETA).astype(np.float32)
SIN = np.sin(THETA).astype(np.float32)
FREQ = np.arange(FREQS, dtype=np.float64)
FR = (1.1 ** (FREQ - FREQS // 2)).astype(np.float32)
SPEED = (1.1 ** (-FREQ)).astype(np.float32)
RFAC = (np.float32(0.5) + np.float32(0.5) * SPEED).astype(np.float32)


def grouped(values):
    kept, place = [], []
    for v in values:
        near = [i for i, k in enumerate(kept) if abs(k - v) <= 4e-7 * abs(k)]
        if not near:
            kept.append(float(v))
        place.append(near[0] if near else len(kept) - 1)
    return kept, place


WEIGHTS, PLACE = grouped(np.abs(np.concatenate([COS, SIN])).astype(np.float64))
KX, KY = PLACE[:DIRS], PLACE[DIRS:]
REST, K0 = grouped([WEIGHTS[KX[d]] + WEIGHTS[KY[d]] for d in range(DIRS)])
COEF = np.concatenate(
    [
        0.42 * SPEED.astype(np.float64)[:, None] * np.array(WEIGHTS)[None, :],
        1.0 - 0.42 * SPEED.astype(np.float64)[:, None] * np.array(REST)[None, :],
    ],
    axis=1,
).astype(np.float32)

FULL = 3
CHUNKS = ((0, 2, False), (2, 1, True))
WHOLE = FULL * BLOCKS
TILES = WHOLE + 3
SUMS_AT = 3 * (WHOLE + 1)
MADE = SUMS_AT + 2 * BLOCKS

SOUTH = [d for d in range(DIRS) if SIN[d] >= 0]
NORTH = [d for d in range(DIRS) if SIN[d] < 0]
REACH = SUB - 1
PLANES = len(SOUTH) + REACH
EXTRAS = []
for k in range(1, REACH + 1):
    EXTRAS += [
        ("s", (SOUTH[-1] + k) % DIRS, k),
        ("s", (SOUTH[0] - k) % DIRS, k),
        ("n", (NORTH[-1] + k) % DIRS, k),
        ("n", (NORTH[0] - k) % DIRS, k),
    ]
EXTRA_AT = {(w, d): i for i, (w, d, _) in enumerate(EXTRAS)}
VMEM_LIMIT = 40 * 1024 * 1024


def window(d):
    return "s" if d in SOUTH else "n"


def tiles_of(chunk):
    return chunk[1] * BLOCKS + (3 if chunk[2] else 0)


def slots_of(chunk):
    return tiles_of(chunk) + chunk[1] + (2 if chunk[2] else 1)


def smem():
    return pl.BlockSpec(memory_space=pltpu.SMEM)


def vmem():
    return pl.BlockSpec(memory_space=pltpu.VMEM)


def call(kernel, name, out, args, n_smem, scratch=(), cost=4_000_000):
    return pl.pallas_call(
        kernel,
        out_shape=jax.tree.map(lambda s: jax.ShapeDtypeStruct(s, jnp.float32), out, is_leaf=lambda s: isinstance(s, tuple) and isinstance(s[0], int)),
        in_specs=[smem()] * n_smem + [vmem()] * (len(args) - n_smem),
        out_specs=jax.tree.map(lambda s: vmem(), out, is_leaf=lambda s: isinstance(s, tuple) and isinstance(s[0], int)),
        scratch_shapes=list(scratch),
        compiler_params=pltpu.CompilerParams(vmem_limit_bytes=VMEM_LIMIT),
        cost_estimate=pl.CostEstimate(flops=1000, bytes_accessed=cost, transcendentals=0),
        interpret=INTERPRET,
        name=name,
    )(*args)


def pack_kernel(spectrum, out, x, arrived):
    copies = [pltpu.make_async_copy(spectrum.at[d], x.at[d], arrived.at[d]) for d in range(3)]
    for copy in copies:
        copy.start()
    zero = jnp.zeros((4, LANES), jnp.float32)
    for d in range(3):
        copies[d].wait()
        for j in range(BLOCKS):
            for i in range(FULL):
                for l in range(BLOCKS):
                    value = x[d, j * FULL + i, :, l * LANES : (l + 1) * LANES]
                    out[j, d, i * BLOCKS + l] = value
            for i in range(3):
                l = j + i - 1
                inside = 0 <= l < BLOCKS
                value = x[d, FREQS - 1, :, l * LANES : (l + 1) * LANES] if inside else zero
                out[j, d, WHOLE + i] = value


def halo_kernel(origin, tiles, with_maps, *refs):
    if with_maps:
        own, maps, up, down = refs
        for k in range(2):
            for l in range(BLOCKS):
                value = maps[k, :, l * LANES : (l + 1) * LANES]
                up[PLANES * tiles + k * BLOCKS + l] = value
                down[PLANES * tiles + k * BLOCKS + l] = value
    else:
        own, up, down = refs
    ends = {
        "s": (SOUTH[-1], SOUTH[0]),
        "n": (NORTH[0], NORTH[-1]),
    }
    n = len(SOUTH)

    def body(t, carry):
        at = origin + t
        for i, d in enumerate(SOUTH):
            up[i * tiles + t] = own[d, at]
        for i, d in enumerate(NORTH):
            down[i * tiles + t] = own[d, at]
        top, low = ends["s"]
        a = [own[(top + k) % DIRS, at] for k in range(1, 4)]
        b = [own[(low - k) % DIRS, at] for k in range(1, 4)]
        up[n * tiles + t] = jnp.concatenate([a[2][3:4], a[0][1:4]], axis=0)
        up[(n + 1) * tiles + t] = jnp.concatenate([b[1][2:4], a[1][2:4]], axis=0)
        up[(n + 2) * tiles + t] = jnp.concatenate([b[2][3:4], b[0][1:4]], axis=0)
        low, top = ends["n"]
        a = [own[(low - k) % DIRS, at] for k in range(1, 4)]
        b = [own[(top + k) % DIRS, at] for k in range(1, 4)]
        down[n * tiles + t] = jnp.concatenate([a[0][0:3], a[2][0:1]], axis=0)
        down[(n + 1) * tiles + t] = jnp.concatenate([a[1][0:2], b[1][0:2]], axis=0)
        down[(n + 2) * tiles + t] = jnp.concatenate([b[0][0:3], b[2][0:1]], axis=0)
        return carry

    lax.fori_loop(0, tiles, body, 0)


def step_kernel(chunk, first_call, group, coef, rfac, frsq, own, south, north, *refs):
    begin, count, tail = chunk
    tiles, slots, origin = tiles_of(chunk), slots_of(chunk), begin * BLOCKS
    if first_call:
        maps, out, around, st_a, st_b, ex_a, ex_b = refs
    else:
        around, given, out, st_a, st_b, ex_a, ex_b = refs
    me = group[0]
    whole = count * BLOCKS

    def f_of(t):
        if isinstance(t, int):
            return FREQS - 1
        f = me * FULL + begin + t // BLOCKS
        return jnp.where(t < whole, f, FREQS - 1) if tail else f

    def map_of(t):
        if isinstance(t, int):
            return me + t - whole
        l = t % BLOCKS + 1
        return jnp.where(t < whole, l, me + t - whole) if tail else l

    def slot_of(t):
        return t + t // BLOCKS + 1

    lane = lax.broadcasted_iota(jnp.int32, (8, LANES), 1)
    row = lax.broadcasted_iota(jnp.int32, (8, LANES), 0)
    start, end, mine = lane == 0, lane == LANES - 1, row < 4
    zero = jnp.zeros((8, LANES), jnp.float32)
    for p in [i * (BLOCKS + 1) for i in range(count + 1)] + ([slots - 1] if tail else []):
        for d in range(DIRS):
            st_a[d, p] = zero
            st_b[d, p] = zero
        for i in range(len(EXTRAS)):
            ex_a[i, p] = zero
            ex_b[i, p] = zero

    if first_call:
        at = PLANES * tiles
        for k in range(2):
            for w, ref in enumerate((south, north)):
                around[k, w, 0] = zero
                around[k, w, BLOCKS + 1] = zero
                for l in range(BLOCKS):
                    mid = maps[k, :, l * LANES : (l + 1) * LANES]
                    around[k, w, l + 1] = jnp.concatenate([mid, ref[at + k * BLOCKS + l]], axis=0)

    def fill(t, carry):
        slot, m = slot_of(t), map_of(t)
        seas = {"s": around[0, 0, m], "n": around[0, 1, m]}
        n = len(SOUTH)

        def whole_tile(w, d, rows):
            return jnp.concatenate([own[d, origin + t], rows], axis=0) * seas[w]

        for i, d in enumerate(SOUTH):
            st_a[d, slot] = whole_tile("s", d, south[i * tiles + t])
        for i, d in enumerate(NORTH):
            st_a[d, slot] = whole_tile("n", d, north[i * tiles + t])
        for w, ref in (("s", south), ("n", north)):
            a, b, c = (ref[(n + i) * tiles + t] for i in range(3))
            swap = jnp.concatenate([b[2:4], b[0:2]], axis=0)
            pick = slice(0, 1) if w == "s" else slice(3, 4)
            far_a = jnp.broadcast_to(a[pick], (4, LANES))
            far_c = jnp.broadcast_to(c[pick], (4, LANES))
            if w == "s":
                top, low = SOUTH[-1], SOUTH[0]
                line = [(top + 1, a), (top + 2, b), (top + 3, far_a)]
                line += [(low - 1, c), (low - 2, swap), (low - 3, far_c)]
            else:
                low, top = NORTH[0], NORTH[-1]
                line = [(low - 1, a), (low - 2, b), (low - 3, far_a)]
                line += [(top + 1, c), (top + 2, swap), (top + 3, far_c)]
            for d, rows in line:
                ex_a[EXTRA_AT[w, d % DIRS], slot] = whole_tile(w, d % DIRS, rows)
        return carry

    lax.fori_loop(0, tiles, fill, 0)

    if first_call:
        for i in range(2 * BLOCKS):
            out[0, SUMS_AT + i] = jnp.zeros((4, LANES), jnp.float32)
    else:
        for i in range(2 * BLOCKS):
            out[0, SUMS_AT + i] = given[0, SUMS_AT + i]
        for s in range(BLOCKS):
            for d in range(3):
                for i in range(origin):
                    out[s, d * WHOLE + i] = given[s, d * WHOLE + i]

    def keep(t, d, new):
        if isinstance(t, int):
            out[d // 3, 3 * WHOLE + d % 3] = new[0:4]
        else:
            out[d // 3, (d % 3) * WHOLE + origin + t] = new[0:4]

    def add_up(t, f, total):
        place = SUMS_AT + (me if isinstance(t, int) else t % BLOCKS)
        total = total[0:4]
        out[0, place] += total
        out[0, place + BLOCKS] += total * frsq[f]

    def make(step, src, src_ex, dst, dst_ex):
        def body(t, carry):
            slot, m, f = slot_of(t), map_of(t), f_of(t)
            rf = rfac[f]
            coefs = [coef[f, i] for i in range(COEF.shape[1])]
            seas = {"s": around[0, 0, m], "n": around[0, 1, m]}
            raw = {"s": around[1, 0, m], "n": around[1, 1, m]}
            mth = {w: jnp.abs(raw[w]) * rf for w in "sn"}
            ahead = {w: raw[w] > 0 for w in "sn"}
            loaded = {}

            def tile(w, d):
                d = d % DIRS
                key = (w, d)
                if window(d) == w or step == SUB - 1:
                    key = (window(d), d)
                if key not in loaded:
                    if key[0] == window(d):
                        loaded[key] = (src, d, src[d, slot])
                    else:
                        i = EXTRA_AT[key]
                        loaded[key] = (src_ex, i, src_ex[i, slot])
                return loaded[key]

            def update(w, d):
                ref, i, a = tile(w, d)
                before, after = tile(w, d - 1)[2], tile(w, d + 1)[2]
                if COS[d] >= 0:
                    x = pltpu.roll(jnp.where(end, ref[i, slot - 1], a), 1, 1)
                else:
                    x = pltpu.roll(jnp.where(start, ref[i, slot + 1], a), LANES - 1, 1)
                y = pltpu.roll(a, 1 if SIN[d] >= 0 else 7, 0)
                turned = mth[w] * (jnp.where(ahead[w], before, after) - a)
                stay = coefs[len(WEIGHTS) + K0[d]]
                return (a * stay + x * coefs[KX[d]] + y * coefs[KY[d]] + turned) * seas[w]

            fresh = {}
            total = None
            for d in range(DIRS):
                new = update(window(d), d)
                if step < SUB - 1:
                    fresh[d] = new
                    dst[d, slot] = new
                else:
                    keep(t, d, new)
                    total = new if total is None else total + new
            for i, (w, d, k) in enumerate(EXTRAS):
                if k < REACH - step:
                    dst_ex[i, slot] = jnp.where(mine, fresh[d], update(w, d))
            if total is not None:
                add_up(t, f, total)
            return carry

        return body

    bufs = [(st_a, ex_a), (st_b, ex_b)]
    for step in range(SUB):
        (src, src_ex), (dst, dst_ex) = bufs[step % 2], bufs[(step + 1) % 2]
        body = make(step, src, src_ex, dst, dst_ex)
        if step < SUB - 1:
            lax.fori_loop(0, tiles, body, 0, unroll=4)
        else:
            lax.fori_loop(0, whole, body, 0, unroll=4)
            if tail:
                body(whole + 1, 0)
    if not first_call:
        for i in range(2 * BLOCKS):
            value = out[0, SUMS_AT + i]
            for s in range(1, BLOCKS):
                out[s, SUMS_AT + i] = value


def step_call(chunk, first_call, group, own, south, north, rest):
    slots = slots_of(chunk)
    state = pltpu.VMEM((DIRS, slots, 8, LANES), jnp.float32)
    extra = pltpu.VMEM((len(EXTRAS), slots, 8, LANES), jnp.float32)
    out = [(BLOCKS, MADE, 4, LANES)]
    if first_call:
        out.append((2, 2, BLOCKS + 2, 8, LANES))
    args = (group, COEF, RFAC, FR * FR, own, south, north, *rest)
    return call(
        functools.partial(step_kernel, chunk, first_call),
        "steps",
        out,
        args,
        4,
        [state, state, extra, extra],
        20_000_000,
    )


def source_kernel(cos, sin, got, wind_u, wind_v, out):
    inverse = 1.0 / (DIRS * FREQS)
    for t in range(BLOCKS):
        cols = slice(t * LANES, (t + 1) * LANES)
        m0 = got[0, SUMS_AT + t]
        m2 = got[0, SUMS_AT + BLOCKS + t]
        for j in range(1, BLOCKS):
            m0 = m0 + got[j, SUMS_AT + t]
            m2 = m2 + got[j, SUMS_AT + BLOCKS + t]
        ratio = 0.5 * (m2 * inverse) / (1.0 + m0 * inverse)
        u, v = wind_u[:, cols], wind_v[:, cols]
        gain = [0.5 * jnp.maximum(u * cos[d] + v * sin[d], 0.0) for d in range(3)]
        for f in range(FREQS):
            fr = float(FR[f])
            shrink = 1.0 / (1.0 + ratio * (fr * fr))
            for d in range(3):
                if f < BLOCKS * FULL:
                    a = got[f // FULL, d * WHOLE + f % FULL * BLOCKS + t]
                else:
                    a = got[t, 3 * WHOLE + d]
                out[d, f, :, cols] = a * (1.0 + gain[d] * fr) * shrink


def on_device(spectrum, sea_mask, turning, wind_u, wind_v):
    me = lax.axis_index("spec")
    group = me.reshape(1)
    count = lax.axis_size("space")
    up = [(i, i + 1) for i in range(count - 1)]
    down = [(j, i) for i, j in up]

    maps = jnp.stack([(sea_mask == 1).astype(jnp.float32), turning])
    pack = pl.pallas_call(
        pack_kernel,
        out_shape=jax.ShapeDtypeStruct((BLOCKS, 3, TILES, 4, LANES), jnp.float32),
        in_specs=[pl.BlockSpec(memory_space=pltpu.HBM)],
        out_specs=vmem(),
        scratch_shapes=[pltpu.VMEM(spectrum.shape, jnp.float32), pltpu.SemaphoreType.DMA((3,))],
        compiler_params=pltpu.CompilerParams(vmem_limit_bytes=VMEM_LIMIT),
        interpret=INTERPRET,
        name="pack",
    )(spectrum)
    own = lax.all_to_all(pack, "spec", 0, 0, tiled=True).reshape(DIRS, TILES, 4, LANES)
    edges = []
    for i, chunk in enumerate(CHUNKS):
        tiles = tiles_of(chunk)
        size = PLANES * tiles + (2 * BLOCKS if i == 0 else 0)
        edges.append(
            call(
                functools.partial(halo_kernel, chunk[0] * BLOCKS, tiles, i == 0),
                "halo",
                [(size, 4, LANES)] * 2,
                (own, maps) if i == 0 else (own,),
                0,
            )
        )
    south, north = lax.ppermute(edges[0][0], "space", up), lax.ppermute(edges[0][1], "space", down)
    south, north, _ = lax.optimization_barrier((south, north, edges[1]))
    south_2, north_2 = lax.ppermute(edges[1][0], "space", up), lax.ppermute(edges[1][1], "space", down)
    made, around = step_call(CHUNKS[0], True, group, own, south, north, (maps,))
    (made,) = step_call(CHUNKS[1], False, group, own, south_2, north_2, (around, made))
    got = lax.all_to_all(made, "spec", 0, 0, tiled=True)
    cos = lax.dynamic_slice_in_dim(jnp.asarray(COS), me * 3, 3)
    sin = lax.dynamic_slice_in_dim(jnp.asarray(SIN), me * 3, 3)
    return call(
        source_kernel,
        "source",
        (3, FREQS, 4, BLOCKS * LANES),
        (cos, sin, got, wind_u, wind_v),
        2,
    )


def solution(mesh):
    rows = P("space", None)
    bins = P("spec", None, "space", None)
    return jax.shard_map(
        on_device,
        mesh=mesh,
        in_specs=(bins, rows, rows, rows, rows),
        out_specs=bins,
        check_vma=False,
    )
```

```python
import functools

import jax
import jax.numpy as jnp
import numpy as np
from jax import lax
from jax.experimental import pallas as pl
from jax.experimental.pallas import tpu as pltpu
from jax.sharding import PartitionSpec as P

DIRS = 24
FREQS = 25
SUB = 4
INTERPRET = False
LANES = 128
BLOCKS = 8

THETA = (np.float32(2.0 * np.pi) * np.arange(DIRS, dtype=np.float32) / np.float32(DIRS)).astype(
    np.float32
)
COS = np.cos(THETA).astype(np.float32)
SIN = np.sin(THETA).astype(np.float32)
FREQ = np.arange(FREQS, dtype=np.float64)
FR = (1.1 ** (FREQ - FREQS // 2)).astype(np.float32)
SPEED = (1.1 ** (-FREQ)).astype(np.float32)
RFAC = (np.float32(0.5) + np.float32(0.5) * SPEED).astype(np.float32)


def grouped(values):
    kept, place = [], []
    for v in values:
        near = [i for i, k in enumerate(kept) if abs(k - v) <= 4e-7 * abs(k)]
        if not near:
            kept.append(float(v))
        place.append(near[0] if near else len(kept) - 1)
    return kept, place


WEIGHTS, PLACE = grouped(np.abs(np.concatenate([COS, SIN])).astype(np.float64))
KX, KY = PLACE[:DIRS], PLACE[DIRS:]
REST, K0 = grouped([WEIGHTS[KX[d]] + WEIGHTS[KY[d]] for d in range(DIRS)])
COEF = np.concatenate(
    [
        0.42 * SPEED.astype(np.float64)[:, None] * np.array(WEIGHTS)[None, :],
        1.0 - 0.42 * SPEED.astype(np.float64)[:, None] * np.array(REST)[None, :],
    ],
    axis=1,
).astype(np.float32)

FULL = 3
CHUNKS = ((0, 2, False), (2, 1, True))
WHOLE = FULL * BLOCKS
TILES = WHOLE + 3
SUMS_AT = 3 * (WHOLE + 1)
MADE = SUMS_AT + 2 * BLOCKS

SOUTH = [d for d in range(DIRS) if SIN[d] >= 0]
NORTH = [d for d in range(DIRS) if SIN[d] < 0]
REACH = SUB - 1
PLANES = len(SOUTH) + REACH
EXTRAS = []
for k in range(1, REACH + 1):
    EXTRAS += [
        ("s", (SOUTH[-1] + k) % DIRS, k),
        ("s", (SOUTH[0] - k) % DIRS, k),
        ("n", (NORTH[-1] + k) % DIRS, k),
        ("n", (NORTH[0] - k) % DIRS, k),
    ]
EXTRA_AT = {(w, d): i for i, (w, d, _) in enumerate(EXTRAS)}
VMEM_LIMIT = 40 * 1024 * 1024


def window(d):
    return "s" if d in SOUTH else "n"


def tiles_of(chunk):
    return chunk[1] * BLOCKS + (3 if chunk[2] else 0)


def slots_of(chunk):
    return tiles_of(chunk) + chunk[1] + (2 if chunk[2] else 1)


def smem():
    return pl.BlockSpec(memory_space=pltpu.SMEM)


def vmem():
    return pl.BlockSpec(memory_space=pltpu.VMEM)


def call(kernel, name, out, args, n_smem, scratch=(), cost=4_000_000):
    return pl.pallas_call(
        kernel,
        out_shape=jax.tree.map(lambda s: jax.ShapeDtypeStruct(s, jnp.float32), out, is_leaf=lambda s: isinstance(s, tuple) and isinstance(s[0], int)),
        in_specs=[smem()] * n_smem + [vmem()] * (len(args) - n_smem),
        out_specs=jax.tree.map(lambda s: vmem(), out, is_leaf=lambda s: isinstance(s, tuple) and isinstance(s[0], int)),
        scratch_shapes=list(scratch),
        compiler_params=pltpu.CompilerParams(vmem_limit_bytes=VMEM_LIMIT),
        cost_estimate=pl.CostEstimate(flops=1000, bytes_accessed=cost, transcendentals=0),
        interpret=INTERPRET,
        name=name,
    )(*args)


def pack_kernel(spectrum, *refs):
    outs, (x, arrived) = refs[: len(CHUNKS)], refs[len(CHUNKS) :]
    copies = [pltpu.make_async_copy(spectrum.at[d], x.at[d], arrived.at[d]) for d in range(3)]
    for copy in copies:
        copy.start()
    zero = jnp.zeros((4, LANES), jnp.float32)
    for d in range(3):
        copies[d].wait()
        for (begin, count, tail), out in zip(CHUNKS, outs):
            for j in range(BLOCKS):
                for i in range(count):
                    for l in range(BLOCKS):
                        value = x[d, j * FULL + begin + i, :, l * LANES : (l + 1) * LANES]
                        out[j, d, i * BLOCKS + l] = value
                for i in range(3 if tail else 0):
                    l = j + i - 1
                    inside = 0 <= l < BLOCKS
                    value = x[d, FREQS - 1, :, l * LANES : (l + 1) * LANES] if inside else zero
                    out[j, d, count * BLOCKS + i] = value


def halo_kernel(tiles, with_maps, *refs):
    if with_maps:
        own, maps, up, down = refs
        for k in range(2):
            for l in range(BLOCKS):
                value = maps[k, :, l * LANES : (l + 1) * LANES]
                up[PLANES * tiles + k * BLOCKS + l] = value
                down[PLANES * tiles + k * BLOCKS + l] = value
    else:
        own, up, down = refs
    ends = {
        "s": (SOUTH[-1], SOUTH[0]),
        "n": (NORTH[0], NORTH[-1]),
    }
    n = len(SOUTH)

    def body(t, carry):
        for i, d in enumerate(SOUTH):
            up[i * tiles + t] = own[d, t]
        for i, d in enumerate(NORTH):
            down[i * tiles + t] = own[d, t]
        top, low = ends["s"]
        a = [own[(top + k) % DIRS, t] for k in range(1, 4)]
        b = [own[(low - k) % DIRS, t] for k in range(1, 4)]
        up[n * tiles + t] = jnp.concatenate([a[2][3:4], a[0][1:4]], axis=0)
        up[(n + 1) * tiles + t] = jnp.concatenate([b[1][2:4], a[1][2:4]], axis=0)
        up[(n + 2) * tiles + t] = jnp.concatenate([b[2][3:4], b[0][1:4]], axis=0)
        low, top = ends["n"]
        a = [own[(low - k) % DIRS, t] for k in range(1, 4)]
        b = [own[(top + k) % DIRS, t] for k in range(1, 4)]
        down[n * tiles + t] = jnp.concatenate([a[0][0:3], a[2][0:1]], axis=0)
        down[(n + 1) * tiles + t] = jnp.concatenate([a[1][0:2], b[1][0:2]], axis=0)
        down[(n + 2) * tiles + t] = jnp.concatenate([b[0][0:3], b[2][0:1]], axis=0)
        return carry

    lax.fori_loop(0, tiles, body, 0, unroll=4)


def step_kernel(chunk, first_call, group, coef, rfac, frsq, own, south, north, *refs):
    begin, count, tail = chunk
    tiles, slots, origin = tiles_of(chunk), slots_of(chunk), begin * BLOCKS
    if first_call:
        maps, out, around, st_a, st_b, ex_a, ex_b = refs
    else:
        around, given, out, st_a, st_b, ex_a, ex_b = refs
    me = group[0]
    whole = count * BLOCKS

    def f_of(t):
        if isinstance(t, int):
            return FREQS - 1
        f = me * FULL + begin + t // BLOCKS
        return jnp.where(t < whole, f, FREQS - 1) if tail else f

    def map_of(t):
        if isinstance(t, int):
            return me + t - whole
        l = t % BLOCKS + 1
        return jnp.where(t < whole, l, me + t - whole) if tail else l

    def slot_of(t):
        return t + t // BLOCKS + 1

    lane = lax.broadcasted_iota(jnp.int32, (8, LANES), 1)
    row = lax.broadcasted_iota(jnp.int32, (8, LANES), 0)
    start, end, mine = lane == 0, lane == LANES - 1, row < 4
    zero = jnp.zeros((8, LANES), jnp.float32)
    for p in [i * (BLOCKS + 1) for i in range(count + 1)] + ([slots - 1] if tail else []):
        for d in range(DIRS):
            st_a[d, p] = zero
            st_b[d, p] = zero
        for i in range(len(EXTRAS)):
            ex_a[i, p] = zero
            ex_b[i, p] = zero

    if first_call:
        at = PLANES * tiles
        for k in range(2):
            for w, ref in enumerate((south, north)):
                around[k, w, 0] = zero
                around[k, w, BLOCKS + 1] = zero
                for l in range(BLOCKS):
                    mid = maps[k, :, l * LANES : (l + 1) * LANES]
                    around[k, w, l + 1] = jnp.concatenate([mid, ref[at + k * BLOCKS + l]], axis=0)

    def fill(t, carry):
        slot, m = slot_of(t), map_of(t)
        seas = {"s": around[0, 0, m], "n": around[0, 1, m]}
        n = len(SOUTH)

        def whole_tile(w, d, rows):
            return jnp.concatenate([own[d, t], rows], axis=0) * seas[w]

        for i, d in enumerate(SOUTH):
            st_a[d, slot] = whole_tile("s", d, south[i * tiles + t])
        for i, d in enumerate(NORTH):
            st_a[d, slot] = whole_tile("n", d, north[i * tiles + t])
        for w, ref in (("s", south), ("n", north)):
            a, b, c = (ref[(n + i) * tiles + t] for i in range(3))
            swap = jnp.concatenate([b[2:4], b[0:2]], axis=0)
            pick = slice(0, 1) if w == "s" else slice(3, 4)
            far_a = jnp.broadcast_to(a[pick], (4, LANES))
            far_c = jnp.broadcast_to(c[pick], (4, LANES))
            if w == "s":
                top, low = SOUTH[-1], SOUTH[0]
                line = [(top + 1, a), (top + 2, b), (top + 3, far_a)]
                line += [(low - 1, c), (low - 2, swap), (low - 3, far_c)]
            else:
                low, top = NORTH[0], NORTH[-1]
                line = [(low - 1, a), (low - 2, b), (low - 3, far_a)]
                line += [(top + 1, c), (top + 2, swap), (top + 3, far_c)]
            for d, rows in line:
                ex_a[EXTRA_AT[w, d % DIRS], slot] = whole_tile(w, d % DIRS, rows)
        return carry

    lax.fori_loop(0, tiles, fill, 0)

    if first_call:
        for i in range(2 * BLOCKS):
            out[0, SUMS_AT + i] = jnp.zeros((4, LANES), jnp.float32)
    else:
        for i in range(2 * BLOCKS):
            out[0, SUMS_AT + i] = given[0, SUMS_AT + i]
        for s in range(BLOCKS):
            for d in range(3):
                for i in range(origin):
                    out[s, d * WHOLE + i] = given[s, d * WHOLE + i]

    def keep(t, d, new):
        if isinstance(t, int):
            out[d // 3, 3 * WHOLE + d % 3] = new[0:4]
        else:
            out[d // 3, (d % 3) * WHOLE + origin + t] = new[0:4]

    def add_up(t, f, total):
        place = SUMS_AT + (me if isinstance(t, int) else t % BLOCKS)
        total = total[0:4]
        out[0, place] += total
        out[0, place + BLOCKS] += total * frsq[f]

    def make(step, src, src_ex, dst, dst_ex):
        def body(t, carry):
            slot, m, f = slot_of(t), map_of(t), f_of(t)
            rf = rfac[f]
            coefs = [coef[f, i] for i in range(COEF.shape[1])]
            seas = {"s": around[0, 0, m], "n": around[0, 1, m]}
            raw = {"s": around[1, 0, m], "n": around[1, 1, m]}
            mth = {w: jnp.abs(raw[w]) * rf for w in "sn"}
            ahead = {w: raw[w] > 0 for w in "sn"}
            loaded = {}

            def tile(w, d):
                d = d % DIRS
                key = (w, d)
                if window(d) == w or step == SUB - 1:
                    key = (window(d), d)
                if key not in loaded:
                    if key[0] == window(d):
                        loaded[key] = (src, d, src[d, slot])
                    else:
                        i = EXTRA_AT[key]
                        loaded[key] = (src_ex, i, src_ex[i, slot])
                return loaded[key]

            def update(w, d):
                ref, i, a = tile(w, d)
                before, after = tile(w, d - 1)[2], tile(w, d + 1)[2]
                if COS[d] >= 0:
                    x = pltpu.roll(jnp.where(end, ref[i, slot - 1], a), 1, 1)
                else:
                    x = pltpu.roll(jnp.where(start, ref[i, slot + 1], a), LANES - 1, 1)
                y = pltpu.roll(a, 1 if SIN[d] >= 0 else 7, 0)
                turned = mth[w] * (jnp.where(ahead[w], before, after) - a)
                stay = coefs[len(WEIGHTS) + K0[d]]
                return (a * stay + x * coefs[KX[d]] + y * coefs[KY[d]] + turned) * seas[w]

            fresh = {}
            total = None
            for d in range(DIRS):
                new = update(window(d), d)
                if step < SUB - 1:
                    fresh[d] = new
                    dst[d, slot] = new
                else:
                    keep(t, d, new)
                    total = new if total is None else total + new
            for i, (w, d, k) in enumerate(EXTRAS):
                if k < REACH - step:
                    dst_ex[i, slot] = jnp.where(mine, fresh[d], update(w, d))
            if total is not None:
                add_up(t, f, total)
            return carry

        return body

    bufs = [(st_a, ex_a), (st_b, ex_b)]
    for step in range(SUB):
        (src, src_ex), (dst, dst_ex) = bufs[step % 2], bufs[(step + 1) % 2]
        body = make(step, src, src_ex, dst, dst_ex)
        if step < SUB - 1:
            lax.fori_loop(0, tiles, body, 0, unroll=4)
        else:
            lax.fori_loop(0, whole, body, 0, unroll=4)
            if tail:
                body(whole + 1, 0)
    if not first_call:
        for i in range(2 * BLOCKS):
            value = out[0, SUMS_AT + i]
            for s in range(1, BLOCKS):
                out[s, SUMS_AT + i] = value


def step_call(chunk, first_call, group, own, south, north, rest):
    slots = slots_of(chunk)
    state = pltpu.VMEM((DIRS, slots, 8, LANES), jnp.float32)
    extra = pltpu.VMEM((len(EXTRAS), slots, 8, LANES), jnp.float32)
    out = [(BLOCKS, MADE, 4, LANES)]
    if first_call:
        out.append((2, 2, BLOCKS + 2, 8, LANES))
    args = (group, COEF, RFAC, FR * FR, own, south, north, *rest)
    return call(
        functools.partial(step_kernel, chunk, first_call),
        "steps",
        out,
        args,
        4,
        [state, state, extra, extra],
        20_000_000,
    )


def source_kernel(cos, sin, got, wind_u, wind_v, out):
    inverse = 1.0 / (DIRS * FREQS)
    for t in range(BLOCKS):
        cols = slice(t * LANES, (t + 1) * LANES)
        m0 = got[0, SUMS_AT + t]
        m2 = got[0, SUMS_AT + BLOCKS + t]
        for j in range(1, BLOCKS):
            m0 = m0 + got[j, SUMS_AT + t]
            m2 = m2 + got[j, SUMS_AT + BLOCKS + t]
        ratio = 0.5 * (m2 * inverse) / (1.0 + m0 * inverse)
        u, v = wind_u[:, cols], wind_v[:, cols]
        gain = [0.5 * jnp.maximum(u * cos[d] + v * sin[d], 0.0) for d in range(3)]
        for f in range(FREQS):
            fr = float(FR[f])
            shrink = 1.0 / (1.0 + ratio * (fr * fr))
            for d in range(3):
                if f < BLOCKS * FULL:
                    a = got[f // FULL, d * WHOLE + f % FULL * BLOCKS + t]
                else:
                    a = got[t, 3 * WHOLE + d]
                out[d, f, :, cols] = a * (1.0 + gain[d] * fr) * shrink


def on_device(spectrum, sea_mask, turning, wind_u, wind_v):
    me = lax.axis_index("spec")
    group = me.reshape(1)
    count = lax.axis_size("space")
    up = [(i, i + 1) for i in range(count - 1)]
    down = [(j, i) for i, j in up]

    maps = jnp.stack([(sea_mask == 1).astype(jnp.float32), turning])
    packs = pl.pallas_call(
        pack_kernel,
        out_shape=[
            jax.ShapeDtypeStruct((BLOCKS, 3, tiles_of(c), 4, LANES), jnp.float32) for c in CHUNKS
        ],
        in_specs=[pl.BlockSpec(memory_space=pltpu.HBM)],
        out_specs=[vmem() for _ in CHUNKS],
        scratch_shapes=[pltpu.VMEM(spectrum.shape, jnp.float32), pltpu.SemaphoreType.DMA((3,))],
        compiler_params=pltpu.CompilerParams(vmem_limit_bytes=60 * 1024 * 1024),
        interpret=INTERPRET,
        name="pack",
    )(spectrum)

    def gather(i, pack):
        tiles = tiles_of(CHUNKS[i])
        own = lax.all_to_all(pack, "spec", 0, 0, tiled=True).reshape(DIRS, tiles, 4, LANES)
        size = PLANES * tiles + (2 * BLOCKS if i == 0 else 0)
        return own, call(
            functools.partial(halo_kernel, tiles, i == 0),
            "halo",
            [(size, 4, LANES)] * 2,
            (own, maps) if i == 0 else (own,),
            0,
        )

    own, (low, high) = gather(0, packs[0])
    pack, low, high = lax.optimization_barrier((packs[1], low, high))
    own_2, (low_2, high_2) = gather(1, pack)
    south, north = lax.ppermute(low, "space", up), lax.ppermute(high, "space", down)
    south, north, _, _ = lax.optimization_barrier((south, north, low_2, high_2))
    south_2, north_2 = lax.ppermute(low_2, "space", up), lax.ppermute(high_2, "space", down)
    made, around = step_call(CHUNKS[0], True, group, own, south, north, (maps,))
    (made,) = step_call(CHUNKS[1], False, group, own_2, south_2, north_2, (around, made))
    got = lax.all_to_all(made, "spec", 0, 0, tiled=True)
    cos = lax.dynamic_slice_in_dim(jnp.asarray(COS), me * 3, 3)
    sin = lax.dynamic_slice_in_dim(jnp.asarray(SIN), me * 3, 3)
    return call(
        source_kernel,
        "source",
        (3, FREQS, 4, BLOCKS * LANES),
        (cos, sin, got, wind_u, wind_v),
        2,
    )


def solution(mesh):
    rows = P("space", None)
    bins = P("spec", None, "space", None)
    return jax.shard_map(
        on_device,
        mesh=mesh,
        in_specs=(bins, rows, rows, rows, rows),
        out_specs=bins,
        check_vma=False,
    )
```

```python
import functools

import jax
import jax.numpy as jnp
import numpy as np
from jax import lax
from jax.experimental import pallas as pl
from jax.experimental.pallas import tpu as pltpu
from jax.sharding import PartitionSpec as P

DIRS = 24
FREQS = 25
SUB = 4
INTERPRET = False
UNROLL = True
LANES = 128
BLOCKS = 8

THETA = (np.float32(2.0 * np.pi) * np.arange(DIRS, dtype=np.float32) / np.float32(DIRS)).astype(
    np.float32
)
COS = np.cos(THETA).astype(np.float32)
SIN = np.sin(THETA).astype(np.float32)
FREQ = np.arange(FREQS, dtype=np.float64)
FR = (1.1 ** (FREQ - FREQS // 2)).astype(np.float32)
SPEED = (1.1 ** (-FREQ)).astype(np.float32)
RFAC = (np.float32(0.5) + np.float32(0.5) * SPEED).astype(np.float32)


def grouped(values):
    kept, place = [], []
    for v in values:
        near = [i for i, k in enumerate(kept) if abs(k - v) <= 4e-7 * abs(k)]
        if not near:
            kept.append(float(v))
        place.append(near[0] if near else len(kept) - 1)
    return kept, place


WEIGHTS, PLACE = grouped(np.abs(np.concatenate([COS, SIN])).astype(np.float64))
KX, KY = PLACE[:DIRS], PLACE[DIRS:]
REST, K0 = grouped([WEIGHTS[KX[d]] + WEIGHTS[KY[d]] for d in range(DIRS)])
COEF = np.concatenate(
    [
        0.42 * SPEED.astype(np.float64)[:, None] * np.array(WEIGHTS)[None, :],
        1.0 - 0.42 * SPEED.astype(np.float64)[:, None] * np.array(REST)[None, :],
    ],
    axis=1,
).astype(np.float32)

FULL = 3
CHUNKS = ((0, 2, False), (2, 1, True))
WHOLE = FULL * BLOCKS
WINDOW = 2
HALF = LANES // 2
SUMS_AT = 3 * (WHOLE + 1)
MADE = SUMS_AT + 2 * BLOCKS

SOUTH = [d for d in range(DIRS) if SIN[d] >= 0]
NORTH = [d for d in range(DIRS) if SIN[d] < 0]
REACH = SUB - 1
PLANES = len(SOUTH) + REACH
EXTRAS = []
for k in range(1, REACH + 1):
    EXTRAS += [
        ("s", (SOUTH[-1] + k) % DIRS, k),
        ("s", (SOUTH[0] - k) % DIRS, k),
        ("n", (NORTH[-1] + k) % DIRS, k),
        ("n", (NORTH[0] - k) % DIRS, k),
    ]
EXTRA_AT = {(w, d): i for i, (w, d, _) in enumerate(EXTRAS)}
VMEM_LIMIT = 40 * 1024 * 1024


def window(d):
    return "s" if d in SOUTH else "n"


def tiles_of(chunk):
    return chunk[1] * BLOCKS + (WINDOW if chunk[2] else 0)


def slots_of(chunk):
    return tiles_of(chunk) + chunk[1] + (2 if chunk[2] else 1)


def smem():
    return pl.BlockSpec(memory_space=pltpu.SMEM)


def vmem():
    return pl.BlockSpec(memory_space=pltpu.VMEM)


def call(kernel, name, out, args, n_smem, scratch=(), cost=4_000_000):
    return pl.pallas_call(
        kernel,
        out_shape=jax.tree.map(lambda s: jax.ShapeDtypeStruct(s, jnp.float32), out, is_leaf=lambda s: isinstance(s, tuple) and isinstance(s[0], int)),
        in_specs=[smem()] * n_smem + [vmem()] * (len(args) - n_smem),
        out_specs=jax.tree.map(lambda s: vmem(), out, is_leaf=lambda s: isinstance(s, tuple) and isinstance(s[0], int)),
        scratch_shapes=list(scratch),
        compiler_params=pltpu.CompilerParams(vmem_limit_bytes=VMEM_LIMIT),
        cost_estimate=pl.CostEstimate(flops=1000, bytes_accessed=cost, transcendentals=0),
        interpret=INTERPRET,
        name=name,
    )(*args)


def first_pack_kernel(spectrum, out, done):
    begin, count, _ = CHUNKS[0]
    copies = [
        pltpu.make_async_copy(
            spectrum.at[d, pl.ds(j * FULL + begin, count)], out.at[j, d], done.at[j, d]
        )
        for d in range(3)
        for j in range(BLOCKS)
    ]
    for copy in copies:
        copy.start()
    for copy in copies:
        copy.wait()


def last_pack_kernel(spectrum, out, x, arrived):
    begin, count, _ = CHUNKS[1]
    copies = [pltpu.make_async_copy(spectrum.at[d], x.at[d], arrived.at[d]) for d in range(3)]
    for copy in copies:
        copy.start()
    zero = jnp.zeros((4, HALF), jnp.float32)
    for d in range(3):
        copies[d].wait()
        for j in range(BLOCKS):
            for i in range(count):
                for l in range(BLOCKS):
                    value = x[d, j * FULL + begin + i, :, l * LANES : (l + 1) * LANES]
                    out[j, d, i * BLOCKS + l] = value
            left, right = j * LANES - HALF, (j + 1) * LANES + HALF
            value = x[d, FREQS - 1, :, max(left, 0) : min(right, BLOCKS * LANES)]
            if left < 0:
                value = jnp.concatenate([zero, value], axis=1)
            if right > BLOCKS * LANES:
                value = jnp.concatenate([value, zero], axis=1)
            for i in range(WINDOW):
                out[j, d, count * BLOCKS + i] = value[:, i * LANES : (i + 1) * LANES]


def halo_kernel(tiles, with_maps, *refs):
    if with_maps:
        own, maps, up, down, done = refs
    else:
        own, up, down, done = refs
    n = len(SOUTH)
    copies = [
        pltpu.make_async_copy(own.at[pl.ds(dirs[0], n)], ref.at[pl.ds(0, n)], done.at[i])
        for i, (dirs, ref) in enumerate(((SOUTH, up), (NORTH, down)))
    ]
    for copy in copies:
        copy.start()
    if with_maps:
        for k in range(2):
            for l in range(BLOCKS):
                value = maps[k, :, l * LANES : (l + 1) * LANES]
                up[PLANES, k * BLOCKS + l] = value
                down[PLANES, k * BLOCKS + l] = value
    ends = {
        "s": (SOUTH[-1], SOUTH[0]),
        "n": (NORTH[0], NORTH[-1]),
    }

    def body(t, carry):
        top, low = ends["s"]
        a = [own[(top + k) % DIRS, t] for k in range(1, 4)]
        b = [own[(low - k) % DIRS, t] for k in range(1, 4)]
        up[n, t] = jnp.concatenate([a[2][3:4], a[0][1:4]], axis=0)
        up[n + 1, t] = jnp.concatenate([b[1][2:4], a[1][2:4]], axis=0)
        up[n + 2, t] = jnp.concatenate([b[2][3:4], b[0][1:4]], axis=0)
        low, top = ends["n"]
        a = [own[(low - k) % DIRS, t] for k in range(1, 4)]
        b = [own[(top + k) % DIRS, t] for k in range(1, 4)]
        down[n, t] = jnp.concatenate([a[0][0:3], a[2][0:1]], axis=0)
        down[n + 1, t] = jnp.concatenate([a[1][0:2], b[1][0:2]], axis=0)
        down[n + 2, t] = jnp.concatenate([b[0][0:3], b[2][0:1]], axis=0)
        return carry

    lax.fori_loop(0, tiles, body, 0, unroll=2)
    for copy in copies:
        copy.wait()


def step_kernel(chunk, first_call, group, coef, rfac, frsq, own, south, north, *refs):
    begin, count, tail = chunk
    tiles, slots, origin = tiles_of(chunk), slots_of(chunk), begin * BLOCKS
    if first_call:
        maps, out, around, st_a, st_b, ex_a, ex_b = refs
    else:
        around, given, out, st_a, st_b, ex_a, ex_b = refs
    me = group[0]
    whole = count * BLOCKS

    def f_of(t):
        if isinstance(t, int):
            return FREQS - 1
        f = me * FULL + begin + t // BLOCKS
        return jnp.where(t < whole, f, FREQS - 1) if tail else f

    def map_of(t):
        if isinstance(t, int):
            return BLOCKS + 2 + t - whole
        l = t % BLOCKS + 1
        return jnp.where(t < whole, l, BLOCKS + 2 + t - whole) if tail else l

    def slot_of(t):
        return t + t // BLOCKS + 1

    lane = lax.broadcasted_iota(jnp.int32, (8, LANES), 1)
    row = lax.broadcasted_iota(jnp.int32, (8, LANES), 0)
    start, end, mine, half = lane == 0, lane == LANES - 1, row < 4, lane < HALF
    zero = jnp.zeros((8, LANES), jnp.float32)
    for p in [i * (BLOCKS + 1) for i in range(count + 1)] + ([slots - 1] if tail else []):
        for d in range(DIRS):
            st_a[d, p] = zero
            st_b[d, p] = zero
        for i in range(len(EXTRAS)):
            ex_a[i, p] = zero
            ex_b[i, p] = zero

    if first_call:
        for k in range(2):
            for w, ref in enumerate((south, north)):
                around[k, w, 0] = zero
                around[k, w, BLOCKS + 1] = zero
                for l in range(BLOCKS):
                    mid = maps[k, :, l * LANES : (l + 1) * LANES]
                    around[k, w, l + 1] = jnp.concatenate([mid, ref[PLANES, k * BLOCKS + l]], axis=0)
                for i in range(WINDOW):
                    left, right = around[k, w, me + i], around[k, w, me + i + 1]
                    around[k, w, BLOCKS + 2 + i] = pltpu.roll(jnp.where(half, right, left), HALF, 1)

    def fill(t, carry):
        slot, m = slot_of(t), map_of(t)
        seas = {"s": around[0, 0, m], "n": around[0, 1, m]}
        n = len(SOUTH)

        def whole_tile(w, d, rows):
            return jnp.concatenate([own[d, t], rows], axis=0) * seas[w]

        for i, d in enumerate(SOUTH):
            st_a[d, slot] = whole_tile("s", d, south[i, t])
        for i, d in enumerate(NORTH):
            st_a[d, slot] = whole_tile("n", d, north[i, t])
        for w, ref in (("s", south), ("n", north)):
            a, b, c = (ref[n + i, t] for i in range(3))
            swap = jnp.concatenate([b[2:4], b[0:2]], axis=0)
            pick = slice(0, 1) if w == "s" else slice(3, 4)
            far_a = jnp.broadcast_to(a[pick], (4, LANES))
            far_c = jnp.broadcast_to(c[pick], (4, LANES))
            if w == "s":
                top, low = SOUTH[-1], SOUTH[0]
                line = [(top + 1, a), (top + 2, b), (top + 3, far_a)]
                line += [(low - 1, c), (low - 2, swap), (low - 3, far_c)]
            else:
                low, top = NORTH[0], NORTH[-1]
                line = [(low - 1, a), (low - 2, b), (low - 3, far_a)]
                line += [(top + 1, c), (top + 2, swap), (top + 3, far_c)]
            for d, rows in line:
                ex_a[EXTRA_AT[w, d % DIRS], slot] = whole_tile(w, d % DIRS, rows)
        return carry

    lax.fori_loop(0, tiles, fill, 0)

    if first_call:
        for i in range(2 * BLOCKS):
            out[0, SUMS_AT + i] = jnp.zeros((4, LANES), jnp.float32)
    else:
        for i in range(2 * BLOCKS):
            out[0, SUMS_AT + i] = given[0, SUMS_AT + i]
        for s in range(BLOCKS):
            for d in range(3):
                for i in range(origin):
                    out[s, d * WHOLE + i] = given[s, d * WHOLE + i]

    def keep(t, d, new):
        out[d // 3, (d % 3) * WHOLE + origin + t] = new[0:4]

    def add_up(t, f, total):
        place = SUMS_AT + (me if isinstance(t, int) else t % BLOCKS)
        total = total[0:4]
        out[0, place] += total
        out[0, place + BLOCKS] += total * frsq[f]

    def make(step, src, src_ex, dst, dst_ex):
        def body(t, carry):
            slot, m, f = slot_of(t), map_of(t), f_of(t)
            rf = rfac[f]
            coefs = [coef[f, i] for i in range(COEF.shape[1])]
            seas = {"s": around[0, 0, m], "n": around[0, 1, m]}
            raw = {"s": around[1, 0, m], "n": around[1, 1, m]}
            mth = {w: jnp.abs(raw[w]) * rf for w in "sn"}
            ahead = {w: raw[w] > 0 for w in "sn"}
            loaded = {}

            def tile(w, d):
                d = d % DIRS
                key = (w, d)
                if window(d) == w or step == SUB - 1:
                    key = (window(d), d)
                if key not in loaded:
                    if key[0] == window(d):
                        loaded[key] = (src, d, src[d, slot])
                    else:
                        i = EXTRA_AT[key]
                        loaded[key] = (src_ex, i, src_ex[i, slot])
                return loaded[key]

            def update(w, d):
                ref, i, a = tile(w, d)
                before, after = tile(w, d - 1)[2], tile(w, d + 1)[2]
                if COS[d] >= 0:
                    x = pltpu.roll(jnp.where(end, ref[i, slot - 1], a), 1, 1)
                else:
                    x = pltpu.roll(jnp.where(start, ref[i, slot + 1], a), LANES - 1, 1)
                y = pltpu.roll(a, 1 if SIN[d] >= 0 else 7, 0)
                turned = mth[w] * (jnp.where(ahead[w], before, after) - a)
                stay = coefs[len(WEIGHTS) + K0[d]]
                return (a * stay + x * coefs[KX[d]] + y * coefs[KY[d]] + turned) * seas[w]

            fresh = {}
            total = None
            for d in range(DIRS):
                new = update(window(d), d)
                if step < SUB - 1 or isinstance(t, int):
                    fresh[d] = new
                    dst[d, slot] = new
                else:
                    keep(t, d, new)
                    total = new if total is None else total + new
            for i, (w, d, k) in enumerate(EXTRAS):
                if k < REACH - step:
                    dst_ex[i, slot] = jnp.where(mine, fresh[d], update(w, d))
            if total is not None:
                add_up(t, f, total)
            return carry

        return body

    bufs = [(st_a, ex_a), (st_b, ex_b)]
    for step in range(SUB):
        (src, src_ex), (dst, dst_ex) = bufs[step % 2], bufs[(step + 1) % 2]
        body = make(step, src, src_ex, dst, dst_ex)
        if step < SUB - 1:
            lax.fori_loop(0, tiles, body, 0, unroll=(tiles if tail else BLOCKS) if UNROLL else 1)
        else:
            lax.fori_loop(0, whole, body, 0, unroll=BLOCKS if UNROLL else 1)
    if tail:
        for t in range(whole, tiles):
            body(t, 0)
        total = None
        for d in range(DIRS):
            left, right = dst[d, slot_of(whole)], dst[d, slot_of(whole + 1)]
            new = pltpu.roll(jnp.where(half, right, left), HALF, 1)
            out[d // 3, 3 * WHOLE + d % 3] = new[0:4]
            total = new if total is None else total + new
        add_up(whole, FREQS - 1, total)
    if not first_call:
        for i in range(2 * BLOCKS):
            value = out[0, SUMS_AT + i]
            for s in range(1, BLOCKS):
                out[s, SUMS_AT + i] = value


def step_call(chunk, first_call, group, own, south, north, rest):
    slots = slots_of(chunk)
    state = pltpu.VMEM((DIRS, slots, 8, LANES), jnp.float32)
    extra = pltpu.VMEM((len(EXTRAS), slots, 8, LANES), jnp.float32)
    out = [(BLOCKS, MADE, 4, LANES)]
    if first_call:
        out.append((2, 2, BLOCKS + 2 + WINDOW, 8, LANES))
    args = (group, COEF, RFAC, FR * FR, own, south, north, *rest)
    return call(
        functools.partial(step_kernel, chunk, first_call),
        "steps",
        out,
        args,
        4,
        [state, state, extra, extra],
        20_000_000,
    )


def source_kernel(cos, sin, got, wind_u, wind_v, out, made, shrink, done):
    inverse = 1.0 / (DIRS * FREQS)
    columns = [slice(t * LANES, (t + 1) * LANES) for t in range(BLOCKS)]
    for t, cols in enumerate(columns):
        m0 = got[0, SUMS_AT + t]
        m2 = got[0, SUMS_AT + BLOCKS + t]
        for j in range(1, BLOCKS):
            m0 = m0 + got[j, SUMS_AT + t]
            m2 = m2 + got[j, SUMS_AT + BLOCKS + t]
        ratio = 0.5 * (m2 * inverse) / (1.0 + m0 * inverse)
        for f in range(FREQS):
            shrink[f, :, cols] = 1.0 / (1.0 + ratio * float(FR[f] * FR[f]))
    copies = []
    for d in range(3):
        for t, cols in enumerate(columns):
            along = wind_u[:, cols] * cos[d] + wind_v[:, cols] * sin[d]
            gain = 0.5 * jnp.maximum(along, 0.0)
            for f in range(FREQS):
                if f < BLOCKS * FULL:
                    a = got[f // FULL, d * WHOLE + f % FULL * BLOCKS + t]
                else:
                    a = got[t, 3 * WHOLE + d]
                made[d, f, :, cols] = a * (1.0 + gain * float(FR[f])) * shrink[f, :, cols]
        copies.append(pltpu.make_async_copy(made.at[d], out.at[d], done.at[d]))
        copies[-1].start()
    for copy in copies:
        copy.wait()


def moving(kernel, name, out, ins, out_space, args, scratch):
    return pl.pallas_call(
        kernel,
        out_shape=[jax.ShapeDtypeStruct(s, jnp.float32) for s in out],
        in_specs=ins,
        out_specs=[out_space for _ in out],
        scratch_shapes=scratch,
        compiler_params=pltpu.CompilerParams(vmem_limit_bytes=60 * 1024 * 1024 if "pack" in name else VMEM_LIMIT),
        interpret=INTERPRET,
        name=name,
    )(*args)


def tiled(rows):
    return jnp.swapaxes(rows.reshape(rows.shape[:-1] + (BLOCKS, LANES)), -2, -3)


def on_device(spectrum, sea_mask, turning, wind_u, wind_v):
    me = lax.axis_index("spec")
    group = me.reshape(1)
    count = lax.axis_size("space")
    up = [(i, i + 1) for i in range(count - 1)]
    down = [(j, i) for i, j in up]

    maps = jnp.stack([(sea_mask == 1).astype(jnp.float32), turning])
    hbm = pl.BlockSpec(memory_space=pltpu.HBM)
    room = pltpu.VMEM(spectrum.shape, jnp.float32)
    first, last = CHUNKS
    (pack,) = moving(
        first_pack_kernel,
        "first_pack",
        [(BLOCKS, 3, first[1]) + spectrum.shape[2:]],
        [hbm],
        hbm,
        (spectrum,),
        [pltpu.SemaphoreType.DMA((BLOCKS, 3))],
    )
    (pack_2,) = moving(
        last_pack_kernel,
        "last_pack",
        [(BLOCKS, 3, tiles_of(last), 4, LANES)],
        [hbm],
        vmem(),
        (spectrum,),
        [room, pltpu.SemaphoreType.DMA((3,))],
    )

    def edges(tiles, planes, *args):
        return moving(
            functools.partial(halo_kernel, tiles, len(args) > 1),
            "halo",
            [(planes, tiles, 4, LANES)] * 2,
            [vmem() for _ in args],
            vmem(),
            args,
            [pltpu.SemaphoreType.DMA((2,))],
        )

    own = lax.all_to_all(pack, "spec", 0, 0, tiled=True)
    own = tiled(own).reshape(DIRS, tiles_of(first), 4, LANES)
    low, high = edges(tiles_of(first), PLANES + 1, own, maps)
    pack_2, low, high = lax.optimization_barrier((pack_2, low, high))
    own_2 = lax.all_to_all(pack_2, "spec", 0, 0, tiled=True)
    own_2 = own_2.reshape(DIRS, tiles_of(last), 4, LANES)
    low_2, high_2 = edges(tiles_of(last), PLANES, own_2)
    south, north = lax.ppermute(low, "space", up), lax.ppermute(high, "space", down)
    south, north, _, _ = lax.optimization_barrier((south, north, low_2, high_2))
    south_2, north_2 = lax.ppermute(low_2, "space", up), lax.ppermute(high_2, "space", down)
    made, around = step_call(CHUNKS[0], True, group, own, south, north, (maps,))
    (made,) = step_call(CHUNKS[1], False, group, own_2, south_2, north_2, (around, made))
    got = lax.all_to_all(made, "spec", 0, 0, tiled=True)
    cos = lax.dynamic_slice_in_dim(jnp.asarray(COS), me * 3, 3)
    sin = lax.dynamic_slice_in_dim(jnp.asarray(SIN), me * 3, 3)
    (result,) = moving(
        source_kernel,
        "source",
        [spectrum.shape],
        [smem(), smem(), vmem(), vmem(), vmem()],
        hbm,
        (cos, sin, got, wind_u, wind_v),
        [room, pltpu.VMEM(spectrum.shape[1:], jnp.float32), pltpu.SemaphoreType.DMA((3,))],
    )
    return result


def solution(mesh):
    rows = P("space", None)
    bins = P("spec", None, "space", None)
    return jax.shard_map(
        on_device,
        mesh=mesh,
        in_specs=(bins, rows, rows, rows, rows),
        out_specs=bins,
        check_vma=False,
    )
```

```python
import functools

import jax
import jax.numpy as jnp
import numpy as np
from jax import lax
from jax.experimental import pallas as pl
from jax.experimental.pallas import tpu as pltpu
from jax.sharding import PartitionSpec as P

DIRS = 24
FREQS = 25
SUB = 4
INTERPRET = False
UNROLL = True
LANES = 128
BLOCKS = 8

THETA = (np.float32(2.0 * np.pi) * np.arange(DIRS, dtype=np.float32) / np.float32(DIRS)).astype(
    np.float32
)
COS = np.cos(THETA).astype(np.float32)
SIN = np.sin(THETA).astype(np.float32)
FREQ = np.arange(FREQS, dtype=np.float64)
FR = (1.1 ** (FREQ - FREQS // 2)).astype(np.float32)
SPEED = (1.1 ** (-FREQ)).astype(np.float32)
RFAC = (np.float32(0.5) + np.float32(0.5) * SPEED).astype(np.float32)


def grouped(values):
    kept, place = [], []
    for v in values:
        near = [i for i, k in enumerate(kept) if abs(k - v) <= 4e-7 * abs(k)]
        if not near:
            kept.append(float(v))
        place.append(near[0] if near else len(kept) - 1)
    return kept, place


WEIGHTS, PLACE = grouped(np.abs(np.concatenate([COS, SIN])).astype(np.float64))
KX, KY = PLACE[:DIRS], PLACE[DIRS:]
REST, K0 = grouped([WEIGHTS[KX[d]] + WEIGHTS[KY[d]] for d in range(DIRS)])
COEF = np.concatenate(
    [
        0.42 * SPEED.astype(np.float64)[:, None] * np.array(WEIGHTS)[None, :],
        1.0 - 0.42 * SPEED.astype(np.float64)[:, None] * np.array(REST)[None, :],
    ],
    axis=1,
).astype(np.float32)

FULL = 3
CHUNKS = ((0, 2, False), (2, 1, True))
WHOLE = FULL * BLOCKS
WINDOW = 2
HALF = LANES // 2
SUMS_AT = 3 * (WHOLE + 1)
MADE = SUMS_AT + 2 * BLOCKS

SOUTH = [d for d in range(DIRS) if SIN[d] >= 0]
NORTH = [d for d in range(DIRS) if SIN[d] < 0]
REACH = SUB - 1
PLANES = len(SOUTH) + REACH
EXTRAS = []
for k in range(1, REACH + 1):
    EXTRAS += [
        ("s", (SOUTH[-1] + k) % DIRS, k),
        ("s", (SOUTH[0] - k) % DIRS, k),
        ("n", (NORTH[-1] + k) % DIRS, k),
        ("n", (NORTH[0] - k) % DIRS, k),
    ]
EXTRA_AT = {(w, d): i for i, (w, d, _) in enumerate(EXTRAS)}
VMEM_LIMIT = 40 * 1024 * 1024


def window(d):
    return "s" if d in SOUTH else "n"


def tiles_of(chunk):
    return chunk[1] * BLOCKS + (WINDOW if chunk[2] else 0)


def slots_of(chunk):
    return tiles_of(chunk) + chunk[1] + (2 if chunk[2] else 1)


def smem():
    return pl.BlockSpec(memory_space=pltpu.SMEM)


def vmem():
    return pl.BlockSpec(memory_space=pltpu.VMEM)


def call(kernel, name, out, args, n_smem, scratch=(), cost=4_000_000):
    return pl.pallas_call(
        kernel,
        out_shape=jax.tree.map(lambda s: jax.ShapeDtypeStruct(s, jnp.float32), out, is_leaf=lambda s: isinstance(s, tuple) and isinstance(s[0], int)),
        in_specs=[smem()] * n_smem + [vmem()] * (len(args) - n_smem),
        out_specs=jax.tree.map(lambda s: vmem(), out, is_leaf=lambda s: isinstance(s, tuple) and isinstance(s[0], int)),
        scratch_shapes=list(scratch),
        compiler_params=pltpu.CompilerParams(vmem_limit_bytes=VMEM_LIMIT),
        cost_estimate=pl.CostEstimate(flops=1000, bytes_accessed=cost, transcendentals=0),
        interpret=INTERPRET,
        name=name,
    )(*args)


def first_pack_kernel(spectrum, out, x, arrived, done):
    begin, count, _ = CHUNKS[0]
    ins = [
        [
            pltpu.make_async_copy(
                spectrum.at[d, pl.ds(j * FULL + begin, count)], x.at[d, j], arrived.at[d, j]
            )
            for j in range(BLOCKS)
        ]
        for d in range(3)
    ]
    outs = [pltpu.make_async_copy(x.at[d], out.at[:, d], done.at[d]) for d in range(3)]
    for copies in ins:
        for copy in copies:
            copy.start()
    for copies, leave in zip(ins, outs):
        for copy in copies:
            copy.wait()
        leave.start()
    for leave in outs:
        leave.wait()


def last_pack_kernel(spectrum, out, x, arrived):
    begin, count, _ = CHUNKS[1]
    copies = [pltpu.make_async_copy(spectrum.at[d], x.at[d], arrived.at[d]) for d in range(3)]
    for copy in copies:
        copy.start()
    zero = jnp.zeros((4, HALF), jnp.float32)
    for d in range(3):
        copies[d].wait()
        for j in range(BLOCKS):
            for i in range(count):
                for l in range(BLOCKS):
                    value = x[d, j * FULL + begin + i, :, l * LANES : (l + 1) * LANES]
                    out[j, d, i * BLOCKS + l] = value
            left, right = j * LANES - HALF, (j + 1) * LANES + HALF
            value = x[d, FREQS - 1, :, max(left, 0) : min(right, BLOCKS * LANES)]
            if left < 0:
                value = jnp.concatenate([zero, value], axis=1)
            if right > BLOCKS * LANES:
                value = jnp.concatenate([value, zero], axis=1)
            for i in range(WINDOW):
                out[j, d, count * BLOCKS + i] = value[:, i * LANES : (i + 1) * LANES]


def halo_kernel(tiles, with_maps, *refs):
    if with_maps:
        own, maps, up, down = refs
    else:
        own, up, down = refs
    n = len(SOUTH)
    if with_maps:
        for k in range(2):
            for l in range(BLOCKS):
                value = maps[k, :, l * LANES : (l + 1) * LANES]
                up[PLANES, k * BLOCKS + l] = value
                down[PLANES, k * BLOCKS + l] = value
    ends = {
        "s": (SOUTH[-1], SOUTH[0]),
        "n": (NORTH[0], NORTH[-1]),
    }

    def body(t, carry):
        for i, d in enumerate(SOUTH):
            up[i, t] = own[d, t]
        for i, d in enumerate(NORTH):
            down[i, t] = own[d, t]
        top, low = ends["s"]
        a = [own[(top + k) % DIRS, t] for k in range(1, 4)]
        b = [own[(low - k) % DIRS, t] for k in range(1, 4)]
        up[n, t] = jnp.concatenate([a[2][3:4], a[0][1:4]], axis=0)
        up[n + 1, t] = jnp.concatenate([b[1][2:4], a[1][2:4]], axis=0)
        up[n + 2, t] = jnp.concatenate([b[2][3:4], b[0][1:4]], axis=0)
        low, top = ends["n"]
        a = [own[(low - k) % DIRS, t] for k in range(1, 4)]
        b = [own[(top + k) % DIRS, t] for k in range(1, 4)]
        down[n, t] = jnp.concatenate([a[0][0:3], a[2][0:1]], axis=0)
        down[n + 1, t] = jnp.concatenate([a[1][0:2], b[1][0:2]], axis=0)
        down[n + 2, t] = jnp.concatenate([b[0][0:3], b[2][0:1]], axis=0)
        return carry

    lax.fori_loop(0, tiles, body, 0, unroll=4)


def step_kernel(chunk, first_call, group, coef, rfac, frsq, own, south, north, *refs):
    begin, count, tail = chunk
    tiles, slots, origin = tiles_of(chunk), slots_of(chunk), begin * BLOCKS
    if first_call:
        maps, out, around, st_a, st_b, ex_a, ex_b = refs
    else:
        around, given, out, st_a, st_b, ex_a, ex_b = refs
    me = group[0]
    whole = count * BLOCKS

    def f_of(t):
        if isinstance(t, int):
            return FREQS - 1
        f = me * FULL + begin + t // BLOCKS
        return jnp.where(t < whole, f, FREQS - 1) if tail else f

    def map_of(t):
        if isinstance(t, int):
            return BLOCKS + 2 + t - whole
        l = t % BLOCKS + 1
        return jnp.where(t < whole, l, BLOCKS + 2 + t - whole) if tail else l

    def slot_of(t):
        return t + t // BLOCKS + 1

    lane = lax.broadcasted_iota(jnp.int32, (8, LANES), 1)
    row = lax.broadcasted_iota(jnp.int32, (8, LANES), 0)
    start, end, mine, half = lane == 0, lane == LANES - 1, row < 4, lane < HALF
    zero = jnp.zeros((8, LANES), jnp.float32)
    for p in [i * (BLOCKS + 1) for i in range(count + 1)] + ([slots - 1] if tail else []):
        for d in range(DIRS):
            st_a[d, p] = zero
            st_b[d, p] = zero
        for i in range(len(EXTRAS)):
            ex_a[i, p] = zero
            ex_b[i, p] = zero

    if first_call:
        for k in range(2):
            for w, ref in enumerate((south, north)):
                around[k, w, 0] = zero
                around[k, w, BLOCKS + 1] = zero
                for l in range(BLOCKS):
                    mid = maps[k, :, l * LANES : (l + 1) * LANES]
                    around[k, w, l + 1] = jnp.concatenate([mid, ref[PLANES, k * BLOCKS + l]], axis=0)
                for i in range(WINDOW):
                    left, right = around[k, w, me + i], around[k, w, me + i + 1]
                    around[k, w, BLOCKS + 2 + i] = pltpu.roll(jnp.where(half, right, left), HALF, 1)

    def fill(t, carry):
        slot, m = slot_of(t), map_of(t)
        seas = {"s": around[0, 0, m], "n": around[0, 1, m]}
        n = len(SOUTH)

        def whole_tile(w, d, rows):
            return jnp.concatenate([own[d, t], rows], axis=0) * seas[w]

        for i, d in enumerate(SOUTH):
            st_a[d, slot] = whole_tile("s", d, south[i, t])
        for i, d in enumerate(NORTH):
            st_a[d, slot] = whole_tile("n", d, north[i, t])
        for w, ref in (("s", south), ("n", north)):
            a, b, c = (ref[n + i, t] for i in range(3))
            swap = jnp.concatenate([b[2:4], b[0:2]], axis=0)
            pick = slice(0, 1) if w == "s" else slice(3, 4)
            far_a = jnp.broadcast_to(a[pick], (4, LANES))
            far_c = jnp.broadcast_to(c[pick], (4, LANES))
            if w == "s":
                top, low = SOUTH[-1], SOUTH[0]
                line = [(top + 1, a), (top + 2, b), (top + 3, far_a)]
                line += [(low - 1, c), (low - 2, swap), (low - 3, far_c)]
            else:
                low, top = NORTH[0], NORTH[-1]
                line = [(low - 1, a), (low - 2, b), (low - 3, far_a)]
                line += [(top + 1, c), (top + 2, swap), (top + 3, far_c)]
            for d, rows in line:
                ex_a[EXTRA_AT[w, d % DIRS], slot] = whole_tile(w, d % DIRS, rows)
        return carry

    lax.fori_loop(0, tiles, fill, 0)

    if first_call:
        for i in range(2 * BLOCKS):
            out[0, SUMS_AT + i] = jnp.zeros((4, LANES), jnp.float32)
    else:
        for i in range(2 * BLOCKS):
            out[0, SUMS_AT + i] = given[0, SUMS_AT + i]
        for s in range(BLOCKS):
            for d in range(3):
                for i in range(origin):
                    out[s, d * WHOLE + i] = given[s, d * WHOLE + i]

    def keep(t, d, new):
        out[d // 3, (d % 3) * WHOLE + origin + t] = new[0:4]

    def add_up(t, f, total):
        place = SUMS_AT + (me if isinstance(t, int) else t % BLOCKS)
        total = total[0:4]
        out[0, place] += total
        out[0, place + BLOCKS] += total * frsq[f]

    def make(step, src, src_ex, dst, dst_ex):
        def body(t, carry):
            slot, m, f = slot_of(t), map_of(t), f_of(t)
            rf = rfac[f]
            coefs = [coef[f, i] for i in range(COEF.shape[1])]
            seas = {"s": around[0, 0, m], "n": around[0, 1, m]}
            raw = {"s": around[1, 0, m], "n": around[1, 1, m]}
            mth = {w: jnp.abs(raw[w]) * rf for w in "sn"}
            ahead = {w: raw[w] > 0 for w in "sn"}
            loaded = {}

            def tile(w, d):
                d = d % DIRS
                key = (w, d)
                if window(d) == w or step == SUB - 1:
                    key = (window(d), d)
                if key not in loaded:
                    if key[0] == window(d):
                        loaded[key] = (src, d, src[d, slot])
                    else:
                        i = EXTRA_AT[key]
                        loaded[key] = (src_ex, i, src_ex[i, slot])
                return loaded[key]

            def update(w, d):
                ref, i, a = tile(w, d)
                before, after = tile(w, d - 1)[2], tile(w, d + 1)[2]
                if COS[d] >= 0:
                    x = pltpu.roll(jnp.where(end, ref[i, slot - 1], a), 1, 1)
                else:
                    x = pltpu.roll(jnp.where(start, ref[i, slot + 1], a), LANES - 1, 1)
                y = pltpu.roll(a, 1 if SIN[d] >= 0 else 7, 0)
                turned = mth[w] * (jnp.where(ahead[w], before, after) - a)
                stay = coefs[len(WEIGHTS) + K0[d]]
                return (a * stay + x * coefs[KX[d]] + y * coefs[KY[d]] + turned) * seas[w]

            fresh = {}
            total = None
            for d in range(DIRS):
                new = update(window(d), d)
                if step < SUB - 1 or isinstance(t, int):
                    fresh[d] = new
                    dst[d, slot] = new
                else:
                    keep(t, d, new)
                    total = new if total is None else total + new
            for i, (w, d, k) in enumerate(EXTRAS):
                if k < REACH - step:
                    dst_ex[i, slot] = jnp.where(mine, fresh[d], update(w, d))
            if total is not None:
                add_up(t, f, total)
            return carry

        return body

    bufs = [(st_a, ex_a), (st_b, ex_b)]
    for step in range(SUB):
        (src, src_ex), (dst, dst_ex) = bufs[step % 2], bufs[(step + 1) % 2]
        body = make(step, src, src_ex, dst, dst_ex)
        if step < SUB - 1:
            lax.fori_loop(0, tiles, body, 0, unroll=(tiles if tail else BLOCKS) if UNROLL else 1)
        else:
            lax.fori_loop(0, whole, body, 0, unroll=BLOCKS if UNROLL else 1)
    if tail:
        for t in range(whole, tiles):
            body(t, 0)
        total = None
        for d in range(DIRS):
            left, right = dst[d, slot_of(whole)], dst[d, slot_of(whole + 1)]
            new = pltpu.roll(jnp.where(half, right, left), HALF, 1)
            out[d // 3, 3 * WHOLE + d % 3] = new[0:4]
            total = new if total is None else total + new
        add_up(whole, FREQS - 1, total)
    if not first_call:
        for i in range(2 * BLOCKS):
            value = out[0, SUMS_AT + i]
            for s in range(1, BLOCKS):
                out[s, SUMS_AT + i] = value


def step_call(chunk, first_call, group, own, south, north, rest):
    slots = slots_of(chunk)
    state = pltpu.VMEM((DIRS, slots, 8, LANES), jnp.float32)
    extra = pltpu.VMEM((len(EXTRAS), slots, 8, LANES), jnp.float32)
    out = [(BLOCKS, MADE, 4, LANES)]
    if first_call:
        out.append((2, 2, BLOCKS + 2 + WINDOW, 8, LANES))
    args = (group, COEF, RFAC, FR * FR, own, south, north, *rest)
    return call(
        functools.partial(step_kernel, chunk, first_call),
        "steps",
        out,
        args,
        4,
        [state, state, extra, extra],
        20_000_000,
    )


def source_kernel(cos, sin, got, wind_u, wind_v, out, made, shrink, done):
    inverse = 1.0 / (DIRS * FREQS)
    columns = [slice(t * LANES, (t + 1) * LANES) for t in range(BLOCKS)]
    for t, cols in enumerate(columns):
        m0 = got[0, SUMS_AT + t]
        m2 = got[0, SUMS_AT + BLOCKS + t]
        for j in range(1, BLOCKS):
            m0 = m0 + got[j, SUMS_AT + t]
            m2 = m2 + got[j, SUMS_AT + BLOCKS + t]
        ratio = 0.5 * (m2 * inverse) / (1.0 + m0 * inverse)
        for f in range(FREQS):
            shrink[f, :, cols] = 1.0 / (1.0 + ratio * float(FR[f] * FR[f]))
    copies = []
    for d in range(3):
        for t, cols in enumerate(columns):
            along = wind_u[:, cols] * cos[d] + wind_v[:, cols] * sin[d]
            gain = 0.5 * jnp.maximum(along, 0.0)
            for f in range(FREQS):
                if f < BLOCKS * FULL:
                    a = got[f // FULL, d * WHOLE + f % FULL * BLOCKS + t]
                else:
                    a = got[t, 3 * WHOLE + d]
                made[d, f, :, cols] = a * (1.0 + gain * float(FR[f])) * shrink[f, :, cols]
        copies.append(pltpu.make_async_copy(made.at[d], out.at[d], done.at[d]))
        copies[-1].start()
    for copy in copies:
        copy.wait()


def moving(kernel, name, out, ins, out_space, args, scratch):
    return pl.pallas_call(
        kernel,
        out_shape=[jax.ShapeDtypeStruct(s, jnp.float32) for s in out],
        in_specs=ins,
        out_specs=[out_space for _ in out],
        scratch_shapes=scratch,
        compiler_params=pltpu.CompilerParams(vmem_limit_bytes=60 * 1024 * 1024 if "pack" in name else VMEM_LIMIT),
        interpret=INTERPRET,
        name=name,
    )(*args)


def tiled(rows):
    return jnp.swapaxes(rows.reshape(rows.shape[:-1] + (BLOCKS, LANES)), -2, -3)


def on_device(spectrum, sea_mask, turning, wind_u, wind_v):
    me = lax.axis_index("spec")
    group = me.reshape(1)
    count = lax.axis_size("space")
    up = [(i, i + 1) for i in range(count - 1)]
    down = [(j, i) for i, j in up]

    maps = jnp.stack([(sea_mask == 1).astype(jnp.float32), turning])
    hbm = pl.BlockSpec(memory_space=pltpu.HBM)
    room = pltpu.VMEM(spectrum.shape, jnp.float32)
    first, last = CHUNKS
    (pack,) = moving(
        first_pack_kernel,
        "first_pack",
        [(BLOCKS, 3, first[1]) + spectrum.shape[2:]],
        [hbm],
        hbm,
        (spectrum,),
        [
            pltpu.VMEM((3, BLOCKS, first[1]) + spectrum.shape[2:], jnp.float32),
            pltpu.SemaphoreType.DMA((3, BLOCKS)),
            pltpu.SemaphoreType.DMA((3,)),
        ],
    )
    (pack_2,) = moving(
        last_pack_kernel,
        "last_pack",
        [(BLOCKS, 3, tiles_of(last), 4, LANES)],
        [hbm],
        vmem(),
        (spectrum,),
        [room, pltpu.SemaphoreType.DMA((3,))],
    )

    def edges(tiles, planes, *args):
        kernel = functools.partial(halo_kernel, tiles, len(args) > 1)
        return call(kernel, "halo", [(planes, tiles, 4, LANES)] * 2, args, 0)

    own = lax.all_to_all(pack, "spec", 0, 0, tiled=True)
    own = tiled(own).reshape(DIRS, tiles_of(first), 4, LANES)
    low, high = edges(tiles_of(first), PLANES + 1, own, maps)
    pack_2, low, high = lax.optimization_barrier((pack_2, low, high))
    own_2 = lax.all_to_all(pack_2, "spec", 0, 0, tiled=True)
    own_2 = own_2.reshape(DIRS, tiles_of(last), 4, LANES)
    low_2, high_2 = edges(tiles_of(last), PLANES, own_2)
    south, north = lax.ppermute(low, "space", up), lax.ppermute(high, "space", down)
    south, north, _, _ = lax.optimization_barrier((south, north, low_2, high_2))
    south_2, north_2 = lax.ppermute(low_2, "space", up), lax.ppermute(high_2, "space", down)
    made, around = step_call(CHUNKS[0], True, group, own, south, north, (maps,))
    (made,) = step_call(CHUNKS[1], False, group, own_2, south_2, north_2, (around, made))
    got = lax.all_to_all(made, "spec", 0, 0, tiled=True)
    cos = lax.dynamic_slice_in_dim(jnp.asarray(COS), me * 3, 3)
    sin = lax.dynamic_slice_in_dim(jnp.asarray(SIN), me * 3, 3)
    (result,) = moving(
        source_kernel,
        "source",
        [spectrum.shape],
        [smem(), smem(), vmem(), vmem(), vmem()],
        hbm,
        (cos, sin, got, wind_u, wind_v),
        [room, pltpu.VMEM(spectrum.shape[1:], jnp.float32), pltpu.SemaphoreType.DMA((3,))],
    )
    return result


def solution(mesh):
    rows = P("space", None)
    bins = P("spec", None, "space", None)
    return jax.shard_map(
        on_device,
        mesh=mesh,
        in_specs=(bins, rows, rows, rows, rows),
        out_specs=bins,
        check_vma=False,
    )
```

```python
import functools

import jax
import jax.numpy as jnp
import numpy as np
from jax import lax
from jax.experimental import pallas as pl
from jax.experimental.pallas import tpu as pltpu
from jax.sharding import PartitionSpec as P

DIRS = 24
FREQS = 25
SUB = 4
INTERPRET = False
UNROLL = True
LANES = 128
BLOCKS = 8

THETA = (np.float32(2.0 * np.pi) * np.arange(DIRS, dtype=np.float32) / np.float32(DIRS)).astype(
    np.float32
)
COS = np.cos(THETA).astype(np.float32)
SIN = np.sin(THETA).astype(np.float32)
FREQ = np.arange(FREQS, dtype=np.float64)
FR = (1.1 ** (FREQ - FREQS // 2)).astype(np.float32)
SPEED = (1.1 ** (-FREQ)).astype(np.float32)
RFAC = (np.float32(0.5) + np.float32(0.5) * SPEED).astype(np.float32)


def grouped(values):
    kept, place = [], []
    for v in values:
        near = [i for i, k in enumerate(kept) if abs(k - v) <= 4e-7 * abs(k)]
        if not near:
            kept.append(float(v))
        place.append(near[0] if near else len(kept) - 1)
    return kept, place


WEIGHTS, PLACE = grouped(np.abs(np.concatenate([COS, SIN])).astype(np.float64))
KX, KY = PLACE[:DIRS], PLACE[DIRS:]
REST, K0 = grouped([WEIGHTS[KX[d]] + WEIGHTS[KY[d]] for d in range(DIRS)])
COEF = np.concatenate(
    [
        0.42 * SPEED.astype(np.float64)[:, None] * np.array(WEIGHTS)[None, :],
        1.0 - 0.42 * SPEED.astype(np.float64)[:, None] * np.array(REST)[None, :],
    ],
    axis=1,
).astype(np.float32)

FULL = 3
CHUNKS = ((0, 2, False), (2, 1, True))
WHOLE = FULL * BLOCKS
WINDOW = 2
HALF = LANES // 2
FIRST_MADE = 3 * CHUNKS[0][1] * BLOCKS
SUMS_AT = 3 * (WHOLE + 1)
MADE = SUMS_AT + 2 * BLOCKS

SOUTH = [d for d in range(DIRS) if SIN[d] >= 0]
NORTH = [d for d in range(DIRS) if SIN[d] < 0]
REACH = SUB - 1
PLANES = len(SOUTH) + REACH
EXTRAS = []
for k in range(1, REACH + 1):
    EXTRAS += [
        ("s", (SOUTH[-1] + k) % DIRS, k),
        ("s", (SOUTH[0] - k) % DIRS, k),
        ("n", (NORTH[-1] + k) % DIRS, k),
        ("n", (NORTH[0] - k) % DIRS, k),
    ]
EXTRA_AT = {(w, d): i for i, (w, d, _) in enumerate(EXTRAS)}
VMEM_LIMIT = 40 * 1024 * 1024


def window(d):
    return "s" if d in SOUTH else "n"


def tiles_of(chunk):
    return chunk[1] * BLOCKS + (WINDOW if chunk[2] else 0)


def slots_of(chunk):
    return tiles_of(chunk) + chunk[1] + (2 if chunk[2] else 1)


def smem():
    return pl.BlockSpec(memory_space=pltpu.SMEM)


def vmem():
    return pl.BlockSpec(memory_space=pltpu.VMEM)


def call(kernel, name, out, args, n_smem, scratch=(), cost=4_000_000):
    return pl.pallas_call(
        kernel,
        out_shape=jax.tree.map(lambda s: jax.ShapeDtypeStruct(s, jnp.float32), out, is_leaf=lambda s: isinstance(s, tuple) and isinstance(s[0], int)),
        in_specs=[smem()] * n_smem + [vmem()] * (len(args) - n_smem),
        out_specs=jax.tree.map(lambda s: vmem(), out, is_leaf=lambda s: isinstance(s, tuple) and isinstance(s[0], int)),
        scratch_shapes=list(scratch),
        compiler_params=pltpu.CompilerParams(vmem_limit_bytes=VMEM_LIMIT),
        cost_estimate=pl.CostEstimate(flops=1000, bytes_accessed=cost, transcendentals=0),
        interpret=INTERPRET,
        name=name,
    )(*args)


def first_pack_kernel(spectrum, out, x, arrived, done):
    begin, count, _ = CHUNKS[0]
    ins = [
        [
            pltpu.make_async_copy(
                spectrum.at[d, pl.ds(j * FULL + begin, count)], x.at[d, j], arrived.at[d, j]
            )
            for j in range(BLOCKS)
        ]
        for d in range(3)
    ]
    outs = [pltpu.make_async_copy(x.at[d], out.at[:, d], done.at[d]) for d in range(3)]
    for copies in ins:
        for copy in copies:
            copy.start()
    for copies, leave in zip(ins, outs):
        for copy in copies:
            copy.wait()
        leave.start()
    for leave in outs:
        leave.wait()


def last_pack_kernel(spectrum, out, x, arrived):
    begin, count, _ = CHUNKS[1]
    copies = [pltpu.make_async_copy(spectrum.at[d], x.at[d], arrived.at[d]) for d in range(3)]
    for copy in copies:
        copy.start()
    zero = jnp.zeros((4, HALF), jnp.float32)
    for d in range(3):
        copies[d].wait()
        for j in range(BLOCKS):
            for i in range(count):
                for l in range(BLOCKS):
                    value = x[d, j * FULL + begin + i, :, l * LANES : (l + 1) * LANES]
                    out[j, d, i * BLOCKS + l] = value
            left, right = j * LANES - HALF, (j + 1) * LANES + HALF
            value = x[d, FREQS - 1, :, max(left, 0) : min(right, BLOCKS * LANES)]
            if left < 0:
                value = jnp.concatenate([zero, value], axis=1)
            if right > BLOCKS * LANES:
                value = jnp.concatenate([value, zero], axis=1)
            for i in range(WINDOW):
                out[j, d, count * BLOCKS + i] = value[:, i * LANES : (i + 1) * LANES]


def halo_kernel(tiles, with_maps, *refs):
    if with_maps:
        own, maps, up, down = refs
    else:
        own, up, down = refs
    n = len(SOUTH)
    if with_maps:
        for k in range(2):
            for l in range(BLOCKS):
                value = maps[k, :, l * LANES : (l + 1) * LANES]
                up[PLANES, k * BLOCKS + l] = value
                down[PLANES, k * BLOCKS + l] = value
    ends = {
        "s": (SOUTH[-1], SOUTH[0]),
        "n": (NORTH[0], NORTH[-1]),
    }

    def body(t, carry):
        for i, d in enumerate(SOUTH):
            up[i, t] = own[d, t]
        for i, d in enumerate(NORTH):
            down[i, t] = own[d, t]
        top, low = ends["s"]
        a = [own[(top + k) % DIRS, t] for k in range(1, 4)]
        b = [own[(low - k) % DIRS, t] for k in range(1, 4)]
        up[n, t] = jnp.concatenate([a[2][3:4], a[0][1:4]], axis=0)
        up[n + 1, t] = jnp.concatenate([b[1][2:4], a[1][2:4]], axis=0)
        up[n + 2, t] = jnp.concatenate([b[2][3:4], b[0][1:4]], axis=0)
        low, top = ends["n"]
        a = [own[(low - k) % DIRS, t] for k in range(1, 4)]
        b = [own[(top + k) % DIRS, t] for k in range(1, 4)]
        down[n, t] = jnp.concatenate([a[0][0:3], a[2][0:1]], axis=0)
        down[n + 1, t] = jnp.concatenate([a[1][0:2], b[1][0:2]], axis=0)
        down[n + 2, t] = jnp.concatenate([b[0][0:3], b[2][0:1]], axis=0)
        return carry

    lax.fori_loop(0, tiles, body, 0, unroll=4)


def step_kernel(chunk, first_call, group, coef, rfac, frsq, own, south, north, *refs):
    begin, count, tail = chunk
    tiles, slots = tiles_of(chunk), slots_of(chunk)
    if first_call:
        maps, out, around, sums, st_a, st_b, ex_a, ex_b = refs
        base = 0
    else:
        around, given, given_sums, result, st_a, st_b, ex_a, ex_b, out, sums, done = refs
        base = FIRST_MADE
        early = pltpu.make_async_copy(given, result.at[:, pl.ds(0, base)], done.at[0])
        late = pltpu.make_async_copy(out, result.at[:, pl.ds(base, MADE - base)], done.at[1])
        early.start()
    me = group[0]
    whole = count * BLOCKS

    def f_of(t):
        if isinstance(t, int):
            return FREQS - 1
        f = me * FULL + begin + t // BLOCKS
        return jnp.where(t < whole, f, FREQS - 1) if tail else f

    def map_of(t):
        if isinstance(t, int):
            return BLOCKS + 2 + t - whole
        l = t % BLOCKS + 1
        return jnp.where(t < whole, l, BLOCKS + 2 + t - whole) if tail else l

    def slot_of(t):
        return t + t // BLOCKS + 1

    lane = lax.broadcasted_iota(jnp.int32, (8, LANES), 1)
    row = lax.broadcasted_iota(jnp.int32, (8, LANES), 0)
    start, end, mine, half = lane == 0, lane == LANES - 1, row < 4, lane < HALF
    zero = jnp.zeros((8, LANES), jnp.float32)
    for p in [i * (BLOCKS + 1) for i in range(count + 1)] + ([slots - 1] if tail else []):
        for d in range(DIRS):
            st_a[d, p] = zero
            st_b[d, p] = zero
        for i in range(len(EXTRAS)):
            ex_a[i, p] = zero
            ex_b[i, p] = zero

    if first_call:
        for k in range(2):
            for w, ref in enumerate((south, north)):
                around[k, w, 0] = zero
                around[k, w, BLOCKS + 1] = zero
                for l in range(BLOCKS):
                    mid = maps[k, :, l * LANES : (l + 1) * LANES]
                    around[k, w, l + 1] = jnp.concatenate([mid, ref[PLANES, k * BLOCKS + l]], axis=0)
                for i in range(WINDOW):
                    left, right = around[k, w, me + i], around[k, w, me + i + 1]
                    around[k, w, BLOCKS + 2 + i] = pltpu.roll(jnp.where(half, right, left), HALF, 1)

    def fill(t, carry):
        slot, m = slot_of(t), map_of(t)
        seas = {"s": around[0, 0, m], "n": around[0, 1, m]}
        n = len(SOUTH)

        def whole_tile(w, d, rows):
            return jnp.concatenate([own[d, t], rows], axis=0) * seas[w]

        for i, d in enumerate(SOUTH):
            st_a[d, slot] = whole_tile("s", d, south[i, t])
        for i, d in enumerate(NORTH):
            st_a[d, slot] = whole_tile("n", d, north[i, t])
        for w, ref in (("s", south), ("n", north)):
            a, b, c = (ref[n + i, t] for i in range(3))
            swap = jnp.concatenate([b[2:4], b[0:2]], axis=0)
            pick = slice(0, 1) if w == "s" else slice(3, 4)
            far_a = jnp.broadcast_to(a[pick], (4, LANES))
            far_c = jnp.broadcast_to(c[pick], (4, LANES))
            if w == "s":
                top, low = SOUTH[-1], SOUTH[0]
                line = [(top + 1, a), (top + 2, b), (top + 3, far_a)]
                line += [(low - 1, c), (low - 2, swap), (low - 3, far_c)]
            else:
                low, top = NORTH[0], NORTH[-1]
                line = [(low - 1, a), (low - 2, b), (low - 3, far_a)]
                line += [(top + 1, c), (top + 2, swap), (top + 3, far_c)]
            for d, rows in line:
                ex_a[EXTRA_AT[w, d % DIRS], slot] = whole_tile(w, d % DIRS, rows)
        return carry

    lax.fori_loop(0, tiles, fill, 0)

    for i in range(2 * BLOCKS):
        sums[i] = jnp.zeros((4, LANES), jnp.float32) if first_call else given_sums[i]

    def keep(t, d, new):
        out[d // 3, (d % 3) * whole + t] = new[0:4]

    def add_up(t, f, total):
        place = me if isinstance(t, int) else t % BLOCKS
        total = total[0:4]
        sums[place] += total
        sums[BLOCKS + place] += total * frsq[f]

    def make(step, src, src_ex, dst, dst_ex):
        def body(t, carry):
            slot, m, f = slot_of(t), map_of(t), f_of(t)
            rf = rfac[f]
            coefs = [coef[f, i] for i in range(COEF.shape[1])]
            seas = {"s": around[0, 0, m], "n": around[0, 1, m]}
            raw = {"s": around[1, 0, m], "n": around[1, 1, m]}
            mth = {w: jnp.abs(raw[w]) * rf for w in "sn"}
            ahead = {w: raw[w] > 0 for w in "sn"}
            loaded = {}

            def tile(w, d):
                d = d % DIRS
                key = (w, d)
                if window(d) == w or step == SUB - 1:
                    key = (window(d), d)
                if key not in loaded:
                    if key[0] == window(d):
                        loaded[key] = (src, d, src[d, slot])
                    else:
                        i = EXTRA_AT[key]
                        loaded[key] = (src_ex, i, src_ex[i, slot])
                return loaded[key]

            def update(w, d):
                ref, i, a = tile(w, d)
                before, after = tile(w, d - 1)[2], tile(w, d + 1)[2]
                if COS[d] >= 0:
                    x = pltpu.roll(jnp.where(end, ref[i, slot - 1], a), 1, 1)
                else:
                    x = pltpu.roll(jnp.where(start, ref[i, slot + 1], a), LANES - 1, 1)
                y = pltpu.roll(a, 1 if SIN[d] >= 0 else 7, 0)
                turned = mth[w] * (jnp.where(ahead[w], before, after) - a)
                stay = coefs[len(WEIGHTS) + K0[d]]
                return (a * stay + x * coefs[KX[d]] + y * coefs[KY[d]] + turned) * seas[w]

            fresh = {}
            total = None
            for d in range(DIRS):
                new = update(window(d), d)
                if step < SUB - 1 or isinstance(t, int):
                    fresh[d] = new
                    dst[d, slot] = new
                else:
                    keep(t, d, new)
                    total = new if total is None else total + new
            for i, (w, d, k) in enumerate(EXTRAS):
                if k < REACH - step:
                    dst_ex[i, slot] = jnp.where(mine, fresh[d], update(w, d))
            if total is not None:
                add_up(t, f, total)
            return carry

        return body

    bufs = [(st_a, ex_a), (st_b, ex_b)]
    for step in range(SUB):
        (src, src_ex), (dst, dst_ex) = bufs[step % 2], bufs[(step + 1) % 2]
        body = make(step, src, src_ex, dst, dst_ex)
        if step < SUB - 1:
            lax.fori_loop(0, tiles, body, 0, unroll=(tiles if tail else BLOCKS) if UNROLL else 1)
        else:
            lax.fori_loop(0, whole, body, 0, unroll=BLOCKS if UNROLL else 1)
    if tail:
        for t in range(whole, tiles):
            body(t, 0)
        total = None
        for d in range(DIRS):
            left, right = dst[d, slot_of(whole)], dst[d, slot_of(whole + 1)]
            new = pltpu.roll(jnp.where(half, right, left), HALF, 1)
            out[d // 3, 3 * whole + d % 3] = new[0:4]
            total = new if total is None else total + new
        add_up(whole, FREQS - 1, total)
    if not first_call:
        for i in range(2 * BLOCKS):
            value = sums[i]
            for s in range(BLOCKS):
                out[s, SUMS_AT - base + i] = value
        late.start()
        early.wait()
        late.wait()


def step_call(chunk, first_call, group, own, south, north, rest):
    slots = slots_of(chunk)
    state = pltpu.VMEM((DIRS, slots, 8, LANES), jnp.float32)
    extra = pltpu.VMEM((len(EXTRAS), slots, 8, LANES), jnp.float32)
    args = (group, COEF, RFAC, FR * FR, own, south, north, *rest)
    scratch = [state, state, extra, extra]
    if first_call:
        out = [
            (BLOCKS, FIRST_MADE, 4, LANES),
            (2, 2, BLOCKS + 2 + WINDOW, 8, LANES),
            (2 * BLOCKS, 4, LANES),
        ]
        space = vmem()
    else:
        out = [(BLOCKS, MADE, 4, LANES)]
        space = pl.BlockSpec(memory_space=pltpu.HBM)
        scratch += [
            pltpu.VMEM((BLOCKS, MADE - FIRST_MADE, 4, LANES), jnp.float32),
            pltpu.VMEM((2 * BLOCKS, 4, LANES), jnp.float32),
            pltpu.SemaphoreType.DMA((2,)),
        ]
    return moving(
        functools.partial(step_kernel, chunk, first_call),
        "steps",
        out,
        [smem()] * 4 + [vmem()] * (len(args) - 4),
        space,
        args,
        scratch,
        20_000_000,
    )


SPAN = 5


def source_kernel(cos, sin, got, wind_u, wind_v, out, made, shrink, gains, done):
    inverse = 1.0 / (DIRS * FREQS)
    columns = [slice(t * LANES, (t + 1) * LANES) for t in range(BLOCKS)]
    for t, cols in enumerate(columns):
        m0 = got[0, SUMS_AT + t]
        m2 = got[0, SUMS_AT + BLOCKS + t]
        for j in range(1, BLOCKS):
            m0 = m0 + got[j, SUMS_AT + t]
            m2 = m2 + got[j, SUMS_AT + BLOCKS + t]
        shrink[t] = 0.5 * (m2 * inverse) / (1.0 + m0 * inverse)
        for d in range(3):
            along = wind_u[:, cols] * cos[d] + wind_v[:, cols] * sin[d]
            gains[d, t] = 0.5 * jnp.maximum(along, 0.0)
    copies = []
    for part in range(FREQS // SPAN):
        span = range(part * SPAN, (part + 1) * SPAN)
        for t, cols in enumerate(columns):
            ratio = shrink[t]
            gain = [gains[d, t] for d in range(3)]
            for f in span:
                less = 1.0 / (1.0 + ratio * float(FR[f] * FR[f]))
                j, i = f // FULL, f % FULL
                for d in range(3):
                    if f == FREQS - 1:
                        a = got[t, 3 * WHOLE + d]
                    elif i < CHUNKS[0][1]:
                        a = got[j, (d * CHUNKS[0][1] + i) * BLOCKS + t]
                    else:
                        a = got[j, FIRST_MADE + d * BLOCKS + t]
                    made[d, f, :, cols] = a * (1.0 + gain[d] * float(FR[f])) * less
        for d in range(3):
            rows = pl.ds(part * SPAN, SPAN)
            copies.append(
                pltpu.make_async_copy(made.at[d, rows], out.at[d, rows], done.at[part, d])
            )
            copies[-1].start()
    for copy in copies:
        copy.wait()


def moving(kernel, name, out, ins, out_space, args, scratch, cost=4_000_000):
    limit = 60 * 1024 * 1024 if "pack" in name else VMEM_LIMIT
    return pl.pallas_call(
        kernel,
        out_shape=[jax.ShapeDtypeStruct(s, jnp.float32) for s in out],
        in_specs=ins,
        out_specs=[out_space for _ in out],
        scratch_shapes=scratch,
        compiler_params=pltpu.CompilerParams(vmem_limit_bytes=limit),
        cost_estimate=pl.CostEstimate(flops=1000, bytes_accessed=cost, transcendentals=0),
        interpret=INTERPRET,
        name=name,
    )(*args)


def tiled(rows):
    return jnp.swapaxes(rows.reshape(rows.shape[:-1] + (BLOCKS, LANES)), -2, -3)


def on_device(spectrum, sea_mask, turning, wind_u, wind_v):
    me = lax.axis_index("spec")
    group = me.reshape(1)
    count = lax.axis_size("space")
    up = [(i, i + 1) for i in range(count - 1)]
    down = [(j, i) for i, j in up]

    maps = jnp.stack([(sea_mask == 1).astype(jnp.float32), turning])
    hbm = pl.BlockSpec(memory_space=pltpu.HBM)
    room = pltpu.VMEM(spectrum.shape, jnp.float32)
    first, last = CHUNKS
    (pack,) = moving(
        first_pack_kernel,
        "first_pack",
        [(BLOCKS, 3, first[1]) + spectrum.shape[2:]],
        [hbm],
        hbm,
        (spectrum,),
        [
            pltpu.VMEM((3, BLOCKS, first[1]) + spectrum.shape[2:], jnp.float32),
            pltpu.SemaphoreType.DMA((3, BLOCKS)),
            pltpu.SemaphoreType.DMA((3,)),
        ],
    )
    (pack_2,) = moving(
        last_pack_kernel,
        "last_pack",
        [(BLOCKS, 3, tiles_of(last), 4, LANES)],
        [hbm],
        vmem(),
        (spectrum,),
        [room, pltpu.SemaphoreType.DMA((3,))],
    )

    def edges(tiles, planes, *args):
        kernel = functools.partial(halo_kernel, tiles, len(args) > 1)
        return call(kernel, "halo", [(planes, tiles, 4, LANES)] * 2, args, 0)

    own = lax.all_to_all(pack, "spec", 0, 0, tiled=True)
    own = tiled(own).reshape(DIRS, tiles_of(first), 4, LANES)
    low, high = edges(tiles_of(first), PLANES + 1, own, maps)
    pack_2, low, high = lax.optimization_barrier((pack_2, low, high))
    own_2 = lax.all_to_all(pack_2, "spec", 0, 0, tiled=True)
    own_2 = own_2.reshape(DIRS, tiles_of(last), 4, LANES)
    low_2, high_2 = edges(tiles_of(last), PLANES, own_2)
    south, north = lax.ppermute(low, "space", up), lax.ppermute(high, "space", down)
    south, north, _, _ = lax.optimization_barrier((south, north, low_2, high_2))
    south_2, north_2 = lax.ppermute(low_2, "space", up), lax.ppermute(high_2, "space", down)
    made, around, sums = step_call(CHUNKS[0], True, group, own, south, north, (maps,))
    (made,) = step_call(CHUNKS[1], False, group, own_2, south_2, north_2, (around, made, sums))
    got = lax.all_to_all(made, "spec", 0, 0, tiled=True)
    cos = lax.dynamic_slice_in_dim(jnp.asarray(COS), me * 3, 3)
    sin = lax.dynamic_slice_in_dim(jnp.asarray(SIN), me * 3, 3)
    (result,) = moving(
        source_kernel,
        "source",
        [spectrum.shape],
        [smem(), smem(), vmem(), vmem(), vmem()],
        hbm,
        (cos, sin, got, wind_u, wind_v),
        [
            room,
            pltpu.VMEM((BLOCKS, 4, LANES), jnp.float32),
            pltpu.VMEM((3, BLOCKS, 4, LANES), jnp.float32),
            pltpu.SemaphoreType.DMA((FREQS // SPAN, 3)),
        ],
    )
    return result


def solution(mesh):
    rows = P("space", None)
    bins = P("spec", None, "space", None)
    return jax.shard_map(
        on_device,
        mesh=mesh,
        in_specs=(bins, rows, rows, rows, rows),
        out_specs=bins,
        check_vma=False,
    )
```

```python
import functools

import jax
import jax.numpy as jnp
import numpy as np
from jax import lax
from jax.experimental import pallas as pl
from jax.experimental.pallas import tpu as pltpu
from jax.sharding import PartitionSpec as P

DIRS = 24
FREQS = 25
SUB = 4
INTERPRET = False
UNROLL = True
LANES = 128
BLOCKS = 8

THETA = (np.float32(2.0 * np.pi) * np.arange(DIRS, dtype=np.float32) / np.float32(DIRS)).astype(
    np.float32
)
COS = np.cos(THETA).astype(np.float32)
SIN = np.sin(THETA).astype(np.float32)
FREQ = np.arange(FREQS, dtype=np.float64)
FR = (1.1 ** (FREQ - FREQS // 2)).astype(np.float32)
SPEED = (1.1 ** (-FREQ)).astype(np.float32)
RFAC = (np.float32(0.5) + np.float32(0.5) * SPEED).astype(np.float32)


def grouped(values):
    kept, place = [], []
    for v in values:
        near = [i for i, k in enumerate(kept) if abs(k - v) <= 4e-7 * abs(k)]
        if not near:
            kept.append(float(v))
        place.append(near[0] if near else len(kept) - 1)
    return kept, place


WEIGHTS, PLACE = grouped(np.abs(np.concatenate([COS, SIN])).astype(np.float64))
KX, KY = PLACE[:DIRS], PLACE[DIRS:]
REST, K0 = grouped([WEIGHTS[KX[d]] + WEIGHTS[KY[d]] for d in range(DIRS)])
COEF = np.concatenate(
    [
        0.42 * SPEED.astype(np.float64)[:, None] * np.array(WEIGHTS)[None, :],
        1.0 - 0.42 * SPEED.astype(np.float64)[:, None] * np.array(REST)[None, :],
    ],
    axis=1,
).astype(np.float32)

FULL = 3
CHUNKS = ((0, 2, False), (2, 1, True))
WHOLE = FULL * BLOCKS
WINDOW = 2
HALF = LANES // 2
FIRST_MADE = 3 * CHUNKS[0][1] * BLOCKS
SUMS_AT = 3 * (WHOLE + 1)
MADE = SUMS_AT + 2 * BLOCKS

SOUTH = [d for d in range(DIRS) if SIN[d] >= 0]
NORTH = [d for d in range(DIRS) if SIN[d] < 0]
REACH = SUB - 1
PLANES = len(SOUTH) + REACH
EXTRAS = []
for k in range(1, REACH + 1):
    EXTRAS += [
        ("s", (SOUTH[-1] + k) % DIRS, k),
        ("s", (SOUTH[0] - k) % DIRS, k),
        ("n", (NORTH[-1] + k) % DIRS, k),
        ("n", (NORTH[0] - k) % DIRS, k),
    ]
EXTRA_AT = {(w, d): i for i, (w, d, _) in enumerate(EXTRAS)}
VMEM_LIMIT = 40 * 1024 * 1024


def window(d):
    return "s" if d in SOUTH else "n"


def tiles_of(chunk):
    return chunk[1] * BLOCKS + (WINDOW if chunk[2] else 0)


def slots_of(chunk):
    return tiles_of(chunk) + chunk[1] + (2 if chunk[2] else 1)


def smem():
    return pl.BlockSpec(memory_space=pltpu.SMEM)


def vmem():
    return pl.BlockSpec(memory_space=pltpu.VMEM)


def call(kernel, name, out, args, n_smem, scratch=(), cost=4_000_000):
    return pl.pallas_call(
        kernel,
        out_shape=jax.tree.map(lambda s: jax.ShapeDtypeStruct(s, jnp.float32), out, is_leaf=lambda s: isinstance(s, tuple) and isinstance(s[0], int)),
        in_specs=[smem()] * n_smem + [vmem()] * (len(args) - n_smem),
        out_specs=jax.tree.map(lambda s: vmem(), out, is_leaf=lambda s: isinstance(s, tuple) and isinstance(s[0], int)),
        scratch_shapes=list(scratch),
        compiler_params=pltpu.CompilerParams(vmem_limit_bytes=VMEM_LIMIT),
        cost_estimate=pl.CostEstimate(flops=1000, bytes_accessed=cost, transcendentals=0),
        interpret=INTERPRET,
        name=name,
    )(*args)


def first_pack_kernel(spectrum, out, x, arrived, done):
    begin, count, _ = CHUNKS[0]
    ins = [
        [
            pltpu.make_async_copy(
                spectrum.at[d, pl.ds(j * FULL + begin, count)], x.at[d, j], arrived.at[d, j]
            )
            for j in range(BLOCKS)
        ]
        for d in range(3)
    ]
    outs = [pltpu.make_async_copy(x.at[d], out.at[:, d], done.at[d]) for d in range(3)]
    for copies in ins:
        for copy in copies:
            copy.start()
    for copies, leave in zip(ins, outs):
        for copy in copies:
            copy.wait()
        leave.start()
    for leave in outs:
        leave.wait()


def last_pack_kernel(spectrum, out, x, arrived):
    begin, count, _ = CHUNKS[1]
    copies = [pltpu.make_async_copy(spectrum.at[d], x.at[d], arrived.at[d]) for d in range(3)]
    for copy in copies:
        copy.start()
    zero = jnp.zeros((4, HALF), jnp.float32)
    for d in range(3):
        copies[d].wait()
        for j in range(BLOCKS):
            for i in range(count):
                for l in range(BLOCKS):
                    value = x[d, j * FULL + begin + i, :, l * LANES : (l + 1) * LANES]
                    out[j, d, i * BLOCKS + l] = value
            left, right = j * LANES - HALF, (j + 1) * LANES + HALF
            value = x[d, FREQS - 1, :, max(left, 0) : min(right, BLOCKS * LANES)]
            if left < 0:
                value = jnp.concatenate([zero, value], axis=1)
            if right > BLOCKS * LANES:
                value = jnp.concatenate([value, zero], axis=1)
            for i in range(WINDOW):
                out[j, d, count * BLOCKS + i] = value[:, i * LANES : (i + 1) * LANES]


def halo_kernel(tiles, with_maps, group, *refs):
    own, far, near = refs[0], refs[-2], refs[-1]
    maps = refs[1] if with_maps else None
    n = len(SOUTH)

    def write(up, down):
        if with_maps:
            for k in range(2):
                for l in range(BLOCKS):
                    value = maps[k, :, l * LANES : (l + 1) * LANES]
                    up[PLANES, k * BLOCKS + l] = value
                    down[PLANES, k * BLOCKS + l] = value
        ends = {
            "s": (SOUTH[-1], SOUTH[0]),
            "n": (NORTH[0], NORTH[-1]),
        }

        def body(t, carry):
            for i, d in enumerate(SOUTH):
                up[i, t] = own[d, t]
            for i, d in enumerate(NORTH):
                down[i, t] = own[d, t]
            top, low = ends["s"]
            a = [own[(top + k) % DIRS, t] for k in range(1, 4)]
            b = [own[(low - k) % DIRS, t] for k in range(1, 4)]
            up[n, t] = jnp.concatenate([a[2][3:4], a[0][1:4]], axis=0)
            up[n + 1, t] = jnp.concatenate([b[1][2:4], a[1][2:4]], axis=0)
            up[n + 2, t] = jnp.concatenate([b[2][3:4], b[0][1:4]], axis=0)
            low, top = ends["n"]
            a = [own[(low - k) % DIRS, t] for k in range(1, 4)]
            b = [own[(top + k) % DIRS, t] for k in range(1, 4)]
            down[n, t] = jnp.concatenate([a[0][0:3], a[2][0:1]], axis=0)
            down[n + 1, t] = jnp.concatenate([a[1][0:2], b[1][0:2]], axis=0)
            down[n + 2, t] = jnp.concatenate([b[0][0:3], b[2][0:1]], axis=0)
            return carry

        lax.fori_loop(0, tiles, body, 0, unroll=4)

    pl.when(group[1] == 1)(lambda: write(far, near))
    pl.when(group[1] == 0)(lambda: write(near, far))


def step_kernel(chunk, first_call, group, coef, rfac, frsq, own, far, near, *refs):
    begin, count, tail = chunk
    tiles, slots = tiles_of(chunk), slots_of(chunk)
    if first_call:
        maps, out, around, sums, st_a, st_b, ex_a, ex_b = refs
        base = 0
    else:
        around, given, given_sums, result, st_a, st_b, ex_a, ex_b, out, sums, done = refs
        base = FIRST_MADE
        early = pltpu.make_async_copy(given, result.at[:, pl.ds(0, base)], done.at[0])
        late = pltpu.make_async_copy(out, result.at[:, pl.ds(base, MADE - base)], done.at[1])
        early.start()
    me = group[0]
    whole = count * BLOCKS

    def f_of(t):
        if isinstance(t, int):
            return FREQS - 1
        f = me * FULL + begin + t // BLOCKS
        return jnp.where(t < whole, f, FREQS - 1) if tail else f

    def map_of(t):
        if isinstance(t, int):
            return BLOCKS + 2 + t - whole
        l = t % BLOCKS + 1
        return jnp.where(t < whole, l, BLOCKS + 2 + t - whole) if tail else l

    def slot_of(t):
        return t + t // BLOCKS + 1

    lane = lax.broadcasted_iota(jnp.int32, (8, LANES), 1)
    row = lax.broadcasted_iota(jnp.int32, (8, LANES), 0)
    start, end, mine, half = lane == 0, lane == LANES - 1, row < 4, lane < HALF
    zero = jnp.zeros((8, LANES), jnp.float32)
    for p in [i * (BLOCKS + 1) for i in range(count + 1)] + ([slots - 1] if tail else []):
        for d in range(DIRS):
            st_a[d, p] = zero
            st_b[d, p] = zero
        for i in range(len(EXTRAS)):
            ex_a[i, p] = zero
            ex_b[i, p] = zero

    def load(south, north):
        if first_call:
            for k in range(2):
                for w, ref in enumerate((south, north)):
                    around[k, w, 0] = zero
                    around[k, w, BLOCKS + 1] = zero
                    for l in range(BLOCKS):
                        mid = maps[k, :, l * LANES : (l + 1) * LANES]
                        around[k, w, l + 1] = jnp.concatenate([mid, ref[PLANES, k * BLOCKS + l]], axis=0)
                    for i in range(WINDOW):
                        left, right = around[k, w, me + i], around[k, w, me + i + 1]
                        around[k, w, BLOCKS + 2 + i] = pltpu.roll(jnp.where(half, right, left), HALF, 1)

        def fill(t, carry):
            slot, m = slot_of(t), map_of(t)
            seas = {"s": around[0, 0, m], "n": around[0, 1, m]}
            n = len(SOUTH)

            def whole_tile(w, d, rows):
                return jnp.concatenate([own[d, t], rows], axis=0) * seas[w]

            for i, d in enumerate(SOUTH):
                st_a[d, slot] = whole_tile("s", d, south[i, t])
            for i, d in enumerate(NORTH):
                st_a[d, slot] = whole_tile("n", d, north[i, t])
            for w, ref in (("s", south), ("n", north)):
                a, b, c = (ref[n + i, t] for i in range(3))
                swap = jnp.concatenate([b[2:4], b[0:2]], axis=0)
                pick = slice(0, 1) if w == "s" else slice(3, 4)
                far_a = jnp.broadcast_to(a[pick], (4, LANES))
                far_c = jnp.broadcast_to(c[pick], (4, LANES))
                if w == "s":
                    top, low = SOUTH[-1], SOUTH[0]
                    line = [(top + 1, a), (top + 2, b), (top + 3, far_a)]
                    line += [(low - 1, c), (low - 2, swap), (low - 3, far_c)]
                else:
                    low, top = NORTH[0], NORTH[-1]
                    line = [(low - 1, a), (low - 2, b), (low - 3, far_a)]
                    line += [(top + 1, c), (top + 2, swap), (top + 3, far_c)]
                for d, rows in line:
                    ex_a[EXTRA_AT[w, d % DIRS], slot] = whole_tile(w, d % DIRS, rows)
            return carry

        lax.fori_loop(0, tiles, fill, 0)

    pl.when(group[1] == 1)(lambda: load(near, far))
    pl.when(group[1] == 0)(lambda: load(far, near))

    for i in range(2 * BLOCKS):
        sums[i] = jnp.zeros((4, LANES), jnp.float32) if first_call else given_sums[i]

    def keep(t, d, new):
        out[d // 3, (d % 3) * whole + t] = new[0:4]

    def add_up(t, f, total):
        place = me if isinstance(t, int) else t % BLOCKS
        total = total[0:4]
        sums[place] += total
        sums[BLOCKS + place] += total * frsq[f]

    def make(step, src, src_ex, dst, dst_ex):
        def body(t, carry):
            slot, m, f = slot_of(t), map_of(t), f_of(t)
            rf = rfac[f]
            coefs = [coef[f, i] for i in range(COEF.shape[1])]
            seas = {"s": around[0, 0, m], "n": around[0, 1, m]}
            raw = {"s": around[1, 0, m], "n": around[1, 1, m]}
            mth = {w: jnp.abs(raw[w]) * rf for w in "sn"}
            ahead = {w: raw[w] > 0 for w in "sn"}
            loaded = {}

            def tile(w, d):
                d = d % DIRS
                key = (w, d)
                if window(d) == w or step == SUB - 1:
                    key = (window(d), d)
                if key not in loaded:
                    if key[0] == window(d):
                        loaded[key] = (src, d, src[d, slot])
                    else:
                        i = EXTRA_AT[key]
                        loaded[key] = (src_ex, i, src_ex[i, slot])
                return loaded[key]

            def update(w, d):
                ref, i, a = tile(w, d)
                before, after = tile(w, d - 1)[2], tile(w, d + 1)[2]
                if COS[d] >= 0:
                    x = pltpu.roll(jnp.where(end, ref[i, slot - 1], a), 1, 1)
                else:
                    x = pltpu.roll(jnp.where(start, ref[i, slot + 1], a), LANES - 1, 1)
                y = pltpu.roll(a, 1 if SIN[d] >= 0 else 7, 0)
                turned = mth[w] * (jnp.where(ahead[w], before, after) - a)
                stay = coefs[len(WEIGHTS) + K0[d]]
                return (a * stay + x * coefs[KX[d]] + y * coefs[KY[d]] + turned) * seas[w]

            fresh = {}
            total = None
            for d in range(DIRS):
                new = update(window(d), d)
                if step < SUB - 1 or isinstance(t, int):
                    fresh[d] = new
                    dst[d, slot] = new
                else:
                    keep(t, d, new)
                    total = new if total is None else total + new
            for i, (w, d, k) in enumerate(EXTRAS):
                if k < REACH - step:
                    dst_ex[i, slot] = jnp.where(mine, fresh[d], update(w, d))
            if total is not None:
                add_up(t, f, total)
            return carry

        return body

    bufs = [(st_a, ex_a), (st_b, ex_b)]
    for step in range(SUB):
        (src, src_ex), (dst, dst_ex) = bufs[step % 2], bufs[(step + 1) % 2]
        body = make(step, src, src_ex, dst, dst_ex)
        if step < SUB - 1:
            lax.fori_loop(0, tiles, body, 0, unroll=(tiles if tail else BLOCKS) if UNROLL else 1)
        else:
            lax.fori_loop(0, whole, body, 0, unroll=BLOCKS if UNROLL else 1)
    if tail:
        for t in range(whole, tiles):
            body(t, 0)
        total = None
        for d in range(DIRS):
            left, right = dst[d, slot_of(whole)], dst[d, slot_of(whole + 1)]
            new = pltpu.roll(jnp.where(half, right, left), HALF, 1)
            out[d // 3, 3 * whole + d % 3] = new[0:4]
            total = new if total is None else total + new
        add_up(whole, FREQS - 1, total)
    if not first_call:
        for i in range(2 * BLOCKS):
            value = sums[i]
            for s in range(BLOCKS):
                out[s, SUMS_AT - base + i] = value
        late.start()
        early.wait()
        late.wait()


def step_call(chunk, first_call, group, own, far, near, rest):
    slots = slots_of(chunk)
    state = pltpu.VMEM((DIRS, slots, 8, LANES), jnp.float32)
    extra = pltpu.VMEM((len(EXTRAS), slots, 8, LANES), jnp.float32)
    args = (group, COEF, RFAC, FR * FR, own, far, near, *rest)
    scratch = [state, state, extra, extra]
    if first_call:
        out = [
            (BLOCKS, FIRST_MADE, 4, LANES),
            (2, 2, BLOCKS + 2 + WINDOW, 8, LANES),
            (2 * BLOCKS, 4, LANES),
        ]
        space = vmem()
    else:
        out = [(BLOCKS, MADE, 4, LANES)]
        space = pl.BlockSpec(memory_space=pltpu.HBM)
        scratch += [
            pltpu.VMEM((BLOCKS, MADE - FIRST_MADE, 4, LANES), jnp.float32),
            pltpu.VMEM((2 * BLOCKS, 4, LANES), jnp.float32),
            pltpu.SemaphoreType.DMA((2,)),
        ]
    return moving(
        functools.partial(step_kernel, chunk, first_call),
        "steps",
        out,
        [smem()] * 4 + [vmem()] * (len(args) - 4),
        space,
        args,
        scratch,
        20_000_000,
    )


SPAN = 5


def source_kernel(cos, sin, got, wind_u, wind_v, out, made, shrink, gains, done):
    inverse = 1.0 / (DIRS * FREQS)
    columns = [slice(t * LANES, (t + 1) * LANES) for t in range(BLOCKS)]
    for t, cols in enumerate(columns):
        m0 = got[0, SUMS_AT + t]
        m2 = got[0, SUMS_AT + BLOCKS + t]
        for j in range(1, BLOCKS):
            m0 = m0 + got[j, SUMS_AT + t]
            m2 = m2 + got[j, SUMS_AT + BLOCKS + t]
        shrink[t] = 0.5 * (m2 * inverse) / (1.0 + m0 * inverse)
        for d in range(3):
            along = wind_u[:, cols] * cos[d] + wind_v[:, cols] * sin[d]
            gains[d, t] = 0.5 * jnp.maximum(along, 0.0)
    copies = []
    for part in range(FREQS // SPAN):
        span = range(part * SPAN, (part + 1) * SPAN)
        for t, cols in enumerate(columns):
            ratio = shrink[t]
            gain = [gains[d, t] for d in range(3)]
            for f in span:
                less = 1.0 / (1.0 + ratio * float(FR[f] * FR[f]))
                j, i = f // FULL, f % FULL
                for d in range(3):
                    if f == FREQS - 1:
                        a = got[t, 3 * WHOLE + d]
                    elif i < CHUNKS[0][1]:
                        a = got[j, (d * CHUNKS[0][1] + i) * BLOCKS + t]
                    else:
                        a = got[j, FIRST_MADE + d * BLOCKS + t]
                    made[d, f, :, cols] = a * (1.0 + gain[d] * float(FR[f])) * less
        for d in range(3):
            rows = pl.ds(part * SPAN, SPAN)
            copies.append(
                pltpu.make_async_copy(made.at[d, rows], out.at[d, rows], done.at[part, d])
            )
            copies[-1].start()
    for copy in copies:
        copy.wait()


def moving(kernel, name, out, ins, out_space, args, scratch, cost=4_000_000):
    limit = 60 * 1024 * 1024 if "pack" in name else VMEM_LIMIT
    return pl.pallas_call(
        kernel,
        out_shape=[jax.ShapeDtypeStruct(s, jnp.float32) for s in out],
        in_specs=ins,
        out_specs=[out_space for _ in out],
        scratch_shapes=scratch,
        compiler_params=pltpu.CompilerParams(vmem_limit_bytes=limit),
        cost_estimate=pl.CostEstimate(flops=1000, bytes_accessed=cost, transcendentals=0),
        interpret=INTERPRET,
        name=name,
    )(*args)


def tiled(rows):
    return jnp.swapaxes(rows.reshape(rows.shape[:-1] + (BLOCKS, LANES)), -2, -3)


def on_device(spectrum, sea_mask, turning, wind_u, wind_v):
    me = lax.axis_index("spec")
    group = jnp.stack([me, lax.axis_index("space") % 2])
    count = lax.axis_size("space")
    swaps = [[(i, i + 1) for i in range(first, count - 1, 2)] for first in (1, 0)]
    over, within = ([*pairs, *((j, i) for i, j in pairs)] for pairs in swaps)

    maps = jnp.stack([(sea_mask == 1).astype(jnp.float32), turning])
    hbm = pl.BlockSpec(memory_space=pltpu.HBM)
    room = pltpu.VMEM(spectrum.shape, jnp.float32)
    first, last = CHUNKS
    (pack,) = moving(
        first_pack_kernel,
        "first_pack",
        [(BLOCKS, 3, first[1]) + spectrum.shape[2:]],
        [hbm],
        hbm,
        (spectrum,),
        [
            pltpu.VMEM((3, BLOCKS, first[1]) + spectrum.shape[2:], jnp.float32),
            pltpu.SemaphoreType.DMA((3, BLOCKS)),
            pltpu.SemaphoreType.DMA((3,)),
        ],
    )
    (pack_2,) = moving(
        last_pack_kernel,
        "last_pack",
        [(BLOCKS, 3, tiles_of(last), 4, LANES)],
        [hbm],
        vmem(),
        (spectrum,),
        [room, pltpu.SemaphoreType.DMA((3,))],
    )

    def edges(tiles, planes, *args):
        kernel = functools.partial(halo_kernel, tiles, len(args) > 1)
        return call(kernel, "halo", [(planes, tiles, 4, LANES)] * 2, (group, *args), 1)

    own = lax.all_to_all(pack, "spec", 0, 0, tiled=True)
    own = tiled(own).reshape(DIRS, tiles_of(first), 4, LANES)
    far, near = edges(tiles_of(first), PLANES + 1, own, maps)
    pack_2, far, near = lax.optimization_barrier((pack_2, far, near))
    own_2 = lax.all_to_all(pack_2, "spec", 0, 0, tiled=True)
    own_2 = own_2.reshape(DIRS, tiles_of(last), 4, LANES)
    far_2, near_2 = edges(tiles_of(last), PLANES, own_2)
    far, near = lax.ppermute(far, "space", over), lax.ppermute(near, "space", within)
    far, near, _, _ = lax.optimization_barrier((far, near, far_2, near_2))
    far_2, near_2 = lax.ppermute(far_2, "space", over), lax.ppermute(near_2, "space", within)
    made, around, sums = step_call(CHUNKS[0], True, group, own, far, near, (maps,))
    (made,) = step_call(CHUNKS[1], False, group, own_2, far_2, near_2, (around, made, sums))
    got = lax.all_to_all(made, "spec", 0, 0, tiled=True)
    cos = lax.dynamic_slice_in_dim(jnp.asarray(COS), me * 3, 3)
    sin = lax.dynamic_slice_in_dim(jnp.asarray(SIN), me * 3, 3)
    (result,) = moving(
        source_kernel,
        "source",
        [spectrum.shape],
        [smem(), smem(), vmem(), vmem(), vmem()],
        hbm,
        (cos, sin, got, wind_u, wind_v),
        [
            room,
            pltpu.VMEM((BLOCKS, 4, LANES), jnp.float32),
            pltpu.VMEM((3, BLOCKS, 4, LANES), jnp.float32),
            pltpu.SemaphoreType.DMA((FREQS // SPAN, 3)),
        ],
    )
    return result


def solution(mesh):
    rows = P("space", None)
    bins = P("spec", None, "space", None)
    return jax.shard_map(
        on_device,
        mesh=mesh,
        in_specs=(bins, rows, rows, rows, rows),
        out_specs=bins,
        check_vma=False,
    )
```

```python
import functools

import jax
import jax.numpy as jnp
import numpy as np
from jax import lax
from jax.experimental import pallas as pl
from jax.experimental.pallas import tpu as pltpu
from jax.sharding import PartitionSpec as P

DIRS = 24
FREQS = 25
SUB = 4
INTERPRET = False
UNROLL = True
LANES = 128
BLOCKS = 8

THETA = (np.float32(2.0 * np.pi) * np.arange(DIRS, dtype=np.float32) / np.float32(DIRS)).astype(
    np.float32
)
COS = np.cos(THETA).astype(np.float32)
SIN = np.sin(THETA).astype(np.float32)
FREQ = np.arange(FREQS, dtype=np.float64)
FR = (1.1 ** (FREQ - FREQS // 2)).astype(np.float32)
SPEED = (1.1 ** (-FREQ)).astype(np.float32)
RFAC = (np.float32(0.5) + np.float32(0.5) * SPEED).astype(np.float32)


def grouped(values):
    kept, place = [], []
    for v in values:
        near = [i for i, k in enumerate(kept) if abs(k - v) <= 4e-7 * abs(k)]
        if not near:
            kept.append(float(v))
        place.append(near[0] if near else len(kept) - 1)
    return kept, place


WEIGHTS, PLACE = grouped(np.abs(np.concatenate([COS, SIN])).astype(np.float64))
KX, KY = PLACE[:DIRS], PLACE[DIRS:]
REST, K0 = grouped([WEIGHTS[KX[d]] + WEIGHTS[KY[d]] for d in range(DIRS)])
COEF = np.concatenate(
    [
        0.42 * SPEED.astype(np.float64)[:, None] * np.array(WEIGHTS)[None, :],
        1.0 - 0.42 * SPEED.astype(np.float64)[:, None] * np.array(REST)[None, :],
    ],
    axis=1,
).astype(np.float32)

FULL = 3
CHUNKS = ((0, 2, False), (2, 1, True))
WHOLE = FULL * BLOCKS
WINDOW = 2
HALF = LANES // 2
FIRST_MADE = 3 * CHUNKS[0][1] * BLOCKS
SUMS_AT = 3 * (WHOLE + 1)
MADE = SUMS_AT + 2 * BLOCKS

SOUTH = [d for d in range(DIRS) if SIN[d] >= 0]
NORTH = [d for d in range(DIRS) if SIN[d] < 0]
REACH = SUB - 1
PLANES = len(SOUTH) + REACH
EXTRAS = []
for k in range(1, REACH + 1):
    EXTRAS += [
        ("s", (SOUTH[-1] + k) % DIRS, k),
        ("s", (SOUTH[0] - k) % DIRS, k),
        ("n", (NORTH[-1] + k) % DIRS, k),
        ("n", (NORTH[0] - k) % DIRS, k),
    ]
EXTRA_AT = {(w, d): i for i, (w, d, _) in enumerate(EXTRAS)}
NEAR_AT = (PLANES + 1) * CHUNKS[0][1] * BLOCKS
VMEM_LIMIT = 40 * 1024 * 1024


def window(d):
    return "s" if d in SOUTH else "n"


def tiles_of(chunk):
    return chunk[1] * BLOCKS + (WINDOW if chunk[2] else 0)


def slots_of(chunk):
    return tiles_of(chunk) + chunk[1] + (2 if chunk[2] else 1)


def smem():
    return pl.BlockSpec(memory_space=pltpu.SMEM)


def vmem():
    return pl.BlockSpec(memory_space=pltpu.VMEM)


def call(kernel, name, out, args, n_smem, scratch=(), cost=4_000_000):
    return pl.pallas_call(
        kernel,
        out_shape=jax.tree.map(lambda s: jax.ShapeDtypeStruct(s, jnp.float32), out, is_leaf=lambda s: isinstance(s, tuple) and isinstance(s[0], int)),
        in_specs=[smem()] * n_smem + [vmem()] * (len(args) - n_smem),
        out_specs=jax.tree.map(lambda s: vmem(), out, is_leaf=lambda s: isinstance(s, tuple) and isinstance(s[0], int)),
        scratch_shapes=list(scratch),
        compiler_params=pltpu.CompilerParams(vmem_limit_bytes=VMEM_LIMIT),
        cost_estimate=pl.CostEstimate(flops=1000, bytes_accessed=cost, transcendentals=0),
        interpret=INTERPRET,
        name=name,
    )(*args)


def first_pack_kernel(spectrum, out, x, arrived, done):
    begin, count, _ = CHUNKS[0]
    ins = [
        [
            pltpu.make_async_copy(
                spectrum.at[d, pl.ds(j * FULL + begin, count)], x.at[d, j], arrived.at[d, j]
            )
            for j in range(BLOCKS)
        ]
        for d in range(3)
    ]
    outs = [pltpu.make_async_copy(x.at[d], out.at[:, d], done.at[d]) for d in range(3)]
    for copies in ins:
        for copy in copies:
            copy.start()
    for copies, leave in zip(ins, outs):
        for copy in copies:
            copy.wait()
        leave.start()
    for leave in outs:
        leave.wait()


def last_pack_kernel(spectrum, out, x, arrived):
    begin, count, _ = CHUNKS[1]
    copies = [pltpu.make_async_copy(spectrum.at[d], x.at[d], arrived.at[d]) for d in range(3)]
    for copy in copies:
        copy.start()
    zero = jnp.zeros((4, HALF), jnp.float32)
    for d in range(3):
        copies[d].wait()
        for j in range(BLOCKS):
            for i in range(count):
                for l in range(BLOCKS):
                    value = x[d, j * FULL + begin + i, :, l * LANES : (l + 1) * LANES]
                    out[j, d, i * BLOCKS + l] = value
            left, right = j * LANES - HALF, (j + 1) * LANES + HALF
            value = x[d, FREQS - 1, :, max(left, 0) : min(right, BLOCKS * LANES)]
            if left < 0:
                value = jnp.concatenate([zero, value], axis=1)
            if right > BLOCKS * LANES:
                value = jnp.concatenate([value, zero], axis=1)
            for i in range(WINDOW):
                out[j, d, count * BLOCKS + i] = value[:, i * LANES : (i + 1) * LANES]


def halo_kernel(tiles, with_maps, group, *refs):
    own, more, far, near = refs
    skip = 0 if with_maps else NEAR_AT
    maps = more
    if skip:
        for i in range(skip):
            near[i] = more[i]
    n = len(SOUTH)

    def write(up, down, up_at, down_at):
        if with_maps:
            for k in range(2):
                for l in range(BLOCKS):
                    value = maps[k, :, l * LANES : (l + 1) * LANES]
                    up[up_at + PLANES * tiles + k * BLOCKS + l] = value
                    down[down_at + PLANES * tiles + k * BLOCKS + l] = value
        ends = {
            "s": (SOUTH[-1], SOUTH[0]),
            "n": (NORTH[0], NORTH[-1]),
        }

        def body(t, carry):
            for i, d in enumerate(SOUTH):
                up[up_at + i * tiles + t] = own[d, t]
            for i, d in enumerate(NORTH):
                down[down_at + i * tiles + t] = own[d, t]
            top, low = ends["s"]
            a = [own[(top + k) % DIRS, t] for k in range(1, 4)]
            b = [own[(low - k) % DIRS, t] for k in range(1, 4)]
            up[up_at + (n) * tiles + t] = jnp.concatenate([a[2][3:4], a[0][1:4]], axis=0)
            up[up_at + (n + 1) * tiles + t] = jnp.concatenate([b[1][2:4], a[1][2:4]], axis=0)
            up[up_at + (n + 2) * tiles + t] = jnp.concatenate([b[2][3:4], b[0][1:4]], axis=0)
            low, top = ends["n"]
            a = [own[(low - k) % DIRS, t] for k in range(1, 4)]
            b = [own[(top + k) % DIRS, t] for k in range(1, 4)]
            down[down_at + (n) * tiles + t] = jnp.concatenate([a[0][0:3], a[2][0:1]], axis=0)
            down[down_at + (n + 1) * tiles + t] = jnp.concatenate([a[1][0:2], b[1][0:2]], axis=0)
            down[down_at + (n + 2) * tiles + t] = jnp.concatenate([b[0][0:3], b[2][0:1]], axis=0)
            return carry

        lax.fori_loop(0, tiles, body, 0, unroll=4)

    pl.when(group[1] == 1)(lambda: write(far, near, 0, skip))
    pl.when(group[1] == 0)(lambda: write(near, far, skip, 0))


def step_kernel(chunk, first_call, group, coef, rfac, frsq, own, far, near, *refs):
    begin, count, tail = chunk
    tiles, slots = tiles_of(chunk), slots_of(chunk)
    if first_call:
        maps, out, around, sums, st_a, st_b, ex_a, ex_b = refs
        base = 0
    else:
        around, given, given_sums, result, st_a, st_b, ex_a, ex_b, out, sums, done = refs
        base = FIRST_MADE
        early = pltpu.make_async_copy(given, result.at[:, pl.ds(0, base)], done.at[0])
        late = pltpu.make_async_copy(out, result.at[:, pl.ds(base, MADE - base)], done.at[1])
        early.start()
    me = group[0]
    whole = count * BLOCKS

    def f_of(t):
        if isinstance(t, int):
            return FREQS - 1
        f = me * FULL + begin + t // BLOCKS
        return jnp.where(t < whole, f, FREQS - 1) if tail else f

    def map_of(t):
        if isinstance(t, int):
            return BLOCKS + 2 + t - whole
        l = t % BLOCKS + 1
        return jnp.where(t < whole, l, BLOCKS + 2 + t - whole) if tail else l

    def slot_of(t):
        return t + t // BLOCKS + 1

    lane = lax.broadcasted_iota(jnp.int32, (8, LANES), 1)
    row = lax.broadcasted_iota(jnp.int32, (8, LANES), 0)
    start, end, mine, half = lane == 0, lane == LANES - 1, row < 4, lane < HALF
    zero = jnp.zeros((8, LANES), jnp.float32)
    for p in [i * (BLOCKS + 1) for i in range(count + 1)] + ([slots - 1] if tail else []):
        for d in range(DIRS):
            st_a[d, p] = zero
            st_b[d, p] = zero
        for i in range(len(EXTRAS)):
            ex_a[i, p] = zero
            ex_b[i, p] = zero

    skip = 0 if first_call else NEAR_AT

    def load(south, north, south_at, north_at):
        if first_call:
            for k in range(2):
                for w, (ref, at) in enumerate(((south, south_at), (north, north_at))):
                    around[k, w, 0] = zero
                    around[k, w, BLOCKS + 1] = zero
                    for l in range(BLOCKS):
                        mid = maps[k, :, l * LANES : (l + 1) * LANES]
                        around[k, w, l + 1] = jnp.concatenate([mid, ref[at + PLANES * tiles + k * BLOCKS + l]], axis=0)
                    for i in range(WINDOW):
                        left, right = around[k, w, me + i], around[k, w, me + i + 1]
                        around[k, w, BLOCKS + 2 + i] = pltpu.roll(jnp.where(half, right, left), HALF, 1)

        def fill(t, carry):
            slot, m = slot_of(t), map_of(t)
            seas = {"s": around[0, 0, m], "n": around[0, 1, m]}
            n = len(SOUTH)

            def whole_tile(w, d, rows):
                return jnp.concatenate([own[d, t], rows], axis=0) * seas[w]

            for i, d in enumerate(SOUTH):
                st_a[d, slot] = whole_tile("s", d, south[south_at + i * tiles + t])
            for i, d in enumerate(NORTH):
                st_a[d, slot] = whole_tile("n", d, north[north_at + i * tiles + t])
            for w, ref, at in (("s", south, south_at), ("n", north, north_at)):
                a, b, c = (ref[at + (n + i) * tiles + t] for i in range(3))
                swap = jnp.concatenate([b[2:4], b[0:2]], axis=0)
                pick = slice(0, 1) if w == "s" else slice(3, 4)
                far_a = jnp.broadcast_to(a[pick], (4, LANES))
                far_c = jnp.broadcast_to(c[pick], (4, LANES))
                if w == "s":
                    top, low = SOUTH[-1], SOUTH[0]
                    line = [(top + 1, a), (top + 2, b), (top + 3, far_a)]
                    line += [(low - 1, c), (low - 2, swap), (low - 3, far_c)]
                else:
                    low, top = NORTH[0], NORTH[-1]
                    line = [(low - 1, a), (low - 2, b), (low - 3, far_a)]
                    line += [(top + 1, c), (top + 2, swap), (top + 3, far_c)]
                for d, rows in line:
                    ex_a[EXTRA_AT[w, d % DIRS], slot] = whole_tile(w, d % DIRS, rows)
            return carry

        lax.fori_loop(0, tiles, fill, 0)

    pl.when(group[1] == 1)(lambda: load(near, far, skip, 0))
    pl.when(group[1] == 0)(lambda: load(far, near, 0, skip))

    for i in range(2 * BLOCKS):
        sums[i] = jnp.zeros((4, LANES), jnp.float32) if first_call else given_sums[i]

    def keep(t, d, new):
        out[d // 3, (d % 3) * whole + t] = new[0:4]

    def add_up(t, f, total):
        place = me if isinstance(t, int) else t % BLOCKS
        total = total[0:4]
        sums[place] += total
        sums[BLOCKS + place] += total * frsq[f]

    def make(step, src, src_ex, dst, dst_ex):
        def body(t, carry):
            slot, m, f = slot_of(t), map_of(t), f_of(t)
            rf = rfac[f]
            coefs = [coef[f, i] for i in range(COEF.shape[1])]
            seas = {"s": around[0, 0, m], "n": around[0, 1, m]}
            raw = {"s": around[1, 0, m], "n": around[1, 1, m]}
            mth = {w: jnp.abs(raw[w]) * rf for w in "sn"}
            ahead = {w: raw[w] > 0 for w in "sn"}
            loaded = {}

            def tile(w, d):
                d = d % DIRS
                key = (w, d)
                if window(d) == w or step == SUB - 1:
                    key = (window(d), d)
                if key not in loaded:
                    if key[0] == window(d):
                        loaded[key] = (src, d, src[d, slot])
                    else:
                        i = EXTRA_AT[key]
                        loaded[key] = (src_ex, i, src_ex[i, slot])
                return loaded[key]

            def update(w, d):
                ref, i, a = tile(w, d)
                before, after = tile(w, d - 1)[2], tile(w, d + 1)[2]
                if COS[d] >= 0:
                    x = pltpu.roll(jnp.where(end, ref[i, slot - 1], a), 1, 1)
                else:
                    x = pltpu.roll(jnp.where(start, ref[i, slot + 1], a), LANES - 1, 1)
                y = pltpu.roll(a, 1 if SIN[d] >= 0 else 7, 0)
                turned = mth[w] * (jnp.where(ahead[w], before, after) - a)
                stay = coefs[len(WEIGHTS) + K0[d]]
                return (a * stay + x * coefs[KX[d]] + y * coefs[KY[d]] + turned) * seas[w]

            fresh = {}
            total = None
            for d in range(DIRS):
                new = update(window(d), d)
                if step < SUB - 1 or isinstance(t, int):
                    fresh[d] = new
                    dst[d, slot] = new
                else:
                    keep(t, d, new)
                    total = new if total is None else total + new
            for i, (w, d, k) in enumerate(EXTRAS):
                if k < REACH - step:
                    dst_ex[i, slot] = jnp.where(mine, fresh[d], update(w, d))
            if total is not None:
                add_up(t, f, total)
            return carry

        return body

    bufs = [(st_a, ex_a), (st_b, ex_b)]
    for step in range(SUB):
        (src, src_ex), (dst, dst_ex) = bufs[step % 2], bufs[(step + 1) % 2]
        body = make(step, src, src_ex, dst, dst_ex)
        if step < SUB - 1:
            lax.fori_loop(0, tiles, body, 0, unroll=(tiles if tail else BLOCKS) if UNROLL else 1)
        else:
            lax.fori_loop(0, whole, body, 0, unroll=BLOCKS if UNROLL else 1)
    if tail:
        for t in range(whole, tiles):
            body(t, 0)
        total = None
        for d in range(DIRS):
            left, right = dst[d, slot_of(whole)], dst[d, slot_of(whole + 1)]
            new = pltpu.roll(jnp.where(half, right, left), HALF, 1)
            out[d // 3, 3 * whole + d % 3] = new[0:4]
            total = new if total is None else total + new
        add_up(whole, FREQS - 1, total)
    if not first_call:
        for i in range(2 * BLOCKS):
            value = sums[i]
            for s in range(BLOCKS):
                out[s, SUMS_AT - base + i] = value
        late.start()
        early.wait()
        late.wait()


def step_call(chunk, first_call, group, own, far, near, rest):
    slots = slots_of(chunk)
    state = pltpu.VMEM((DIRS, slots, 8, LANES), jnp.float32)
    extra = pltpu.VMEM((len(EXTRAS), slots, 8, LANES), jnp.float32)
    args = (group, COEF, RFAC, FR * FR, own, far, near, *rest)
    scratch = [state, state, extra, extra]
    if first_call:
        out = [
            (BLOCKS, FIRST_MADE, 4, LANES),
            (2, 2, BLOCKS + 2 + WINDOW, 8, LANES),
            (2 * BLOCKS, 4, LANES),
        ]
        space = vmem()
    else:
        out = [(BLOCKS, MADE, 4, LANES)]
        space = pl.BlockSpec(memory_space=pltpu.HBM)
        scratch += [
            pltpu.VMEM((BLOCKS, MADE - FIRST_MADE, 4, LANES), jnp.float32),
            pltpu.VMEM((2 * BLOCKS, 4, LANES), jnp.float32),
            pltpu.SemaphoreType.DMA((2,)),
        ]
    return moving(
        functools.partial(step_kernel, chunk, first_call),
        "steps",
        out,
        [smem()] * 4 + [vmem()] * (len(args) - 4),
        space,
        args,
        scratch,
        20_000_000,
    )


SPAN = 5


def source_kernel(cos, sin, got, wind_u, wind_v, out, made, shrink, gains, done):
    inverse = 1.0 / (DIRS * FREQS)
    columns = [slice(t * LANES, (t + 1) * LANES) for t in range(BLOCKS)]
    for t, cols in enumerate(columns):
        m0 = got[0, SUMS_AT + t]
        m2 = got[0, SUMS_AT + BLOCKS + t]
        for j in range(1, BLOCKS):
            m0 = m0 + got[j, SUMS_AT + t]
            m2 = m2 + got[j, SUMS_AT + BLOCKS + t]
        shrink[t] = 0.5 * (m2 * inverse) / (1.0 + m0 * inverse)
        for d in range(3):
            along = wind_u[:, cols] * cos[d] + wind_v[:, cols] * sin[d]
            gains[d, t] = 0.5 * jnp.maximum(along, 0.0)
    copies = []
    for part in range(FREQS // SPAN):
        span = range(part * SPAN, (part + 1) * SPAN)
        for t, cols in enumerate(columns):
            ratio = shrink[t]
            gain = [gains[d, t] for d in range(3)]
            for f in span:
                less = 1.0 / (1.0 + ratio * float(FR[f] * FR[f]))
                j, i = f // FULL, f % FULL
                for d in range(3):
                    if f == FREQS - 1:
                        a = got[t, 3 * WHOLE + d]
                    elif i < CHUNKS[0][1]:
                        a = got[j, (d * CHUNKS[0][1] + i) * BLOCKS + t]
                    else:
                        a = got[j, FIRST_MADE + d * BLOCKS + t]
                    made[d, f, :, cols] = a * (1.0 + gain[d] * float(FR[f])) * less
        for d in range(3):
            rows = pl.ds(part * SPAN, SPAN)
            copies.append(
                pltpu.make_async_copy(made.at[d, rows], out.at[d, rows], done.at[part, d])
            )
            copies[-1].start()
    for copy in copies:
        copy.wait()


def moving(kernel, name, out, ins, out_space, args, scratch, cost=4_000_000):
    limit = 60 * 1024 * 1024 if "pack" in name else VMEM_LIMIT
    return pl.pallas_call(
        kernel,
        out_shape=[jax.ShapeDtypeStruct(s, jnp.float32) for s in out],
        in_specs=ins,
        out_specs=[out_space for _ in out],
        scratch_shapes=scratch,
        compiler_params=pltpu.CompilerParams(vmem_limit_bytes=limit),
        cost_estimate=pl.CostEstimate(flops=1000, bytes_accessed=cost, transcendentals=0),
        interpret=INTERPRET,
        name=name,
    )(*args)


def tiled(rows):
    return jnp.swapaxes(rows.reshape(rows.shape[:-1] + (BLOCKS, LANES)), -2, -3)


def on_device(spectrum, sea_mask, turning, wind_u, wind_v):
    me = lax.axis_index("spec")
    group = jnp.stack([me, lax.axis_index("space") % 2])
    count = lax.axis_size("space")
    swaps = [[(i, i + 1) for i in range(first, count - 1, 2)] for first in (1, 0)]
    over, within = ([*pairs, *((j, i) for i, j in pairs)] for pairs in swaps)

    maps = jnp.stack([(sea_mask == 1).astype(jnp.float32), turning])
    hbm = pl.BlockSpec(memory_space=pltpu.HBM)
    room = pltpu.VMEM(spectrum.shape, jnp.float32)
    first, last = CHUNKS
    (pack,) = moving(
        first_pack_kernel,
        "first_pack",
        [(BLOCKS, 3, first[1]) + spectrum.shape[2:]],
        [hbm],
        hbm,
        (spectrum,),
        [
            pltpu.VMEM((3, BLOCKS, first[1]) + spectrum.shape[2:], jnp.float32),
            pltpu.SemaphoreType.DMA((3, BLOCKS)),
            pltpu.SemaphoreType.DMA((3,)),
        ],
    )
    (pack_2,) = moving(
        last_pack_kernel,
        "last_pack",
        [(BLOCKS, 3, tiles_of(last), 4, LANES)],
        [hbm],
        vmem(),
        (spectrum,),
        [room, pltpu.SemaphoreType.DMA((3,))],
    )

    def edges(tiles, sizes, with_maps, *args):
        kernel = functools.partial(halo_kernel, tiles, with_maps)
        return call(kernel, "halo", [(n, 4, LANES) for n in sizes], (group, *args), 1)

    own = lax.all_to_all(pack, "spec", 0, 0, tiled=True)
    own = tiled(own).reshape(DIRS, tiles_of(first), 4, LANES)
    far, near = edges(tiles_of(first), [NEAR_AT] * 2, True, own, maps)
    pack_2, far, near = lax.optimization_barrier((pack_2, far, near))
    own_2 = lax.all_to_all(pack_2, "spec", 0, 0, tiled=True)
    own_2 = own_2.reshape(DIRS, tiles_of(last), 4, LANES)
    extra = PLANES * tiles_of(last)
    far_2, near = edges(tiles_of(last), [extra, NEAR_AT + extra], False, own_2, near)
    far, near = lax.ppermute(far, "space", over), lax.ppermute(near, "space", within)
    far, near, _ = lax.optimization_barrier((far, near, far_2))
    far_2 = lax.ppermute(far_2, "space", over)
    made, around, sums = step_call(CHUNKS[0], True, group, own, far, near, (maps,))
    (made,) = step_call(CHUNKS[1], False, group, own_2, far_2, near, (around, made, sums))
    got = lax.all_to_all(made, "spec", 0, 0, tiled=True)
    cos = lax.dynamic_slice_in_dim(jnp.asarray(COS), me * 3, 3)
    sin = lax.dynamic_slice_in_dim(jnp.asarray(SIN), me * 3, 3)
    (result,) = moving(
        source_kernel,
        "source",
        [spectrum.shape],
        [smem(), smem(), vmem(), vmem(), vmem()],
        hbm,
        (cos, sin, got, wind_u, wind_v),
        [
            room,
            pltpu.VMEM((BLOCKS, 4, LANES), jnp.float32),
            pltpu.VMEM((3, BLOCKS, 4, LANES), jnp.float32),
            pltpu.SemaphoreType.DMA((FREQS // SPAN, 3)),
        ],
    )
    return result


def solution(mesh):
    rows = P("space", None)
    bins = P("spec", None, "space", None)
    return jax.shard_map(
        on_device,
        mesh=mesh,
        in_specs=(bins, rows, rows, rows, rows),
        out_specs=bins,
        check_vma=False,
    )
```

```python
import functools

import jax
import jax.numpy as jnp
import numpy as np
from jax import lax
from jax.experimental import pallas as pl
from jax.experimental.pallas import tpu as pltpu
from jax.sharding import PartitionSpec as P

DIRS = 24
FREQS = 25
SUB = 4
INTERPRET = False
UNROLL = True
LANES = 128
BLOCKS = 8

THETA = (np.float32(2.0 * np.pi) * np.arange(DIRS, dtype=np.float32) / np.float32(DIRS)).astype(
    np.float32
)
COS = np.cos(THETA).astype(np.float32)
SIN = np.sin(THETA).astype(np.float32)
FREQ = np.arange(FREQS, dtype=np.float64)
FR = (1.1 ** (FREQ - FREQS // 2)).astype(np.float32)
SPEED = (1.1 ** (-FREQ)).astype(np.float32)
RFAC = (np.float32(0.5) + np.float32(0.5) * SPEED).astype(np.float32)


def grouped(values):
    kept, place = [], []
    for v in values:
        near = [i for i, k in enumerate(kept) if abs(k - v) <= 4e-7 * abs(k)]
        if not near:
            kept.append(float(v))
        place.append(near[0] if near else len(kept) - 1)
    return kept, place


WEIGHTS, PLACE = grouped(np.abs(np.concatenate([COS, SIN])).astype(np.float64))
KX, KY = PLACE[:DIRS], PLACE[DIRS:]
REST, K0 = grouped([WEIGHTS[KX[d]] + WEIGHTS[KY[d]] for d in range(DIRS)])
COEF = np.concatenate(
    [
        0.42 * SPEED.astype(np.float64)[:, None] * np.array(WEIGHTS)[None, :],
        1.0 - 0.42 * SPEED.astype(np.float64)[:, None] * np.array(REST)[None, :],
    ],
    axis=1,
).astype(np.float32)

FULL = 3
CHUNKS = ((0, 2, False), (2, 1, True))
WHOLE = FULL * BLOCKS
WINDOW = 2
HALF = LANES // 2
FIRST_MADE = 3 * CHUNKS[0][1] * BLOCKS
SUMS_AT = 3 * (WHOLE + 1)
MADE = SUMS_AT + 2 * BLOCKS

SOUTH = [d for d in range(DIRS) if SIN[d] >= 0]
NORTH = [d for d in range(DIRS) if SIN[d] < 0]
REACH = SUB - 1
PLANES = len(SOUTH) + REACH
EXTRAS = []
for k in range(1, REACH + 1):
    EXTRAS += [
        ("s", (SOUTH[-1] + k) % DIRS, k),
        ("s", (SOUTH[0] - k) % DIRS, k),
        ("n", (NORTH[-1] + k) % DIRS, k),
        ("n", (NORTH[0] - k) % DIRS, k),
    ]
EXTRA_AT = {(w, d): i for i, (w, d, _) in enumerate(EXTRAS)}
VMEM_LIMIT = 40 * 1024 * 1024


def window(d):
    return "s" if d in SOUTH else "n"


def tiles_of(chunk):
    return chunk[1] * BLOCKS + (WINDOW if chunk[2] else 0)


def slots_of(chunk):
    return tiles_of(chunk) + chunk[1] + (2 if chunk[2] else 1)


def smem():
    return pl.BlockSpec(memory_space=pltpu.SMEM)


def vmem():
    return pl.BlockSpec(memory_space=pltpu.VMEM)


def call(kernel, name, out, args, n_smem, scratch=(), cost=4_000_000):
    return pl.pallas_call(
        kernel,
        out_shape=jax.tree.map(lambda s: jax.ShapeDtypeStruct(s, jnp.float32), out, is_leaf=lambda s: isinstance(s, tuple) and isinstance(s[0], int)),
        in_specs=[smem()] * n_smem + [vmem()] * (len(args) - n_smem),
        out_specs=jax.tree.map(lambda s: vmem(), out, is_leaf=lambda s: isinstance(s, tuple) and isinstance(s[0], int)),
        scratch_shapes=list(scratch),
        compiler_params=pltpu.CompilerParams(vmem_limit_bytes=VMEM_LIMIT),
        cost_estimate=pl.CostEstimate(flops=1000, bytes_accessed=cost, transcendentals=0),
        interpret=INTERPRET,
        name=name,
    )(*args)


def first_pack_kernel(spectrum, out, x, arrived, done):
    begin, count, _ = CHUNKS[0]
    ins = [
        [
            pltpu.make_async_copy(
                spectrum.at[d, pl.ds(j * FULL + begin, count)], x.at[d, j], arrived.at[d, j]
            )
            for j in range(BLOCKS)
        ]
        for d in range(3)
    ]
    outs = [pltpu.make_async_copy(x.at[d], out.at[:, d], done.at[d]) for d in range(3)]
    for copies in ins:
        for copy in copies:
            copy.start()
    for copies, leave in zip(ins, outs):
        for copy in copies:
            copy.wait()
        leave.start()
    for leave in outs:
        leave.wait()


def last_pack_kernel(spectrum, out, x, arrived):
    begin, count, _ = CHUNKS[1]
    copies = [pltpu.make_async_copy(spectrum.at[d], x.at[d], arrived.at[d]) for d in range(3)]
    for copy in copies:
        copy.start()
    zero = jnp.zeros((4, HALF), jnp.float32)
    for d in range(3):
        copies[d].wait()
        for j in range(BLOCKS):
            for i in range(count):
                for l in range(BLOCKS):
                    value = x[d, j * FULL + begin + i, :, l * LANES : (l + 1) * LANES]
                    out[j, d, i * BLOCKS + l] = value
            left, right = j * LANES - HALF, (j + 1) * LANES + HALF
            value = x[d, FREQS - 1, :, max(left, 0) : min(right, BLOCKS * LANES)]
            if left < 0:
                value = jnp.concatenate([zero, value], axis=1)
            if right > BLOCKS * LANES:
                value = jnp.concatenate([value, zero], axis=1)
            for i in range(WINDOW):
                out[j, d, count * BLOCKS + i] = value[:, i * LANES : (i + 1) * LANES]


def halo_kernel(tiles, with_maps, group, *refs):
    own, far, near = refs[0], refs[-2], refs[-1]
    maps = refs[1] if with_maps else None
    n = len(SOUTH)

    def write(up, down):
        if with_maps:
            for k in range(2):
                for l in range(BLOCKS):
                    value = maps[k, :, l * LANES : (l + 1) * LANES]
                    up[PLANES, k * BLOCKS + l] = value
                    down[PLANES, k * BLOCKS + l] = value
        ends = {
            "s": (SOUTH[-1], SOUTH[0]),
            "n": (NORTH[0], NORTH[-1]),
        }

        def body(t, carry):
            for i, d in enumerate(SOUTH):
                up[i, t] = own[d, t]
            for i, d in enumerate(NORTH):
                down[i, t] = own[d, t]
            top, low = ends["s"]
            a = [own[(top + k) % DIRS, t] for k in range(1, 4)]
            b = [own[(low - k) % DIRS, t] for k in range(1, 4)]
            up[n, t] = jnp.concatenate([a[2][3:4], a[0][1:4]], axis=0)
            up[n + 1, t] = jnp.concatenate([b[1][2:4], a[1][2:4]], axis=0)
            up[n + 2, t] = jnp.concatenate([b[2][3:4], b[0][1:4]], axis=0)
            low, top = ends["n"]
            a = [own[(low - k) % DIRS, t] for k in range(1, 4)]
            b = [own[(top + k) % DIRS, t] for k in range(1, 4)]
            down[n, t] = jnp.concatenate([a[0][0:3], a[2][0:1]], axis=0)
            down[n + 1, t] = jnp.concatenate([a[1][0:2], b[1][0:2]], axis=0)
            down[n + 2, t] = jnp.concatenate([b[0][0:3], b[2][0:1]], axis=0)
            return carry

        lax.fori_loop(0, tiles, body, 0, unroll=4)

    pl.when(group[1] == 1)(lambda: write(far, near))
    pl.when(group[1] == 0)(lambda: write(near, far))


def step_kernel(chunk, first_call, group, coef, rfac, frsq, own, far, near, *refs):
    begin, count, tail = chunk
    tiles, slots = tiles_of(chunk), slots_of(chunk)
    if first_call:
        maps, out, around, sums, st_a, st_b, ex_a, ex_b = refs
        base = 0
    else:
        around, given, given_sums, result, st_a, st_b, ex_a, ex_b, out, sums, done = refs
        base = FIRST_MADE
        early = pltpu.make_async_copy(given, result.at[:, pl.ds(0, base)], done.at[0])
        late = pltpu.make_async_copy(out, result.at[:, pl.ds(base, MADE - base)], done.at[1])
        early.start()
    me = group[0]
    whole = count * BLOCKS

    def f_of(t):
        if isinstance(t, int):
            return FREQS - 1
        f = me * FULL + begin + t // BLOCKS
        return jnp.where(t < whole, f, FREQS - 1) if tail else f

    def map_of(t):
        if isinstance(t, int):
            return BLOCKS + 2 + t - whole
        l = t % BLOCKS + 1
        return jnp.where(t < whole, l, BLOCKS + 2 + t - whole) if tail else l

    def slot_of(t):
        return t + t // BLOCKS + 1

    lane = lax.broadcasted_iota(jnp.int32, (8, LANES), 1)
    row = lax.broadcasted_iota(jnp.int32, (8, LANES), 0)
    start, end, mine, half = lane == 0, lane == LANES - 1, row < 4, lane < HALF
    zero = jnp.zeros((8, LANES), jnp.float32)
    for p in [i * (BLOCKS + 1) for i in range(count + 1)] + ([slots - 1] if tail else []):
        for d in range(DIRS):
            st_a[d, p] = zero
            st_b[d, p] = zero
        for i in range(len(EXTRAS)):
            ex_a[i, p] = zero
            ex_b[i, p] = zero

    def load(south, north):
        if first_call:
            for k in range(2):
                for w, ref in enumerate((south, north)):
                    around[k, w, 0] = zero
                    around[k, w, BLOCKS + 1] = zero
                    for l in range(BLOCKS):
                        mid = maps[k, :, l * LANES : (l + 1) * LANES]
                        around[k, w, l + 1] = jnp.concatenate([mid, ref[PLANES, k * BLOCKS + l]], axis=0)
                    for i in range(WINDOW):
                        left, right = around[k, w, me + i], around[k, w, me + i + 1]
                        around[k, w, BLOCKS + 2 + i] = pltpu.roll(jnp.where(half, right, left), HALF, 1)

        def fill(t, carry):
            slot, m = slot_of(t), map_of(t)
            seas = {"s": around[0, 0, m], "n": around[0, 1, m]}
            n = len(SOUTH)

            def whole_tile(w, d, rows):
                return jnp.concatenate([own[d, t], rows], axis=0) * seas[w]

            for i, d in enumerate(SOUTH):
                st_a[d, slot] = whole_tile("s", d, south[i, t])
            for i, d in enumerate(NORTH):
                st_a[d, slot] = whole_tile("n", d, north[i, t])
            for w, ref in (("s", south), ("n", north)):
                a, b, c = (ref[n + i, t] for i in range(3))
                swap = jnp.concatenate([b[2:4], b[0:2]], axis=0)
                pick = slice(0, 1) if w == "s" else slice(3, 4)
                far_a = jnp.broadcast_to(a[pick], (4, LANES))
                far_c = jnp.broadcast_to(c[pick], (4, LANES))
                if w == "s":
                    top, low = SOUTH[-1], SOUTH[0]
                    line = [(top + 1, a), (top + 2, b), (top + 3, far_a)]
                    line += [(low - 1, c), (low - 2, swap), (low - 3, far_c)]
                else:
                    low, top = NORTH[0], NORTH[-1]
                    line = [(low - 1, a), (low - 2, b), (low - 3, far_a)]
                    line += [(top + 1, c), (top + 2, swap), (top + 3, far_c)]
                for d, rows in line:
                    ex_a[EXTRA_AT[w, d % DIRS], slot] = whole_tile(w, d % DIRS, rows)
            return carry

        lax.fori_loop(0, tiles, fill, 0, unroll=2 if UNROLL else 1)

    pl.when(group[1] == 1)(lambda: load(near, far))
    pl.when(group[1] == 0)(lambda: load(far, near))

    for i in range(2 * BLOCKS):
        sums[i] = jnp.zeros((4, LANES), jnp.float32) if first_call else given_sums[i]

    def keep(t, d, new):
        out[d // 3, (d % 3) * whole + t] = new[0:4]

    def add_up(t, f, total):
        place = me if isinstance(t, int) else t % BLOCKS
        total = total[0:4]
        sums[place] += total
        sums[BLOCKS + place] += total * frsq[f]

    def make(step, src, src_ex, dst, dst_ex):
        def body(t, carry):
            slot, m, f = slot_of(t), map_of(t), f_of(t)
            rf = rfac[f]
            coefs = [coef[f, i] for i in range(COEF.shape[1])]
            seas = {"s": around[0, 0, m], "n": around[0, 1, m]}
            raw = {"s": around[1, 0, m], "n": around[1, 1, m]}
            mth = {w: jnp.abs(raw[w]) * rf for w in "sn"}
            ahead = {w: raw[w] > 0 for w in "sn"}
            loaded = {}

            def tile(w, d):
                d = d % DIRS
                key = (w, d)
                if window(d) == w or step == SUB - 1:
                    key = (window(d), d)
                if key not in loaded:
                    if key[0] == window(d):
                        loaded[key] = (src, d, src[d, slot])
                    else:
                        i = EXTRA_AT[key]
                        loaded[key] = (src_ex, i, src_ex[i, slot])
                return loaded[key]

            def update(w, d):
                ref, i, a = tile(w, d)
                before, after = tile(w, d - 1)[2], tile(w, d + 1)[2]
                if COS[d] >= 0:
                    x = pltpu.roll(jnp.where(end, ref[i, slot - 1], a), 1, 1)
                else:
                    x = pltpu.roll(jnp.where(start, ref[i, slot + 1], a), LANES - 1, 1)
                y = pltpu.roll(a, 1 if SIN[d] >= 0 else 7, 0)
                turned = mth[w] * (jnp.where(ahead[w], before, after) - a)
                stay = coefs[len(WEIGHTS) + K0[d]]
                return (a * stay + x * coefs[KX[d]] + y * coefs[KY[d]] + turned) * seas[w]

            fresh = {}
            total = None
            for d in range(DIRS):
                new = update(window(d), d)
                if step < SUB - 1 or isinstance(t, int):
                    fresh[d] = new
                    dst[d, slot] = new
                else:
                    keep(t, d, new)
                    total = new if total is None else total + new
            for i, (w, d, k) in enumerate(EXTRAS):
                if k < REACH - step:
                    dst_ex[i, slot] = jnp.where(mine, fresh[d], update(w, d))
            if total is not None:
                add_up(t, f, total)
            return carry

        return body

    bufs = [(st_a, ex_a), (st_b, ex_b)]
    for step in range(SUB):
        (src, src_ex), (dst, dst_ex) = bufs[step % 2], bufs[(step + 1) % 2]
        body = make(step, src, src_ex, dst, dst_ex)
        if step < SUB - 1:
            lax.fori_loop(0, tiles, body, 0, unroll=(tiles if tail else BLOCKS) if UNROLL else 1)
        else:
            lax.fori_loop(0, whole, body, 0, unroll=BLOCKS if UNROLL else 1)
    if tail:
        for t in range(whole, tiles):
            body(t, 0)
        total = None
        for d in range(DIRS):
            left, right = dst[d, slot_of(whole)], dst[d, slot_of(whole + 1)]
            new = pltpu.roll(jnp.where(half, right, left), HALF, 1)
            out[d // 3, 3 * whole + d % 3] = new[0:4]
            total = new if total is None else total + new
        add_up(whole, FREQS - 1, total)
    if not first_call:
        for i in range(2 * BLOCKS):
            value = sums[i]
            for s in range(BLOCKS):
                out[s, SUMS_AT - base + i] = value
        late.start()
        early.wait()
        late.wait()


def step_call(chunk, first_call, group, own, far, near, rest):
    slots = slots_of(chunk)
    state = pltpu.VMEM((DIRS, slots, 8, LANES), jnp.float32)
    extra = pltpu.VMEM((len(EXTRAS), slots, 8, LANES), jnp.float32)
    args = (group, COEF, RFAC, FR * FR, own, far, near, *rest)
    scratch = [state, state, extra, extra]
    if first_call:
        out = [
            (BLOCKS, FIRST_MADE, 4, LANES),
            (2, 2, BLOCKS + 2 + WINDOW, 8, LANES),
            (2 * BLOCKS, 4, LANES),
        ]
        space = vmem()
    else:
        out = [(BLOCKS, MADE, 4, LANES)]
        space = pl.BlockSpec(memory_space=pltpu.HBM)
        scratch += [
            pltpu.VMEM((BLOCKS, MADE - FIRST_MADE, 4, LANES), jnp.float32),
            pltpu.VMEM((2 * BLOCKS, 4, LANES), jnp.float32),
            pltpu.SemaphoreType.DMA((2,)),
        ]
    return moving(
        functools.partial(step_kernel, chunk, first_call),
        "steps",
        out,
        [smem()] * 4 + [vmem()] * (len(args) - 4),
        space,
        args,
        scratch,
        20_000_000,
    )


SPAN = 5


def source_kernel(cos, sin, got, wind_u, wind_v, out, made, shrink, gains, done):
    inverse = 1.0 / (DIRS * FREQS)
    columns = [slice(t * LANES, (t + 1) * LANES) for t in range(BLOCKS)]
    for t, cols in enumerate(columns):
        m0 = got[0, SUMS_AT + t]
        m2 = got[0, SUMS_AT + BLOCKS + t]
        for j in range(1, BLOCKS):
            m0 = m0 + got[j, SUMS_AT + t]
            m2 = m2 + got[j, SUMS_AT + BLOCKS + t]
        shrink[t] = 0.5 * (m2 * inverse) / (1.0 + m0 * inverse)
        for d in range(3):
            along = wind_u[:, cols] * cos[d] + wind_v[:, cols] * sin[d]
            gains[d, t] = 0.5 * jnp.maximum(along, 0.0)
    copies = []
    for part in range(FREQS // SPAN):
        span = range(part * SPAN, (part + 1) * SPAN)
        for t, cols in enumerate(columns):
            ratio = shrink[t]
            gain = [gains[d, t] for d in range(3)]
            for f in span:
                less = 1.0 / (1.0 + ratio * float(FR[f] * FR[f]))
                j, i = f // FULL, f % FULL
                for d in range(3):
                    if f == FREQS - 1:
                        a = got[t, 3 * WHOLE + d]
                    elif i < CHUNKS[0][1]:
                        a = got[j, (d * CHUNKS[0][1] + i) * BLOCKS + t]
                    else:
                        a = got[j, FIRST_MADE + d * BLOCKS + t]
                    made[d, f, :, cols] = a * (1.0 + gain[d] * float(FR[f])) * less
        for d in range(3):
            rows = pl.ds(part * SPAN, SPAN)
            copies.append(
                pltpu.make_async_copy(made.at[d, rows], out.at[d, rows], done.at[part, d])
            )
            copies[-1].start()
    for copy in copies:
        copy.wait()


def moving(kernel, name, out, ins, out_space, args, scratch, cost=4_000_000):
    limit = 60 * 1024 * 1024 if "pack" in name else VMEM_LIMIT
    return pl.pallas_call(
        kernel,
        out_shape=[jax.ShapeDtypeStruct(s, jnp.float32) for s in out],
        in_specs=ins,
        out_specs=[out_space for _ in out],
        scratch_shapes=scratch,
        compiler_params=pltpu.CompilerParams(vmem_limit_bytes=limit),
        cost_estimate=pl.CostEstimate(flops=1000, bytes_accessed=cost, transcendentals=0),
        interpret=INTERPRET,
        name=name,
    )(*args)


def tiled(rows):
    return jnp.swapaxes(rows.reshape(rows.shape[:-1] + (BLOCKS, LANES)), -2, -3)


def on_device(spectrum, sea_mask, turning, wind_u, wind_v):
    me = lax.axis_index("spec")
    group = jnp.stack([me, lax.axis_index("space") % 2])
    count = lax.axis_size("space")
    swaps = [[(i, i + 1) for i in range(first, count - 1, 2)] for first in (1, 0)]
    over, within = ([*pairs, *((j, i) for i, j in pairs)] for pairs in swaps)

    maps = jnp.stack([(sea_mask == 1).astype(jnp.float32), turning])
    hbm = pl.BlockSpec(memory_space=pltpu.HBM)
    room = pltpu.VMEM(spectrum.shape, jnp.float32)
    first, last = CHUNKS
    (pack,) = moving(
        first_pack_kernel,
        "first_pack",
        [(BLOCKS, 3, first[1]) + spectrum.shape[2:]],
        [hbm],
        hbm,
        (spectrum,),
        [
            pltpu.VMEM((3, BLOCKS, first[1]) + spectrum.shape[2:], jnp.float32),
            pltpu.SemaphoreType.DMA((3, BLOCKS)),
            pltpu.SemaphoreType.DMA((3,)),
        ],
    )
    (pack_2,) = moving(
        last_pack_kernel,
        "last_pack",
        [(BLOCKS, 3, tiles_of(last), 4, LANES)],
        [hbm],
        vmem(),
        (spectrum,),
        [room, pltpu.SemaphoreType.DMA((3,))],
    )

    def edges(tiles, planes, *args):
        kernel = functools.partial(halo_kernel, tiles, len(args) > 1)
        return call(kernel, "halo", [(planes, tiles, 4, LANES)] * 2, (group, *args), 1)

    own = lax.all_to_all(pack, "spec", 0, 0, tiled=True)
    own = tiled(own).reshape(DIRS, tiles_of(first), 4, LANES)
    far, near = edges(tiles_of(first), PLANES + 1, own, maps)
    pack_2, far, near = lax.optimization_barrier((pack_2, far, near))
    own_2 = lax.all_to_all(pack_2, "spec", 0, 0, tiled=True)
    own_2 = own_2.reshape(DIRS, tiles_of(last), 4, LANES)
    far_2, near_2 = edges(tiles_of(last), PLANES, own_2)
    far, near = lax.ppermute(far, "space", over), lax.ppermute(near, "space", within)
    far, near, _, _ = lax.optimization_barrier((far, near, far_2, near_2))
    far_2, near_2 = lax.ppermute(far_2, "space", over), lax.ppermute(near_2, "space", within)
    made, around, sums = step_call(CHUNKS[0], True, group, own, far, near, (maps,))
    (made,) = step_call(CHUNKS[1], False, group, own_2, far_2, near_2, (around, made, sums))
    got = lax.all_to_all(made, "spec", 0, 0, tiled=True)
    cos = lax.dynamic_slice_in_dim(jnp.asarray(COS), me * 3, 3)
    sin = lax.dynamic_slice_in_dim(jnp.asarray(SIN), me * 3, 3)
    (result,) = moving(
        source_kernel,
        "source",
        [spectrum.shape],
        [smem(), smem(), vmem(), vmem(), vmem()],
        hbm,
        (cos, sin, got, wind_u, wind_v),
        [
            room,
            pltpu.VMEM((BLOCKS, 4, LANES), jnp.float32),
            pltpu.VMEM((3, BLOCKS, 4, LANES), jnp.float32),
            pltpu.SemaphoreType.DMA((FREQS // SPAN, 3)),
        ],
    )
    return result


def solution(mesh):
    rows = P("space", None)
    bins = P("spec", None, "space", None)
    return jax.shard_map(
        on_device,
        mesh=mesh,
        in_specs=(bins, rows, rows, rows, rows),
        out_specs=bins,
        check_vma=False,
    )
```
